128 devices in a mesh: head: 2 (over core), outer: 8 (over z_hi, y), inner: 8 (over z_lo, x).
Axes of the slice: x: 4, y: 4, z: 4 (z_hi: 2, z_lo: 2; z = z_hi * 2 + z_lo), core: 2. Of those that a mesh axis runs over, the one named last changes fastest.
Arguments:
- queries: bfloat16 [8192, 4096], P(('outer', 'inner'), 'head'), may hold values from -17 to 17
- keys: bfloat16 [8192, 1024], P(('outer', 'inner'), 'head'), may hold values from -17 to 17
- values: bfloat16 [8192, 1024], P(('outer', 'inner'), 'head'), may hold values from -6 to 6
- permutation: int32 [128], replicated, may hold values from 0 to 127, each once
- segment: int32 [8192], replicated, may hold values from 0 to 7, never falling along the last dimension, each value on 1 to 2048 neighbouring positions
Outputs:
- attended: bfloat16 [8192, 4096], P(('outer', 'inner'), 'head')
The draws below stay inside these ranges and needn't reach their ends.
Inputs may be any that keep to these rules, and one draw needn't show every extreme that they name: `permutation`: each of the 128 episode blocks is held by exactly one slot. `segment`: ids never fall along the episode; each id covers 1 to 2048 positions and one covers exactly 2048.
All inputs are finite; a program needn't handle non-finite values.
Results may differ from the reference program's by a relative error of at most 0.0054.
Values may be sent and summed in bfloat16 or wider, within the bound.
A program may use at most 192 MiB of HBM per device.

```python
import math
import jax
import jax.numpy as jnp
import numpy as np
from jax import lax

HEADS = 32
KV_HEADS = 8
HEAD_DIM = 128
SEGMENTS = 8
STRETCH = 64
STRETCHES = 128
SEQ = 8192
MOST = 2048


def draw_queries(key, part):
    key = jax.random.fold_in(key, 11)
    result = jax.random.truncated_normal(key, -4.0, 4.0, (SEQ, HEADS, HEAD_DIM), jnp.float32)
    return result.reshape(SEQ, HEADS * HEAD_DIM).astype(jnp.bfloat16)


def draw_keys(key, part):
    key = jax.random.fold_in(key, 23)
    result = jax.random.truncated_normal(key, -4.0, 4.0, (SEQ, KV_HEADS, HEAD_DIM), jnp.float32)
    return result.reshape(SEQ, KV_HEADS * HEAD_DIM).astype(jnp.bfloat16)


def level_of(rng, extent, split, low, high):
    def one(dim, shards_of):
        heights = jax.random.uniform(jax.random.fold_in(jax.random.fold_in(rng, 6), dim), (shards_of,), jnp.float32, low / len(split), high / len(split))
        return jnp.repeat(jnp.exp(heights), extent[dim] // shards_of).reshape((-1,) + (1,) * (len(extent) - dim - 1))

    gain = one(*split[0])
    for cut in split[1:]:
        gain = gain * one(*cut)
    return gain


def split_up(number_of, total, limit, skew):
    portions = [(1 << 20) // math.isqrt(standing ** skew) + 1 for standing in range(2, number_of + 1)]
    surplus, holding = total - limit - (number_of - 1), [1] * (number_of - 1)
    while surplus > 0:
        movable = [i for i in range(number_of - 1) if holding[i] < limit]
        pool, budget = sum([portions[i] for i in movable]), surplus
        for i in movable:
            extra = min(limit - holding[i], max(1, budget * portions[i] // pool), surplus)
            holding[i] = holding[i] + extra
            surplus = surplus - extra
    return np.array([limit] + holding)


def ragged_sizes(key, number_of, total, bound, slope):
    if number_of == 2:
        one = jax.random.randint(key, (), max(1, total - bound), min(bound, total - 1) + 1)
        return jnp.stack([one, total - one])
    tallies = jnp.asarray(split_up(number_of, total, bound, slope), jnp.int32)
    pairs = (number_of - 1) // 2
    donor, receiver = tallies[1:1 + 2 * pairs:2], tallies[2:2 + 2 * pairs:2]
    margin = jnp.minimum(donor - 1, bound - receiver)
    shifted = jax.random.randint(jax.random.fold_in(key, 1), (pairs,), 0, 1 << 20) % (margin + 1)
    tallies = tallies.at[1:1 + 2 * pairs:2].set(donor - shifted).at[2:2 + 2 * pairs:2].set(receiver + shifted)
    return tallies[jax.random.permutation(jax.random.fold_in(key, 2), number_of)]


def centred(rng, shape, scale, bound, cuts=(), kind=jnp.bfloat16):
    array = scale * jax.random.normal(rng, shape, jnp.float32)
    if cuts:
        array = array * level_of(rng, shape, cuts, -0.22, 0.18)
    return jnp.clip(array, -bound, bound).astype(kind)


def setup_inputs(seed: int = 0) -> dict:
    seeds = jax.random.split(jax.random.key(seed), 6)
    queries = draw_queries(jax.random.fold_in(seeds[5], 71), 0)
    keys = draw_keys(jax.random.fold_in(seeds[5], 71), 0)
    values = centred(seeds[2], (SEQ, KV_HEADS * HEAD_DIM), 1.0, 6.0, ((0, 64), (1, 2)))
    permutation = jax.random.permutation(seeds[3], STRETCHES).astype(jnp.int32)
    segment = jnp.searchsorted(jnp.cumsum(ragged_sizes(seeds[4], SEGMENTS, SEQ, MOST, 0)), jnp.arange(SEQ), side="right").astype(jnp.int32)
    return dict(queries=queries, keys=keys, values=values, permutation=permutation, segment=segment)


def reference(queries, keys, values, permutation, segment):
    stored = jnp.arange(SEQ, dtype=jnp.int32)
    position = (permutation[stored // STRETCH] * STRETCH + stored % STRETCH).astype(jnp.int32)
    episode = segment[position]
    group_size = HEADS // KV_HEADS
    grouped = queries.reshape(SEQ, KV_HEADS, group_size, HEAD_DIM).astype(jnp.float32)
    every_key_row = keys.reshape(SEQ, KV_HEADS, HEAD_DIM).astype(jnp.float32)
    every_value_row = values.reshape(SEQ, KV_HEADS, HEAD_DIM).astype(jnp.float32)
    logit_scale = HEAD_DIM ** -0.5
    block_rows = 128

    def one_block(block_start):
        query_tile = lax.dynamic_slice_in_dim(grouped, block_start, block_rows, 0)
        pos_block = lax.dynamic_slice_in_dim(position, block_start, block_rows, 0)
        seg_block = lax.dynamic_slice_in_dim(episode, block_start, block_rows, 0)
        attention_logits = jnp.einsum("xfph,vfh->fpxv", query_tile, every_key_row) * logit_scale
        visible = (position[None, :] <= pos_block[:, None]) & (episode[None, :] == seg_block[:, None])
        attention_logits = jnp.where(visible, attention_logits, -1e30)
        row_max = jnp.max(attention_logits, axis=-1)
        weights = jnp.where(visible, jnp.exp(attention_logits - row_max[..., None]), 0.0)
        totals = jnp.sum(weights, axis=-1)
        rounded_output = lax.optimization_barrier(weights.astype(jnp.bfloat16)).astype(jnp.float32)
        blended_values = jnp.einsum("xwqz,zxb->qxwb", rounded_output, every_value_row)
        result = blended_values / jnp.moveaxis(totals, 2, 0)[..., None]
        return result.reshape(block_rows, HEADS * HEAD_DIM).astype(jnp.bfloat16)

    starts = jnp.arange(SEQ // block_rows, dtype=jnp.int32) * block_rows
    output = lax.map(one_block, starts)
    return output.reshape(SEQ, HEADS * HEAD_DIM)
```

```python
import functools
import math

import jax
import jax.numpy as jnp
from jax import lax
from jax.experimental import pallas as pl
from jax.experimental.pallas import tpu as pltpu
from jax.sharding import Mesh, PartitionSpec as P

HEAD_DIM = 128
BLOCK = 64
BLOCKS = 128
SEQ = 8192
SEGMENTS = 8
GROUP = 4
TILE = 4
MAX_TILES = 9
ROWS = GROUP * BLOCK
SCALE = math.log2(math.e) / math.sqrt(HEAD_DIM)
NEG = -1e30


def attend_kernel(perm_ref, base_ref, seg_ref, q_ref, k_ref, v_ref, o_ref, inv, scores, acc, top):
    def invert(i, carry):
        inv[perm_ref[i]] = i
        return carry

    lax.fori_loop(0, BLOCKS, invert, 0, unroll=8)
    seg = seg_ref[...]
    starts = [jnp.int32(0)] + [jnp.sum((seg < s).astype(jnp.int32)) for s in range(1, SEGMENTS)]
    base = base_ref[0]
    blocks = q_ref.shape[0] // BLOCK

    def one_block(i, carry):
        place = perm_ref[base + i]
        first = place * BLOCK
        low = jnp.int32(0)
        row_pos = first + lax.broadcasted_iota(jnp.int32, (BLOCK, HEAD_DIM), 0)
        row_low = jnp.zeros((BLOCK, HEAD_DIM), jnp.int32)
        for s in range(1, SEGMENTS):
            low = jnp.where(starts[s] <= first, starts[s], low)
            row_low = jnp.where(starts[s] <= row_pos, starts[s], row_low)
        low_block = low // BLOCK
        tiles = (place - low_block) // TILE + 1
        rows = pl.ds(pl.multiple_of(i * BLOCK, BLOCK), BLOCK)
        top[...] = jnp.full(top.shape, NEG, jnp.float32)
        acc[...] = jnp.zeros(acc.shape, jnp.float32)
        q = jnp.concatenate(
            [q_ref[rows, j * HEAD_DIM:(j + 1) * HEAD_DIM] for j in range(GROUP)], axis=0
        )

        def gather(ref, t):
            parts = []
            for u in range(TILE):
                block = jnp.minimum(low_block + t * TILE + u, BLOCKS - 1)
                at = pl.multiple_of(inv[block] * BLOCK, BLOCK)
                parts.append(ref[pl.ds(at, BLOCK), :])
            return jnp.concatenate(parts, axis=0)

        def score(t, c):
            s = lax.dot_general(
                q, gather(k_ref, t), (((1,), (1,)), ((), ())), preferred_element_type=jnp.float32
            )
            for half in range(2):
                col = (low_block + t * TILE) * BLOCK + half * HEAD_DIM + lax.broadcasted_iota(
                    jnp.int32, (BLOCK, HEAD_DIM), 1
                )
                seen = (col <= row_pos) & (col >= row_low)
                for j in range(GROUP):
                    at = slice(j * BLOCK, (j + 1) * BLOCK)
                    piece = s[at, half * HEAD_DIM:(half + 1) * HEAD_DIM] * SCALE
                    piece = jnp.where(seen, piece, NEG)
                    scores[t, at, half * HEAD_DIM:(half + 1) * HEAD_DIM] = piece
                    top[at, :] = jnp.maximum(top[at, :], piece)
            return c

        lax.fori_loop(0, tiles, score, 0)
        top[...] = jnp.broadcast_to(jnp.max(top[...], axis=1, keepdims=True), top.shape)

        def blend(t, c):
            peak = top[...]
            weights = jnp.exp2(scores[t] - jnp.concatenate([peak, peak], axis=1)).astype(jnp.bfloat16)
            v = gather(v_ref, t)
            v = jnp.concatenate([v, jnp.ones_like(v)], axis=1)
            acc[...] += jnp.dot(weights, v, preferred_element_type=jnp.float32)
            return c

        lax.fori_loop(0, tiles, blend, 0)
        out = (acc[:, :HEAD_DIM] / acc[:, HEAD_DIM:]).astype(jnp.bfloat16)
        for j in range(GROUP):
            o_ref[rows, j * HEAD_DIM:(j + 1) * HEAD_DIM] = out[j * BLOCK:(j + 1) * BLOCK]
        return carry

    lax.fori_loop(0, blocks, one_block, 0)


def attend(permutation, base, segment, q, k, v):
    smem = pl.BlockSpec(memory_space=pltpu.SMEM)
    vmem = pl.BlockSpec(memory_space=pltpu.VMEM)
    return pl.pallas_call(
        attend_kernel,
        out_shape=jax.ShapeDtypeStruct(q.shape, jnp.bfloat16),
        in_specs=[smem, smem, vmem, vmem, vmem, vmem],
        out_specs=vmem,
        scratch_shapes=[
            pltpu.SMEM((BLOCKS,), jnp.int32),
            pltpu.VMEM((MAX_TILES, ROWS, TILE * BLOCK), jnp.float32),
            pltpu.VMEM((ROWS, 2 * HEAD_DIM), jnp.float32),
            pltpu.VMEM((ROWS, HEAD_DIM), jnp.float32),
        ],
        compiler_params=pltpu.CompilerParams(vmem_limit_bytes=32 << 20),
        name="attend",
    )(permutation, base, segment.reshape(BLOCK, BLOCKS), q, k, v)


def shards(queries, keys, values, permutation, segment):
    rest = ("z_hi", "y", "z_lo")
    q = lax.all_to_all(queries, "x", split_axis=1, concat_axis=0, tiled=True)
    kv = jnp.stack([keys, values])
    kv = lax.all_to_all(kv, "x", split_axis=2, concat_axis=1, tiled=True)
    kv = lax.all_gather(kv, rest, axis=1, tiled=True)
    base = (lax.axis_index(rest) * (q.shape[0] // BLOCK)).astype(jnp.int32)[None]
    o = attend(permutation, base, segment, q, kv[0], kv[1])
    return lax.all_to_all(o, "x", split_axis=0, concat_axis=1, tiled=True)


def solution(mesh):
    fine = Mesh(mesh.devices.reshape(2, 2, 4, 2, 4), ("head", "z_hi", "y", "z_lo", "x"))
    slots = ("z_hi", "y", "z_lo", "x")
    return jax.shard_map(
        shards,
        mesh=fine,
        in_specs=(P(slots, "head"), P(slots, "head"), P(slots, "head"), P(), P()),
        out_specs=P(slots, "head"),
        check_vma=False,
    )
```

```python
import functools
import math

import jax
import jax.numpy as jnp
from jax import lax
from jax.experimental import pallas as pl
from jax.experimental.pallas import tpu as pltpu
from jax.sharding import Mesh, PartitionSpec as P

HEAD_DIM = 128
BLOCK = 64
BLOCKS = 128
SEQ = 8192
SEGMENTS = 8
GROUP = 4
TILE = 4
MAX_TILES = 9
ROWS = GROUP * BLOCK
SCALE = math.log2(math.e) / math.sqrt(HEAD_DIM)
NEG = -1e30
MESH = pl.DeviceIdType.MESH
AXES = ("head", "z_hi", "y", "z_lo", "x")
RING = 4
LOCAL = 128
PART = RING * LOCAL
WIDE = GROUP * HEAD_DIM


def landing_row(slot):
    z = slot // 64 * 2 + slot // 8 % 2
    y = slot // 16 % 4
    return (z * RING + y) * 2 * PART + slot % 8 * BLOCK


def place():
    core, z_hi, y, z_lo, x = (lax.axis_index(a) for a in AXES)
    z = z_hi * 2 + z_lo

    def at(dx=0, dy=0, dz=0):
        far_z = lax.rem(z + dz + RING, RING)
        far_y = lax.rem(y + dy + RING, RING)
        far_x = lax.rem(x + dx + RING, RING)
        return (core, far_z // 2, far_y, lax.rem(far_z, 2), far_x)

    return x, y, z, at


def greet(devices):
    barrier = pltpu.get_barrier_semaphore()
    for device in devices:
        pl.semaphore_signal(barrier, inc=1, device_id=device, device_id_type=MESH)
    pl.semaphore_wait(barrier, len(devices))


def spread_kernel(q_ref, k_ref, v_ref, q_out, kv_out, send_sem, recv_sem, local_sem):
    x, y, z, at = place()
    greet([at(dx=d) for d in (1, 2, 3)] + [at(dy=1), at(dy=-1), at(dz=1), at(dz=-1)])
    count = [0]
    sent = []

    def send(src, dst, device):
        n = count[0]
        count[0] += 1
        copy = pltpu.make_async_remote_copy(
            src_ref=src,
            dst_ref=dst,
            send_sem=send_sem.at[n],
            recv_sem=recv_sem.at[n],
            device_id=device,
            device_id_type=MESH,
        )
        copy.start()
        sent.append(copy)
        return copy

    def columns(j, width):
        return pl.ds(pl.multiple_of(j * width, width), width)

    mine = pl.ds(pl.multiple_of(x * LOCAL, LOCAL), LOCAL)
    first = []
    for d in (1, 3, 2):
        j = lax.rem(x + d, RING)
        for part, ref in ((0, k_ref), (1, v_ref)):
            first.append(
                send(ref.at[:, columns(j, HEAD_DIM)], kv_out.at[z, y, part, mine], at(dx=d))
            )
    local = []
    for n, (src, dst) in enumerate((
        (k_ref.at[:, columns(x, HEAD_DIM)], kv_out.at[z, y, 0, mine]),
        (v_ref.at[:, columns(x, HEAD_DIM)], kv_out.at[z, y, 1, mine]),
        (q_ref.at[:, columns(x, WIDE)], q_out.at[x]),
    )):
        copy = pltpu.make_async_copy(src, dst, local_sem.at[n])
        copy.start()
        local.append(copy)
    for copy in local[:2]:
        copy.wait()
    for copy in first:
        copy.wait_recv()

    def step(part, along):
        def go(d):
            return at(dy=d) if along == "y" else at(dz=d)

        def ref(shift, other):
            here = lax.rem((y if along == "y" else z) + shift + RING, RING)
            return kv_out.at[other, here, part] if along == "y" else kv_out.at[here, other, part]

        def out(other):
            piece = ref(0, other)
            return send(piece, piece, go(1)), send(piece, piece, go(-1))

        def hand_on(pair, other):
            up, down = pair
            up.wait_recv()
            low = ref(-1, other).at[pl.ds(0, PART // 2)]
            far_up = send(low, low, go(1))
            down.wait_recv()
            high = ref(1, other).at[pl.ds(PART // 2, PART // 2)]
            far_down = send(high, high, go(-1))
            return far_up, far_down

        return out, hand_on

    def turn(value, shift):
        return lax.rem(value + shift + RING, RING)

    k_out1, k_on1 = step(0, "y")
    v_out1, v_on1 = step(1, "z")
    k_out2, k_on2 = step(0, "z")
    v_out2, v_on2 = step(1, "y")
    k_one = k_out1(z)
    v_one = v_out1(y)
    k_two = [k_out2(y)]
    v_two = [v_out2(z)]
    for d in (1, 3, 2):
        j = lax.rem(x + d, RING)
        first.append(send(q_ref.at[:, columns(j, WIDE)], q_out.at[x], at(dx=d)))
    k_far = k_on1(k_one, z)
    v_far = v_on1(v_one, y)
    for d in (-1, 1):
        k_two.append(k_out2(turn(y, d)))
        v_two.append(v_out2(turn(z, d)))
    k_last = list(k_on2(k_two[0], y))
    v_last = list(v_on2(v_two[0], z))
    for copy in k_far + v_far:
        copy.wait_recv()
    k_two.append(k_out2(turn(y, 2)))
    v_two.append(v_out2(turn(z, 2)))
    for n, d in ((1, -1), (2, 1), (3, 2)):
        k_last += k_on2(k_two[n], turn(y, d))
        v_last += v_on2(v_two[n], turn(z, d))
    for copy in k_last + v_last + first[6:]:
        copy.wait_recv()
    local[2].wait()
    for copy in sent:
        copy.wait_send()


SPREAD = 6 + 3 + 2 * 4 + 2 * 16


def spread(q, k, v):
    hbm = pl.BlockSpec(memory_space=pl.ANY)
    return pl.pallas_call(
        spread_kernel,
        out_shape=(
            jax.ShapeDtypeStruct((RING, LOCAL, WIDE), jnp.bfloat16),
            jax.ShapeDtypeStruct((RING, RING, 2, PART, HEAD_DIM), jnp.bfloat16),
        ),
        in_specs=[hbm] * 3,
        out_specs=(hbm, hbm),
        scratch_shapes=[
            pltpu.SemaphoreType.DMA((SPREAD,)),
            pltpu.SemaphoreType.DMA((SPREAD,)),
            pltpu.SemaphoreType.DMA((3,)),
        ],
        compiler_params=pltpu.CompilerParams(collective_id=0, has_side_effects=True),
        name="spread",
    )(q, k, v)


def collect_kernel(o_ref, out_ref, send_sem, recv_sem, local_sem):
    x, y, z, at = place()
    greet([at(dx=d) for d in (1, 2, 3)])
    mine = pl.ds(pl.multiple_of(x * WIDE, WIDE), WIDE)
    copies = []
    for n, d in enumerate((1, 3, 2)):
        copy = pltpu.make_async_remote_copy(
            src_ref=o_ref.at[lax.rem(x + d, RING)],
            dst_ref=out_ref.at[:, mine],
            send_sem=send_sem.at[n],
            recv_sem=recv_sem.at[n],
            device_id=at(dx=d),
            device_id_type=MESH,
        )
        copy.start()
        copies.append(copy)
    local = pltpu.make_async_copy(o_ref.at[x], out_ref.at[:, mine], local_sem)
    local.start()
    local.wait()
    for copy in copies:
        copy.wait()


def collect(o):
    hbm = pl.BlockSpec(memory_space=pl.ANY)
    return pl.pallas_call(
        collect_kernel,
        out_shape=jax.ShapeDtypeStruct((LOCAL, RING * WIDE), jnp.bfloat16),
        in_specs=[hbm],
        out_specs=hbm,
        scratch_shapes=[
            pltpu.SemaphoreType.DMA((3,)),
            pltpu.SemaphoreType.DMA((3,)),
            pltpu.SemaphoreType.DMA,
        ],
        compiler_params=pltpu.CompilerParams(collective_id=1, has_side_effects=True),
        name="collect",
    )(o)


def attend_kernel(perm_ref, base_ref, seg_ref, q_ref, kv_ref, o_ref, inv, scores, acc, top):
    for slot in range(BLOCKS):
        inv[perm_ref[slot]] = landing_row(slot)
    seg = seg_ref[...]
    starts = [jnp.int32(0)] + [jnp.sum((seg < s).astype(jnp.int32)) for s in range(1, SEGMENTS)]
    base = base_ref[0]
    blocks = q_ref.shape[0] // BLOCK

    def one_block(i, carry):
        place = perm_ref[base + i]
        first = place * BLOCK
        low = jnp.int32(0)
        row_pos = first + lax.broadcasted_iota(jnp.int32, (BLOCK, HEAD_DIM), 0)
        row_low = jnp.zeros((BLOCK, HEAD_DIM), jnp.int32)
        for s in range(1, SEGMENTS):
            low = jnp.where(starts[s] <= first, starts[s], low)
            row_low = jnp.where(starts[s] <= row_pos, starts[s], row_low)
        low_block = low // BLOCK
        tiles = (place - low_block) // TILE + 1
        rows = pl.ds(pl.multiple_of(i * BLOCK, BLOCK), BLOCK)
        top[...] = jnp.full(top.shape, NEG, jnp.float32)
        acc[...] = jnp.zeros(acc.shape, jnp.float32)
        q = jnp.concatenate(
            [q_ref[rows, j * HEAD_DIM:(j + 1) * HEAD_DIM] for j in range(GROUP)], axis=0
        )

        def gather(shift, t):
            parts = []
            for u in range(TILE):
                block = jnp.minimum(low_block + t * TILE + u, BLOCKS - 1)
                at = pl.multiple_of(inv[block] + shift, BLOCK)
                parts.append(kv_ref[pl.ds(at, BLOCK), :])
            return jnp.concatenate(parts, axis=0)

        def score(t, c):
            s = lax.dot_general(
                q, gather(0, t), (((1,), (1,)), ((), ())), preferred_element_type=jnp.float32
            )
            for half in range(2):
                col = (low_block + t * TILE) * BLOCK + half * HEAD_DIM + lax.broadcasted_iota(
                    jnp.int32, (BLOCK, HEAD_DIM), 1
                )
                seen = (col <= row_pos) & (col >= row_low)
                for j in range(GROUP):
                    at = slice(j * BLOCK, (j + 1) * BLOCK)
                    piece = s[at, half * HEAD_DIM:(half + 1) * HEAD_DIM] * SCALE
                    piece = jnp.where(seen, piece, NEG)
                    scores[t, at, half * HEAD_DIM:(half + 1) * HEAD_DIM] = piece
                    top[at, :] = jnp.maximum(top[at, :], piece)
            return c

        lax.fori_loop(0, tiles, score, 0)
        top[...] = jnp.broadcast_to(jnp.max(top[...], axis=1, keepdims=True), top.shape)

        def blend(t, c):
            peak = top[...]
            weights = jnp.exp2(scores[t] - jnp.concatenate([peak, peak], axis=1)).astype(jnp.bfloat16)
            v = gather(PART, t)
            v = jnp.concatenate([v, jnp.ones_like(v)], axis=1)
            acc[...] += jnp.dot(weights, v, preferred_element_type=jnp.float32)
            return c

        lax.fori_loop(0, tiles, blend, 0)
        out = (acc[:, :HEAD_DIM] / acc[:, HEAD_DIM:]).astype(jnp.bfloat16)
        for j in range(GROUP):
            o_ref[rows, j * HEAD_DIM:(j + 1) * HEAD_DIM] = out[j * BLOCK:(j + 1) * BLOCK]
        return carry

    lax.fori_loop(0, blocks, one_block, 0)


def attend(permutation, base, segment, q, kv):
    smem = pl.BlockSpec(memory_space=pltpu.SMEM)
    vmem = pl.BlockSpec(memory_space=pltpu.VMEM)
    return pl.pallas_call(
        attend_kernel,
        out_shape=jax.ShapeDtypeStruct(q.shape, jnp.bfloat16),
        in_specs=[smem, smem, vmem, vmem, vmem],
        out_specs=vmem,
        scratch_shapes=[
            pltpu.SMEM((BLOCKS,), jnp.int32),
            pltpu.VMEM((MAX_TILES, ROWS, TILE * BLOCK), jnp.float32),
            pltpu.VMEM((ROWS, 2 * HEAD_DIM), jnp.float32),
            pltpu.VMEM((ROWS, HEAD_DIM), jnp.float32),
        ],
        compiler_params=pltpu.CompilerParams(vmem_limit_bytes=32 << 20),
        name="attend",
    )(permutation, base, segment.reshape(BLOCK, BLOCKS), q, kv)


def shards(queries, keys, values, permutation, segment):
    q, kv = spread(queries, keys, values)
    base = (lax.axis_index(AXES[1:4]) * (RING * LOCAL // BLOCK)).astype(jnp.int32)[None]
    o = attend(permutation, base, segment, q.reshape(PART, WIDE), kv.reshape(-1, HEAD_DIM))
    return collect(o.reshape(RING, LOCAL, WIDE))


def solution(mesh):
    fine = Mesh(mesh.devices.reshape(2, 2, 4, 2, 4), AXES)
    slots = AXES[1:]
    return jax.shard_map(
        shards,
        mesh=fine,
        in_specs=(P(slots, "head"), P(slots, "head"), P(slots, "head"), P(), P()),
        out_specs=P(slots, "head"),
        check_vma=False,
    )
```

```python
import functools
import math

import jax
import jax.numpy as jnp
from jax import lax
from jax.experimental import pallas as pl
from jax.experimental.pallas import tpu as pltpu
from jax.sharding import Mesh, PartitionSpec as P

HEAD_DIM = 128
BLOCK = 64
BLOCKS = 128
SEQ = 8192
SEGMENTS = 8
GROUP = 4
TILE = 4
MAX_TILES = 9
ROWS = GROUP * BLOCK
SCALE = math.log2(math.e) / math.sqrt(HEAD_DIM)
NEG = -1e30
MESH = pl.DeviceIdType.MESH
AXES = ("head", "z_hi", "y", "z_lo", "x")
RING = 4
LOCAL = 128
PART = RING * LOCAL
WIDE = GROUP * HEAD_DIM


def landing_row(slot):
    z = slot // 64 * 2 + slot // 8 % 2
    y = slot // 16 % 4
    return (z * RING + y) * 2 * PART + slot % 8 * BLOCK


def place():
    core, z_hi, y, z_lo, x = (lax.axis_index(a) for a in AXES)
    z = z_hi * 2 + z_lo

    def at(dx=0, dy=0, dz=0):
        far_z = lax.rem(z + dz + RING, RING)
        far_y = lax.rem(y + dy + RING, RING)
        far_x = lax.rem(x + dx + RING, RING)
        return (core, far_z // 2, far_y, lax.rem(far_z, 2), far_x)

    return x, y, z, at


def greet(devices):
    barrier = pltpu.get_barrier_semaphore()
    for device in devices:
        pl.semaphore_signal(barrier, inc=1, device_id=device, device_id_type=MESH)
    pl.semaphore_wait(barrier, len(devices))


def tables(perm, seg):
    lane = lax.broadcasted_iota(jnp.int32, (1, BLOCKS), 1)
    starts = jnp.zeros((1, BLOCKS), jnp.int32)
    for s in range(1, SEGMENTS):
        count = jnp.sum((seg < s).astype(jnp.int32), axis=1, keepdims=True)
        count = jnp.sum(count, axis=0, keepdims=True)
        starts = jnp.where(lane == s, count, starts)
    slot = lax.broadcasted_iota(jnp.int32, (BLOCKS, BLOCKS), 0)
    block = lax.broadcasted_iota(jnp.int32, (BLOCKS, BLOCKS), 1)
    held = jnp.sum(jnp.where(slot == block, perm, 0), axis=1, keepdims=True)
    inverse = jnp.sum(jnp.where(held == block, landing_row(slot), 0), axis=0, keepdims=True)
    return jnp.concatenate([perm, starts, inverse, jnp.zeros((5, BLOCKS), jnp.int32)], axis=0)


def spread_kernel(
    q_ref, k_ref, v_ref, perm_ref, seg_ref, q_out, kv_out, meta_out, perm, seg, send_sem, recv_sem, local_sem
):
    x, y, z, at = place()
    greet([at(dx=d) for d in (1, 2, 3)] + [at(dy=1), at(dy=-1), at(dz=1), at(dz=-1)])
    count = [0]
    sent = []

    def send(src, dst, device):
        n = count[0]
        count[0] += 1
        copy = pltpu.make_async_remote_copy(
            src_ref=src,
            dst_ref=dst,
            send_sem=send_sem.at[n],
            recv_sem=recv_sem.at[n],
            device_id=device,
            device_id_type=MESH,
        )
        copy.start()
        sent.append(copy)
        return copy

    def columns(j, width):
        return pl.ds(pl.multiple_of(j * width, width), width)

    mine = pl.ds(pl.multiple_of(x * LOCAL, LOCAL), LOCAL)
    first = []
    for d in (1, 3, 2):
        j = lax.rem(x + d, RING)
        for part, ref in ((0, k_ref), (1, v_ref)):
            first.append(
                send(ref.at[:, columns(j, HEAD_DIM)], kv_out.at[z, y, part, mine], at(dx=d))
            )
    local = []
    for n, (src, dst) in enumerate((
        (k_ref.at[:, columns(x, HEAD_DIM)], kv_out.at[z, y, 0, mine]),
        (v_ref.at[:, columns(x, HEAD_DIM)], kv_out.at[z, y, 1, mine]),
        (q_ref.at[:, columns(x, WIDE)], q_out.at[x]),
        (perm_ref, perm),
        (seg_ref, seg),
    )):
        copy = pltpu.make_async_copy(src, dst, local_sem.at[n])
        copy.start()
        local.append(copy)
    for copy in local:
        copy.wait()
    meta_out[...] = tables(perm[...], seg[...])
    for copy in first:
        copy.wait_recv()

    def step(part, along):
        def go(d):
            return at(dy=d) if along == "y" else at(dz=d)

        def ref(shift, other):
            here = lax.rem((y if along == "y" else z) + shift + RING, RING)
            return kv_out.at[other, here, part] if along == "y" else kv_out.at[here, other, part]

        def out(other):
            piece = ref(0, other)
            return send(piece, piece, go(1)), send(piece, piece, go(-1))

        def hand_on(pair, other):
            up, down = pair
            up.wait_recv()
            low = ref(-1, other).at[pl.ds(0, PART // 2)]
            far_up = send(low, low, go(1))
            down.wait_recv()
            high = ref(1, other).at[pl.ds(PART // 2, PART // 2)]
            far_down = send(high, high, go(-1))
            return far_up, far_down

        return out, hand_on

    def turn(value, shift):
        return lax.rem(value + shift + RING, RING)

    k_out1, k_on1 = step(0, "y")
    v_out1, v_on1 = step(1, "z")
    k_out2, k_on2 = step(0, "z")
    v_out2, v_on2 = step(1, "y")
    k_one = k_out1(z)
    v_one = v_out1(y)
    k_two = [k_out2(y)]
    v_two = [v_out2(z)]
    for d in (1, 3, 2):
        j = lax.rem(x + d, RING)
        first.append(send(q_ref.at[:, columns(j, WIDE)], q_out.at[x], at(dx=d)))
    k_far = k_on1(k_one, z)
    v_far = v_on1(v_one, y)
    for d in (-1, 1):
        k_two.append(k_out2(turn(y, d)))
        v_two.append(v_out2(turn(z, d)))
    k_last = list(k_on2(k_two[0], y))
    v_last = list(v_on2(v_two[0], z))
    for copy in k_far + v_far:
        copy.wait_recv()
    k_two.append(k_out2(turn(y, 2)))
    v_two.append(v_out2(turn(z, 2)))
    for n, d in ((1, -1), (2, 1), (3, 2)):
        k_last += k_on2(k_two[n], turn(y, d))
        v_last += v_on2(v_two[n], turn(z, d))
    for copy in k_last + v_last + first[6:]:
        copy.wait_recv()
    for copy in sent:
        copy.wait_send()


SPREAD = 6 + 3 + 2 * 4 + 2 * 16


def spread(q, k, v, permutation, segment):
    hbm = pl.BlockSpec(memory_space=pltpu.HBM)
    vmem = pl.BlockSpec(memory_space=pltpu.VMEM)
    return pl.pallas_call(
        spread_kernel,
        out_shape=(
            jax.ShapeDtypeStruct((RING, LOCAL, WIDE), jnp.bfloat16),
            jax.ShapeDtypeStruct((RING, RING, 2, PART, HEAD_DIM), jnp.bfloat16),
            jax.ShapeDtypeStruct((8, BLOCKS), jnp.int32),
        ),
        in_specs=[hbm] * 5,
        out_specs=(vmem, vmem, vmem),
        scratch_shapes=[
            pltpu.VMEM((1, BLOCKS), jnp.int32),
            pltpu.VMEM((SEQ // BLOCKS, BLOCKS), jnp.int32),
            pltpu.SemaphoreType.DMA((SPREAD,)),
            pltpu.SemaphoreType.DMA((SPREAD,)),
            pltpu.SemaphoreType.DMA((5,)),
        ],
        compiler_params=pltpu.CompilerParams(
            collective_id=0, has_side_effects=True, vmem_limit_bytes=16 << 20
        ),
        name="spread",
    )(*(
        pltpu.with_memory_space_constraint(a, pltpu.HBM)
        for a in (q, k, v, permutation.reshape(1, BLOCKS), segment.reshape(SEQ // BLOCKS, BLOCKS))
    ))


def collect_kernel(o_ref, out_ref, send_sem, recv_sem, local_sem):
    x, y, z, at = place()
    greet([at(dx=d) for d in (1, 2, 3)])
    mine = pl.ds(pl.multiple_of(x * WIDE, WIDE), WIDE)
    copies = []
    for n, d in enumerate((1, 3, 2)):
        copy = pltpu.make_async_remote_copy(
            src_ref=o_ref.at[lax.rem(x + d, RING)],
            dst_ref=out_ref.at[:, mine],
            send_sem=send_sem.at[n],
            recv_sem=recv_sem.at[n],
            device_id=at(dx=d),
            device_id_type=MESH,
        )
        copy.start()
        copies.append(copy)
    local = pltpu.make_async_copy(o_ref.at[x], out_ref.at[:, mine], local_sem)
    local.start()
    local.wait()
    for copy in copies:
        copy.wait()


def collect(o):
    vmem = pl.BlockSpec(memory_space=pltpu.VMEM)
    return pl.pallas_call(
        collect_kernel,
        out_shape=jax.ShapeDtypeStruct((LOCAL, RING * WIDE), jnp.bfloat16),
        in_specs=[vmem],
        out_specs=vmem,
        scratch_shapes=[
            pltpu.SemaphoreType.DMA((3,)),
            pltpu.SemaphoreType.DMA((3,)),
            pltpu.SemaphoreType.DMA,
        ],
        compiler_params=pltpu.CompilerParams(
            collective_id=1, has_side_effects=True, vmem_limit_bytes=4 << 20
        ),
        name="collect",
    )(o)


def attend_kernel(meta_ref, base_ref, q_ref, kv_ref, o_ref):
    base = base_ref[0]
    blocks = q_ref.shape[0] // BLOCK

    def one_block(i, carry):
        block = meta_ref[0, base + i]
        first = block * BLOCK
        low = jnp.int32(0)
        row_pos = first + lax.broadcasted_iota(jnp.int32, (BLOCK, HEAD_DIM), 0)
        row_low = jnp.zeros((BLOCK, HEAD_DIM), jnp.int32)
        for s in range(1, SEGMENTS):
            start = meta_ref[1, s]
            low = jnp.where(start <= first, start, low)
            row_low = jnp.where(start <= row_pos, start, row_low)
        low_block = low // BLOCK
        tiles = (block - low_block) // TILE + 1
        rows = pl.ds(pl.multiple_of(i * BLOCK, BLOCK), BLOCK)

        def gather(shift, t):
            parts = []
            for u in range(TILE):
                there = jnp.minimum(low_block + t * TILE + u, BLOCKS - 1)
                at = pl.multiple_of(meta_ref[2, there] + shift, BLOCK)
                parts.append(kv_ref[pl.ds(at, BLOCK), :])
            return jnp.concatenate(parts, axis=0)

        def whole(count):
            q = jnp.concatenate(
                [q_ref[rows, j * HEAD_DIM:(j + 1) * HEAD_DIM] for j in range(GROUP)], axis=0
            )
            scores = []
            top = None
            for t in range(count):
                s = lax.dot_general(
                    q, gather(0, t), (((1,), (1,)), ((), ())), preferred_element_type=jnp.float32
                )
                for half in range(2):
                    col = (low_block + t * TILE) * BLOCK + half * HEAD_DIM + lax.broadcasted_iota(
                        jnp.int32, (BLOCK, HEAD_DIM), 1
                    )
                    seen = (col <= row_pos) & (col >= row_low)
                    seen = jnp.concatenate([seen] * GROUP, axis=0)
                    piece = jnp.where(seen, s[:, half * HEAD_DIM:(half + 1) * HEAD_DIM], NEG)
                    scores.append(piece)
                    top = piece if top is None else jnp.maximum(top, piece)
            top = jnp.max(top, axis=1, keepdims=True)
            total = jnp.zeros((ROWS, 2 * HEAD_DIM), jnp.float32)
            for t in range(count):
                weights = jnp.concatenate(
                    [jnp.exp2((piece - top) * SCALE) for piece in scores[2 * t:2 * t + 2]], axis=1
                ).astype(jnp.bfloat16)
                v = gather(PART, t)
                v = jnp.concatenate([v, jnp.ones_like(v)], axis=1)
                total += jnp.dot(weights, v, preferred_element_type=jnp.float32)
            out = (total[:, :HEAD_DIM] / total[:, HEAD_DIM:]).astype(jnp.bfloat16)
            for j in range(GROUP):
                o_ref[rows, j * HEAD_DIM:(j + 1) * HEAD_DIM] = out[j * BLOCK:(j + 1) * BLOCK]

        for count in range(1, MAX_TILES + 1):
            pl.when(tiles == count)(functools.partial(whole, count))
        return carry

    lax.fori_loop(0, blocks, one_block, 0)


def attend(meta, base, q, kv):
    smem = pl.BlockSpec(memory_space=pltpu.SMEM)
    vmem = pl.BlockSpec(memory_space=pltpu.VMEM)
    return pl.pallas_call(
        attend_kernel,
        out_shape=jax.ShapeDtypeStruct(q.shape, jnp.bfloat16),
        in_specs=[smem, smem, vmem, vmem],
        out_specs=vmem,
        compiler_params=pltpu.CompilerParams(vmem_limit_bytes=24 << 20),
        name="attend",
    )(meta, base, q, kv)


def shards(queries, keys, values, permutation, segment):
    q, kv, meta = spread(queries, keys, values, permutation, segment)
    base = (lax.axis_index(AXES[1:4]) * (RING * LOCAL // BLOCK)).astype(jnp.int32)[None]
    o = attend(meta, base, q.reshape(PART, WIDE), kv.reshape(-1, HEAD_DIM))
    return collect(o.reshape(RING, LOCAL, WIDE))


def solution(mesh):
    fine = Mesh(mesh.devices.reshape(2, 2, 4, 2, 4), AXES)
    slots = AXES[1:]
    return jax.shard_map(
        shards,
        mesh=fine,
        in_specs=(P(slots, "head"), P(slots, "head"), P(slots, "head"), P(), P()),
        out_specs=P(slots, "head"),
        check_vma=False,
    )
```

```python
import functools
import math

import jax
import jax.numpy as jnp
from jax import lax
from jax.experimental import pallas as pl
from jax.experimental.pallas import tpu as pltpu
from jax.sharding import Mesh, PartitionSpec as P

HEAD_DIM = 128
BLOCK = 64
BLOCKS = 128
SEQ = 8192
SEGMENTS = 8
GROUP = 4
TILE = 4
MAX_TILES = 9
ROWS = GROUP * BLOCK
SCALE = math.log2(math.e) / math.sqrt(HEAD_DIM)
NEG = -1e30
MESH = pl.DeviceIdType.MESH
AXES = ("head", "z_hi", "y", "z_lo", "x")
RING = 4
LOCAL = 128
PART = BLOCKS * BLOCK
WIDE = GROUP * HEAD_DIM


def landing_row(slot):
    z = slot // 64 * 2 + slot // 8 % 2
    y = slot // 16 % 4
    return (y * RING + z) * RING * LOCAL + slot % 8 * BLOCK


def place():
    core, z_hi, y, z_lo, x = (lax.axis_index(a) for a in AXES)
    z = z_hi * 2 + z_lo

    def at(to_core, dx=0, dy=0, dz=0):
        far_z, far_y, far_x = turn(z, dz), turn(y, dy), turn(x, dx)
        return (to_core, far_z // 2, far_y, lax.rem(far_z, 2), far_x)

    return core, x, y, z, at


def turn(value, shift):
    return lax.rem(value + shift + RING, RING)


def greet(devices, own=None):
    barrier = pltpu.get_barrier_semaphore()
    count = jnp.int32(len(devices))
    for n, device in enumerate(devices):
        def tell(device=device):
            pl.semaphore_signal(barrier, inc=1, device_id=device, device_id_type=MESH)

        if own is not None and n == own[0]:
            pl.when(jnp.logical_not(own[1]))(tell)
            count -= own[1].astype(jnp.int32)
        else:
            tell()
    pl.semaphore_wait(barrier, count)


class Courier:
    def __init__(self, send_sem, recv_sem):
        self.send_sem, self.recv_sem, self.sent = send_sem, recv_sem, []

    def send(self, src, dst, n, device, here=None):
        copy = pltpu.make_async_remote_copy(
            src_ref=src,
            dst_ref=dst,
            send_sem=self.send_sem.at[len(self.sent)],
            recv_sem=self.recv_sem.at[n],
            device_id=device,
            device_id_type=MESH,
        )
        self.sent.append((copy, here))
        if here is None:
            copy.start()
        else:
            pl.when(jnp.logical_not(here))(copy.start)
            pl.when(here)(pltpu.make_async_copy(src, dst, self.recv_sem.at[n]).start)

    def landed(self, ref, n):
        pltpu.make_async_copy(ref, ref, self.recv_sem.at[n]).wait()

    def finish(self):
        for copy, here in self.sent:
            if here is None:
                copy.wait_send()
            else:
                pl.when(jnp.logical_not(here))(copy.wait_send)


def columns(j, width):
    return pl.ds(pl.multiple_of(j * width, width), width)


def tables(perm, seg):
    lane = lax.broadcasted_iota(jnp.int32, (1, BLOCKS), 1)
    starts = jnp.zeros((1, BLOCKS), jnp.int32)
    for s in range(1, SEGMENTS):
        count = jnp.sum((seg < s).astype(jnp.int32), axis=1, keepdims=True)
        count = jnp.sum(count, axis=0, keepdims=True)
        starts = jnp.where(lane == s, count, starts)
    slot = lax.broadcasted_iota(jnp.int32, (BLOCKS, BLOCKS), 0)
    block = lax.broadcasted_iota(jnp.int32, (BLOCKS, BLOCKS), 1)
    held = jnp.sum(jnp.where(slot == block, perm, 0), axis=1, keepdims=True)
    inverse = jnp.sum(jnp.where(held == block, landing_row(slot), 0), axis=0, keepdims=True)
    return jnp.concatenate([perm, starts, inverse, jnp.zeros((5, BLOCKS), jnp.int32)], axis=0)


def spread_kernel(
    q_ref, k_ref, v_ref, perm_ref, seg_ref, q_out, kv_out, meta_out, perm, seg, send_sem, recv_sem, local_sem
):
    core, x, y, z, at = place()
    odd = lax.rem(z, 2)
    apart = lax.rem(odd + core, 2)
    other = 1 - core
    pair = jnp.where(apart == 0, 0, 1 - 2 * odd)
    home = apart == 0
    givers = [at(odd, dx, 0, dz) for dz in range(RING) for dx in range(RING)]
    greet(givers + [at(core, dy=1), at(core, dy=-1), at(other)], own=(0, home))
    courier = Courier(send_sem, recv_sem)

    for dx in (1, 3, 2, 0):
        j = turn(x, dx)
        for k in range(2):
            for part, ref in ((0, k_ref), (1, v_ref)):
                courier.send(
                    ref.at[:, columns(j, HEAD_DIM)],
                    kv_out.at[part, y, z, x],
                    z * RING + x,
                    at(part, dx, 0, apart + 2 * k),
                    home & (core == part) if dx == 0 and k == 0 else None,
                )
    from_q = 16
    for dx in (1, 3, 2, 0):
        j = turn(x, dx)
        for b in range(2):
            courier.send(
                q_ref.at[b * BLOCK:(b + 1) * BLOCK, columns(j, WIDE)],
                q_out.at[odd * RING + x],
                from_q + odd * RING + x,
                at(b, dx, 0, pair),
                home & (core == b) if dx == 0 else None,
            )
    local = [pltpu.make_async_copy(perm_ref, perm, local_sem.at[0])]
    local.append(pltpu.make_async_copy(seg_ref, seg, local_sem.at[1]))
    for copy in local:
        copy.start()
    for copy in local:
        copy.wait()
    meta_out[...] = tables(perm[...], seg[...])

    below, above, far_below, far_above, beside = 24, 28, 32, 36, 40
    half = RING // 2
    lines = [turn(z, dz) for dz in (0, 1, 3, 2)]

    def share(piece, n):
        courier.send(piece, piece, beside + n, at(other))

    for line in lines:
        piece = kv_out.at[core, y, line]
        for other_x in range(RING):
            courier.landed(kv_out.at[core, y, line, other_x], line * RING + other_x)
        courier.send(piece, piece, below + line, at(core, dy=1))
        courier.send(piece, piece, above + line, at(core, dy=-1))
        share(piece, line)
    for line in lines:
        low, high = kv_out.at[core, turn(y, -1), line], kv_out.at[core, turn(y, 1), line]
        courier.landed(low, below + line)
        courier.send(low.at[:half], low.at[:half], far_below + line, at(core, dy=1))
        share(low, 4 + line)
        courier.landed(high, above + line)
        courier.send(high.at[half:], high.at[half:], far_above + line, at(core, dy=-1))
        share(high, 8 + line)
    for line in lines:
        far = kv_out.at[core, turn(y, 2), line]
        courier.landed(far.at[:half], far_below + line)
        share(far.at[:half], 12 + line)
        courier.landed(far.at[half:], far_above + line)
        share(far.at[half:], 16 + line)
    for n in range(8):
        courier.landed(q_out.at[n], from_q + n)
    for line in range(RING):
        courier.landed(kv_out.at[other, y, line], beside + line)
        courier.landed(kv_out.at[other, turn(y, -1), line], beside + 4 + line)
        courier.landed(kv_out.at[other, turn(y, 1), line], beside + 8 + line)
        courier.landed(kv_out.at[other, turn(y, 2), line, :half], beside + 12 + line)
        courier.landed(kv_out.at[other, turn(y, 2), line, half:], beside + 16 + line)
    courier.finish()


SPREAD = 16 + 8 + 16 + 20


def spread(q, k, v, permutation, segment):
    hbm = pl.BlockSpec(memory_space=pltpu.HBM)
    vmem = pl.BlockSpec(memory_space=pltpu.VMEM)
    return pl.pallas_call(
        spread_kernel,
        out_shape=(
            jax.ShapeDtypeStruct((2 * RING, BLOCK, WIDE), jnp.bfloat16),
            jax.ShapeDtypeStruct((2, RING, RING, RING, LOCAL, HEAD_DIM), jnp.bfloat16),
            jax.ShapeDtypeStruct((8, BLOCKS), jnp.int32),
        ),
        in_specs=[hbm] * 5,
        out_specs=(vmem, vmem, vmem),
        scratch_shapes=[
            pltpu.VMEM((1, BLOCKS), jnp.int32),
            pltpu.VMEM((SEQ // BLOCKS, BLOCKS), jnp.int32),
            pltpu.SemaphoreType.DMA((SPREAD,)),
            pltpu.SemaphoreType.DMA((SPREAD,)),
            pltpu.SemaphoreType.DMA((2,)),
        ],
        compiler_params=pltpu.CompilerParams(
            collective_id=0, has_side_effects=True, vmem_limit_bytes=16 << 20
        ),
        name="spread",
    )(*(
        pltpu.with_memory_space_constraint(a, pltpu.HBM)
        for a in (q, k, v, permutation.reshape(1, BLOCKS), segment.reshape(SEQ // BLOCKS, BLOCKS))
    ))


def collect_kernel(o_ref, out_ref, send_sem, recv_sem):
    core, x, y, z, at = place()
    odd = lax.rem(z, 2)
    apart = lax.rem(odd + core, 2)
    pair = jnp.where(apart == 0, 0, 1 - 2 * odd)
    home = apart == 0
    greet(
        [at(core, 0, 0, pair), at(1 - core, 0, 0, pair)]
        + [at(b, dx, 0, pair) for dx in (1, 3, 2) for b in range(2)],
        own=(0, home),
    )
    courier = Courier(send_sem, recv_sem)
    rows = pl.ds(pl.multiple_of(core * BLOCK, BLOCK), BLOCK)
    for dx in (2, 1, 3, 0):
        for dz in range(2):
            to_odd = lax.rem(odd + dz, 2)
            courier.send(
                o_ref.at[to_odd * RING + turn(x, dx)],
                out_ref.at[rows, columns(x, WIDE)],
                core * RING + x,
                at(odd, dx, 0, to_odd - odd),
                home if dx == 0 and dz == 0 else None,
            )
    for b in range(2):
        for j in range(RING):
            courier.landed(
                out_ref.at[b * BLOCK:(b + 1) * BLOCK, j * WIDE:(j + 1) * WIDE], b * RING + j
            )
    courier.finish()


def collect(o):
    vmem = pl.BlockSpec(memory_space=pltpu.VMEM)
    return pl.pallas_call(
        collect_kernel,
        out_shape=jax.ShapeDtypeStruct((LOCAL, RING * WIDE), jnp.bfloat16),
        in_specs=[vmem],
        out_specs=vmem,
        scratch_shapes=[
            pltpu.SemaphoreType.DMA((2 * RING,)),
            pltpu.SemaphoreType.DMA((2 * RING,)),
        ],
        compiler_params=pltpu.CompilerParams(
            collective_id=1, has_side_effects=True, vmem_limit_bytes=4 << 20
        ),
        name="collect",
    )(o)


def attend_kernel(meta_ref, base_ref, q_ref, kv_ref, o_ref):
    base = base_ref[0]
    blocks = q_ref.shape[0] // BLOCK

    def one_block(i, carry):
        block = meta_ref[0, base + 2 * i]
        first = block * BLOCK
        low = jnp.int32(0)
        row_pos = first + lax.broadcasted_iota(jnp.int32, (BLOCK, HEAD_DIM), 0)
        row_low = jnp.zeros((BLOCK, HEAD_DIM), jnp.int32)
        for s in range(1, SEGMENTS):
            start = meta_ref[1, s]
            low = jnp.where(start <= first, start, low)
            row_low = jnp.where(start <= row_pos, start, row_low)
        low_block = low // BLOCK
        tiles = (block - low_block) // TILE + 1
        rows = pl.ds(pl.multiple_of(i * BLOCK, BLOCK), BLOCK)

        def gather(shift, t):
            parts = []
            for u in range(TILE):
                there = jnp.minimum(low_block + t * TILE + u, BLOCKS - 1)
                at = pl.multiple_of(meta_ref[2, there] + shift, BLOCK)
                parts.append(kv_ref[pl.ds(at, BLOCK), :])
            return jnp.concatenate(parts, axis=0)

        def whole(count):
            q = jnp.concatenate(
                [q_ref[rows, j * HEAD_DIM:(j + 1) * HEAD_DIM] for j in range(GROUP)], axis=0
            )
            scores = []
            top = None
            for t in range(count):
                s = lax.dot_general(
                    q, gather(0, t), (((1,), (1,)), ((), ())), preferred_element_type=jnp.float32
                )
                for half in range(2):
                    col = (low_block + t * TILE) * BLOCK + half * HEAD_DIM + lax.broadcasted_iota(
                        jnp.int32, (BLOCK, HEAD_DIM), 1
                    )
                    seen = (col <= row_pos) & (col >= row_low)
                    seen = jnp.concatenate([seen] * GROUP, axis=0)
                    piece = jnp.where(seen, s[:, half * HEAD_DIM:(half + 1) * HEAD_DIM], NEG)
                    scores.append(piece)
                    top = piece if top is None else jnp.maximum(top, piece)
            top = jnp.max(top, axis=1, keepdims=True)
            total = jnp.zeros((ROWS, 2 * HEAD_DIM), jnp.float32)
            for t in range(count):
                weights = jnp.concatenate(
                    [jnp.exp2((piece - top) * SCALE) for piece in scores[2 * t:2 * t + 2]], axis=1
                ).astype(jnp.bfloat16)
                v = gather(PART, t)
                v = jnp.concatenate([v, jnp.ones_like(v)], axis=1)
                total += jnp.dot(weights, v, preferred_element_type=jnp.float32)
            out = (total[:, :HEAD_DIM] / total[:, HEAD_DIM:]).astype(jnp.bfloat16)
            for j in range(GROUP):
                o_ref[rows, j * HEAD_DIM:(j + 1) * HEAD_DIM] = out[j * BLOCK:(j + 1) * BLOCK]

        for count in range(1, MAX_TILES + 1):
            pl.when(tiles == count)(functools.partial(whole, count))
        return carry

    lax.fori_loop(0, blocks, one_block, 0)


def attend(meta, base, q, kv):
    smem = pl.BlockSpec(memory_space=pltpu.SMEM)
    vmem = pl.BlockSpec(memory_space=pltpu.VMEM)
    return pl.pallas_call(
        attend_kernel,
        out_shape=jax.ShapeDtypeStruct(q.shape, jnp.bfloat16),
        in_specs=[smem, smem, vmem, vmem],
        out_specs=vmem,
        compiler_params=pltpu.CompilerParams(vmem_limit_bytes=24 << 20),
        name="attend",
    )(meta, base, q, kv)


def shards(queries, keys, values, permutation, segment):
    q, kv, meta = spread(queries, keys, values, permutation, segment)
    first = lax.axis_index(AXES[1:3]) * 16 + lax.axis_index("head")
    o = attend(meta, first.astype(jnp.int32)[None], q.reshape(-1, WIDE), kv.reshape(-1, HEAD_DIM))
    return collect(o.reshape(q.shape))


def solution(mesh):
    fine = Mesh(mesh.devices.reshape(2, 2, 4, 2, 4), AXES)
    slots = AXES[1:]
    return jax.shard_map(
        shards,
        mesh=fine,
        in_specs=(P(slots, "head"), P(slots, "head"), P(slots, "head"), P(), P()),
        out_specs=P(slots, "head"),
        check_vma=False,
    )
```

```python
import math

import jax
import jax.numpy as jnp
from jax import lax
from jax.experimental import pallas as pl
from jax.experimental.pallas import tpu as pltpu
from jax.sharding import Mesh, PartitionSpec as P

HEAD_DIM = 128
BLOCK = 64
BLOCKS = 128
SEQ = 8192
SEGMENTS = 8
GROUP = 4
RING = 4
LOCAL = 128
ROWS = GROUP * BLOCK
WIDE = GROUP * HEAD_DIM
HELD = 2 * RING
REACH = 34
WIDTH = REACH * BLOCK
SCALE = math.log2(math.e) / math.sqrt(HEAD_DIM)
NEG = -1e30
MESH = pl.DeviceIdType.MESH
AXES = ("head", "z_hi", "y", "z_lo", "x")


def landing(slot):
    z = slot // 64 * 2 + slot // 8 % 2
    y = slot // 16 % 4
    return (z * RING + y) * HELD + slot % 8


def turn(value, shift):
    return lax.rem(value + shift + RING, RING)


def stored(ref, z, y, x, count):
    return ref.at[pl.ds(((z * RING + y) * RING + x) * 2, 2 * count)]


def columns(j, width):
    return pl.ds(pl.multiple_of(j * width, width), width)


def tables(perm, seg):
    lane = lax.broadcasted_iota(jnp.int32, (1, BLOCKS), 1)
    starts = jnp.zeros((1, BLOCKS), jnp.int32)
    for s in range(1, SEGMENTS):
        count = jnp.sum((seg < s).astype(jnp.int32), axis=1, keepdims=True)
        count = jnp.sum(count, axis=0, keepdims=True)
        starts = jnp.where(lane == s, count, starts)
    slot = lax.broadcasted_iota(jnp.int32, (BLOCKS, BLOCKS), 0)
    block = lax.broadcasted_iota(jnp.int32, (BLOCKS, BLOCKS), 1)
    held = jnp.sum(jnp.where(slot == block, perm, 0), axis=1, keepdims=True)
    inverse = jnp.sum(jnp.where(held == block, landing(slot), 0), axis=0, keepdims=True)
    inverse = jnp.minimum(inverse, BLOCKS - 1)
    return jnp.concatenate([perm, starts, inverse, jnp.zeros((5, BLOCKS), jnp.int32)], axis=0)


def episode_kernel(
    q_ref, k_ref, v_ref, perm_ref, seg_ref, out_ref,
    perm, seg, meta_vec, meta, q_all, k_all, v_all, weights, scale, o_all,
    send_sem, recv_sem, o_send, o_recv, local_sem,
):
    core, z_hi, y, z_lo, x = (lax.axis_index(a) for a in AXES)
    z = z_hi * 2 + z_lo

    def at(dx=0, dy=0, dz=0):
        far_z = turn(z, dz)
        return (core, far_z // 2, turn(y, dy), lax.rem(far_z, 2), turn(x, dx))

    barrier = pltpu.get_barrier_semaphore()
    partners = [at(dx=d) for d in (1, 2, 3)] + [at(dy=1), at(dy=-1), at(dz=1), at(dz=-1)]
    for device in partners:
        pl.semaphore_signal(barrier, inc=1, device_id=device, device_id_type=MESH)
    local = [
        pltpu.make_async_copy(src, dst, local_sem.at[n])
        for n, (src, dst) in enumerate((
            (k_ref.at[:, :, columns(x, HEAD_DIM)], stored(k_all, z, y, x, 1)),
            (v_ref.at[:, :, columns(x, HEAD_DIM)], stored(v_all, z, y, x, 1)),
            (q_ref.at[:, :, columns(x, WIDE)], q_all.at[pl.ds(2 * x, 2)]),
            (perm_ref, perm),
            (seg_ref, seg),
        ))
    ]
    for copy in local:
        copy.start()
    pl.semaphore_wait(barrier, len(partners))

    sent = []

    def send(src, dst, device):
        n = len(sent)
        copy = pltpu.make_async_remote_copy(
            src_ref=src,
            dst_ref=dst,
            send_sem=send_sem.at[n],
            recv_sem=recv_sem.at[n],
            device_id=device,
            device_id_type=MESH,
        )
        copy.start()
        sent.append(copy)
        return copy

    def exchange(src, width, dst):
        return [
            send(src.at[:, :, columns(turn(x, d), width)], dst, at(dx=d)) for d in (1, 3, 2)
        ]

    k_first = exchange(k_ref, HEAD_DIM, stored(k_all, z, y, x, 1))
    v_first = exchange(v_ref, HEAD_DIM, stored(v_all, z, y, x, 1))
    q_first = exchange(q_ref, WIDE, q_all.at[pl.ds(2 * x, 2)])
    for copy in local:
        copy.wait()
    meta_vec[...] = tables(perm[...], seg[...])
    to_scalars = pltpu.make_async_copy(meta_vec, meta, local_sem.at[5])
    to_scalars.start()
    to_scalars.wait()

    def gather(ref, first):
        def line(half, along_y):
            lo = 2 * half

            def piece(shift, other, which=None):
                here = turn(y if along_y else z, shift)
                spot = (other, here) if along_y else (here, other)
                return stored(ref, *spot, lo, 2) if which is None else stored(ref, *spot, lo + which, 1)

            def go(d):
                return at(dy=d) if along_y else at(dz=d)

            def out(other):
                here = piece(0, other)
                return send(here, here, go(1)), send(here, here, go(-1))

            def hand_on(pair, other):
                pair[0].wait_recv()
                low = piece(-1, other, 0)
                far = [send(low, low, go(1))]
                pair[1].wait_recv()
                high = piece(1, other, 1)
                return far + [send(high, high, go(-1))]

            return out, hand_on

        halves = []
        for half in range(2):
            out1, on1 = line(half, half == 0)
            out2, on2 = line(half, half == 1)
            mine1, mine2 = (z, y) if half == 0 else (y, z)
            halves.append((out1, on1, out2, on2, mine1, mine2))
        for copy in first:
            copy.wait_recv()
        one = [h[0](h[4]) for h in halves]
        yield
        two = [[h[2](h[5])] for h in halves]
        yield
        far = [h[1](pair, h[4]) for h, pair in zip(halves, one)]
        for d in (-1, 1):
            for h, pairs in zip(halves, two):
                pairs.append(h[2](turn(h[5], d)))
        yield
        last = []
        for h, pairs in zip(halves, two):
            last += h[3](pairs[0], h[5])
        yield
        for copies in far:
            for copy in copies:
                copy.wait_recv()
        for h, pairs in zip(halves, two):
            pairs.append(h[2](turn(h[5], 2)))
        yield
        for n, d in ((1, -1), (2, 1)):
            for h, pairs in zip(halves, two):
                last += h[3](pairs[n], turn(h[5], d))
        yield
        for h, pairs in zip(halves, two):
            last += h[3](pairs[3], turn(h[5], 2))
        yield
        for copy in last:
            copy.wait_recv()
        yield

    k_steps, v_steps = gather(k_all, k_first), gather(v_all, v_first)
    for step in "kkvkvkvkkkk":
        next(k_steps if step == "k" else v_steps)
    for copy in q_first:
        copy.wait_recv()

    base = (z_hi * 8 + y * 2 + z_lo) * HELD

    def rows_of(ref, block, start, count):
        parts = []
        for u in range(count):
            there = jnp.clip(block - (REACH - 1) + start + u, 0, BLOCKS - 1)
            parts.append(ref[meta[2, there]])
        return jnp.concatenate(parts, axis=0)

    def score(i, carry):
        block = meta[0, base + i]
        row_pos = block * BLOCK + lax.broadcasted_iota(jnp.int32, (BLOCK, HEAD_DIM), 0)
        row_low = jnp.zeros((BLOCK, HEAD_DIM), jnp.int32)
        for s in range(1, SEGMENTS):
            row_low = jnp.where(meta[1, s] <= row_pos, meta[1, s], row_low)
        q = jnp.concatenate(
            [q_all[i, :, j * HEAD_DIM:(j + 1) * HEAD_DIM] for j in range(GROUP)], axis=0
        )
        pieces = []
        top = None
        for start in range(-2, REACH - 2, 4):
            begin, count = max(start, 0), 4 + min(start, 0)
            s = lax.dot_general(
                q, rows_of(k_all, block, begin, count), (((1,), (1,)), ((), ())),
                preferred_element_type=jnp.float32,
            )
            for half in range(count // 2):
                index = begin + 2 * half
                col = (block - (REACH - 1) + index) * BLOCK + lax.broadcasted_iota(
                    jnp.int32, (BLOCK, HEAD_DIM), 1
                )
                seen = col >= row_low
                if index == REACH - 2:
                    seen = seen & (col <= row_pos)
                seen = jnp.concatenate([seen] * GROUP, axis=0)
                piece = jnp.where(seen, s[:, half * HEAD_DIM:(half + 1) * HEAD_DIM], NEG)
                pieces.append(piece)
                top = piece if top is None else jnp.maximum(top, piece)
        top = jnp.max(top, axis=1, keepdims=True)
        total = None
        for n, piece in enumerate(pieces):
            weight = jnp.exp2((piece - top) * SCALE)
            total = weight if total is None else total + weight
            weights[i, :, n * HEAD_DIM:(n + 1) * HEAD_DIM] = weight.astype(jnp.bfloat16)
        total = jnp.sum(total, axis=1, keepdims=True)
        scale[i] = jnp.broadcast_to(1.0 / total, (ROWS, HEAD_DIM))
        return carry

    for pair in range(4):
        lax.fori_loop(2 * pair, 2 * pair + 2, score, 0)
        next(v_steps)
    for _ in v_steps:
        pass

    def blend(i):
        block = meta[0, base + i]
        mixed = jnp.dot(weights[i], rows_of(v_all, block, 0, REACH), preferred_element_type=jnp.float32)
        return (mixed * scale[i]).astype(jnp.bfloat16)

    def place(ref, mixed):
        for j in range(GROUP):
            ref[:, j * HEAD_DIM:(j + 1) * HEAD_DIM] = mixed[j * BLOCK:(j + 1) * BLOCK]

    def answer(n):
        d = 3 - n // 2
        rows = pl.ds(pl.multiple_of(lax.rem(n, 2) * BLOCK, BLOCK), BLOCK)
        return pltpu.make_async_remote_copy(
            src_ref=o_all.at[n],
            dst_ref=out_ref.at[rows, columns(x, WIDE)],
            send_sem=o_send.at[n],
            recv_sem=o_recv.at[n],
            device_id=at(dx=d),
            device_id_type=MESH,
        )

    def away(n, carry):
        i = 2 * turn(x, 3 - n // 2) + lax.rem(n, 2)
        place(o_all.at[n], blend(i))
        answer(n).start()
        return carry

    def here(n, carry):
        rows = pl.ds(pl.multiple_of(n * BLOCK, BLOCK), BLOCK)
        place(out_ref.at[rows, columns(x, WIDE)], blend(2 * x + n))
        return carry

    lax.fori_loop(0, 6, away, 0)
    lax.fori_loop(0, 2, here, 0)
    for copy in sent:
        copy.wait_send()

    def finish(n, carry):
        answer(n).wait()
        return carry

    lax.fori_loop(0, 6, finish, 0)


COPIES = 9 + 2 * 40


def shards(queries, keys, values, permutation, segment):
    hbm = pl.BlockSpec(memory_space=pltpu.HBM)
    inputs = (
        *(a.reshape(2, BLOCK, -1) for a in (queries, keys, values)),
        permutation.reshape(1, BLOCKS),
        segment.reshape(SEQ // BLOCKS, BLOCKS),
    )
    return pl.pallas_call(
        episode_kernel,
        out_shape=jax.ShapeDtypeStruct(queries.shape, jnp.bfloat16),
        in_specs=[hbm] * 5,
        out_specs=pl.BlockSpec(memory_space=pltpu.VMEM),
        scratch_shapes=[
            pltpu.VMEM((1, BLOCKS), jnp.int32),
            pltpu.VMEM((SEQ // BLOCKS, BLOCKS), jnp.int32),
            pltpu.VMEM((8, BLOCKS), jnp.int32),
            pltpu.SMEM((8, BLOCKS), jnp.int32),
            pltpu.VMEM((HELD, BLOCK, WIDE), jnp.bfloat16),
            pltpu.VMEM((BLOCKS, BLOCK, HEAD_DIM), jnp.bfloat16),
            pltpu.VMEM((BLOCKS, BLOCK, HEAD_DIM), jnp.bfloat16),
            pltpu.VMEM((HELD, ROWS, WIDTH), jnp.bfloat16),
            pltpu.VMEM((HELD, ROWS, HEAD_DIM), jnp.float32),
            pltpu.VMEM((6, BLOCK, WIDE), jnp.bfloat16),
            pltpu.SemaphoreType.DMA((COPIES,)),
            pltpu.SemaphoreType.DMA((COPIES,)),
            pltpu.SemaphoreType.DMA((6,)),
            pltpu.SemaphoreType.DMA((6,)),
            pltpu.SemaphoreType.DMA((6,)),
        ],
        compiler_params=pltpu.CompilerParams(
            collective_id=0, has_side_effects=True, vmem_limit_bytes=40 << 20
        ),
        name="episode",
    )(*(pltpu.with_memory_space_constraint(a, pltpu.HBM) for a in inputs))


def solution(mesh):
    fine = Mesh(mesh.devices.reshape(2, 2, 4, 2, 4), AXES)
    slots = AXES[1:]
    return jax.shard_map(
        shards,
        mesh=fine,
        in_specs=(P(slots, "head"), P(slots, "head"), P(slots, "head"), P(), P()),
        out_specs=P(slots, "head"),
        check_vma=False,
    )
```

```python
import math

import jax
import jax.numpy as jnp
from jax import lax
from jax.experimental import pallas as pl
from jax.experimental.pallas import tpu as pltpu
from jax.sharding import Mesh, PartitionSpec as P

HEAD_DIM = 128
BLOCK = 64
BLOCKS = 128
SEQ = 8192
SEGMENTS = 8
GROUP = 4
RING = 4
LOCAL = 128
ROWS = GROUP * BLOCK
WIDE = GROUP * HEAD_DIM
HELD = 2 * RING
REACH = 34
WIDTH = REACH * BLOCK
SCALE = math.log2(math.e) / math.sqrt(HEAD_DIM)
NEG = -1e30
MESH = pl.DeviceIdType.MESH
AXES = ("head", "z_hi", "y", "z_lo", "x")


def landing(slot):
    z = slot // 64 * 2 + slot // 8 % 2
    y = slot // 16 % 4
    return (z * RING + y) * HELD + slot % 8


def turn(value, shift):
    return lax.rem(value + shift + RING, RING)


def stored(ref, z, y, x, count):
    return ref.at[pl.ds(((z * RING + y) * RING + x) * 2, 2 * count)]


def columns(j, width):
    return pl.ds(pl.multiple_of(j * width, width), width)


def tables(perm, seg):
    lane = lax.broadcasted_iota(jnp.int32, (1, BLOCKS), 1)
    starts = jnp.zeros((1, BLOCKS), jnp.int32)
    for s in range(1, SEGMENTS):
        count = jnp.sum((seg < s).astype(jnp.int32), axis=1, keepdims=True)
        count = jnp.sum(count, axis=0, keepdims=True)
        starts = jnp.where(lane == s, count, starts)
    slot = lax.broadcasted_iota(jnp.int32, (BLOCKS, BLOCKS), 0)
    block = lax.broadcasted_iota(jnp.int32, (BLOCKS, BLOCKS), 1)
    held = jnp.sum(jnp.where(slot == block, perm, 0), axis=1, keepdims=True)
    inverse = jnp.sum(jnp.where(held == block, landing(slot), 0), axis=0, keepdims=True)
    inverse = jnp.minimum(inverse, BLOCKS - 1)
    return jnp.concatenate([perm, starts, inverse, jnp.zeros((5, BLOCKS), jnp.int32)], axis=0)


def episode_kernel(
    q_ref, k_ref, v_ref, perm_ref, seg_ref, out_ref,
    perm, seg, meta_vec, meta, q_all, k_all, v_all, weights, scale, o_all,
    send_sem, recv_sem, first_send, first_recv, o_send, o_recv, local_sem,
):
    core, z_hi, y, z_lo, x = (lax.axis_index(a) for a in AXES)
    z = z_hi * 2 + z_lo
    other = 1 - core
    apart = lax.rem(z_lo + core, 2)
    home = apart == 0
    away = jnp.logical_not(home)
    to_pair = 1 - 2 * z_lo
    pair = apart * to_pair

    def at(to_core, dx=0, dy=0, dz=0):
        far_z = turn(z, dz)
        return (to_core, far_z // 2, turn(y, dy), lax.rem(far_z, 2), turn(x, dx))

    barrier = pltpu.get_barrier_semaphore()

    def tell(device):
        pl.semaphore_signal(barrier, inc=1, device_id=device, device_id_type=MESH)

    left = 2 * core - x
    for dx in (1, 2, 3):
        tell(at(z_lo, dx))
    pl.when(away)(lambda: tell(at(z_lo)))
    for dx in range(RING):
        tell(at(z_lo, dx, 0, to_pair))
        tell(at(1 - z_lo, dx, 0, pair))
    for n in range(2):
        for dz in (2, 2 + to_pair):
            tell(at(z_lo, left + n, 0, dz))
    for dy in (1, 2, 3):
        tell(at(core, 0, dy))
    local = [
        pltpu.make_async_copy(src, dst, local_sem.at[n])
        for n, (src, dst) in enumerate(((perm_ref, perm), (seg_ref, seg)))
    ]
    for copy in local:
        copy.start()
    pl.semaphore_wait(barrier, 18 + apart)

    firsts = []

    def first(src, dst, n, device, own=False):
        copy = pltpu.make_async_remote_copy(
            src_ref=src,
            dst_ref=dst,
            send_sem=first_send.at[len(firsts)],
            recv_sem=first_recv.at[n],
            device_id=device,
            device_id_type=MESH,
        )
        firsts.append((copy, own))
        if own is False:
            copy.start()
        else:
            pl.when(jnp.logical_not(own))(copy.start)
            pl.when(own)(pltpu.make_async_copy(src, dst, first_recv.at[n]).start)

    def landed(ref, n):
        pltpu.make_async_copy(ref, ref, first_recv.at[n]).wait()

    sent = []

    def send(ref, device):
        n = len(sent)
        copy = pltpu.make_async_remote_copy(
            src_ref=ref,
            dst_ref=ref,
            send_sem=send_sem.at[n],
            recv_sem=recv_sem.at[n],
            device_id=device,
            device_id_type=MESH,
        )
        copy.start()
        sent.append(copy)
        return copy

    half = x // 2
    for ref, dst, offset in ((k_ref, k_all, 0), (v_ref, v_all, 16)):
        for k in range(2):
            for dx in (1, 3, 2, 0):
                first(
                    ref.at[:, :, columns(turn(x, dx), HEAD_DIM)],
                    stored(dst, z, y, x, 1),
                    offset + z * RING + x,
                    at(half, dx, 0, apart + 2 * k),
                    home & (half == core) if dx == 0 and k == 0 else False,
                )
    for copy in local:
        copy.wait()
    meta_vec[...] = tables(perm[...], seg[...])
    to_scalars = pltpu.make_async_copy(meta_vec, meta, local_sem.at[2])
    to_scalars.start()

    lines = [turn(z, dz) for dz in (0, 1, 3, 2)]
    shares = ([], [])

    def share(part, ref):
        shares[part].append(send(ref, at(other)))

    def own(part, ref, line):
        offset = 16 * part
        for n in range(2):
            far_x = 2 * core + n
            landed(stored(ref, line, y, far_x, 1), offset + line * RING + far_x)
        return stored(ref, line, y, 2 * core, 2)

    k_along = []
    for line in lines:
        piece = own(0, k_all, line)
        k_along.append([send(piece, at(core, 0, dy)) for dy in (1, 3, 2)])
        share(0, piece)
    for dx in (1, 3, 2, 0):
        for b in range(2):
            first(
                q_ref.at[b, :, columns(turn(x, dx), WIDE)],
                q_all.at[z_lo * RING + x],
                32 + z_lo * RING + x,
                at(b, dx, 0, pair),
                home & (core == b) if dx == 0 else False,
            )
    v_along = []
    for line in lines:
        piece = own(1, v_all, line)
        v_along.append([send(piece, at(core, 0, dy)) for dy in (1, 3)])
        share(1, piece)
    for n, line in enumerate(lines):
        for copy, dy in zip(k_along[n], (-1, 1, 2)):
            copy.wait_recv()
            share(0, stored(k_all, line, turn(y, dy), 2 * core, 2))
    to_scalars.wait()
    for n in range(HELD):
        landed(q_all.at[n], 32 + n)
    for copy in shares[0]:
        copy.wait_recv()

    def later():
        far = []
        for n, line in enumerate(lines):
            pieces = []
            for copy, dy, part in zip(v_along[n], (-1, 1), (0, 1)):
                copy.wait_recv()
                low = stored(v_all, line, turn(y, dy), 2 * core + part, 1)
                pieces.append(send(low, at(core, 0, -dy)))
                share(1, stored(v_all, line, turn(y, dy), 2 * core, 2))
            far.append(pieces)
            yield
        for n, line in enumerate(lines):
            for copy in far[n]:
                copy.wait_recv()
            share(1, stored(v_all, line, turn(y, 2), 2 * core, 2))
            yield
        for copy in shares[1]:
            copy.wait_recv()
        yield

    v_steps = later()
    base = (z_hi * RING + y) * 16 + core

    def rows_of(ref, block, start, count):
        parts = []
        for u in range(count):
            there = jnp.clip(block - (REACH - 1) + start + u, 0, BLOCKS - 1)
            parts.append(ref[meta[2, there]])
        return jnp.concatenate(parts, axis=0)

    def score(i, carry):
        block = meta[0, base + 2 * i]
        row_pos = block * BLOCK + lax.broadcasted_iota(jnp.int32, (BLOCK, HEAD_DIM), 0)
        row_low = jnp.zeros((BLOCK, HEAD_DIM), jnp.int32)
        for s in range(1, SEGMENTS):
            row_low = jnp.where(meta[1, s] <= row_pos, meta[1, s], row_low)
        q = jnp.concatenate(
            [q_all[i, :, j * HEAD_DIM:(j + 1) * HEAD_DIM] for j in range(GROUP)], axis=0
        )
        pieces = []
        top = None
        for start in range(-2, REACH - 2, 4):
            begin, count = max(start, 0), 4 + min(start, 0)
            s = lax.dot_general(
                q, rows_of(k_all, block, begin, count), (((1,), (1,)), ((), ())),
                preferred_element_type=jnp.float32,
            )
            for half in range(count // 2):
                index = begin + 2 * half
                col = (block - (REACH - 1) + index) * BLOCK + lax.broadcasted_iota(
                    jnp.int32, (BLOCK, HEAD_DIM), 1
                )
                seen = col >= row_low
                if index == REACH - 2:
                    seen = seen & (col <= row_pos)
                seen = jnp.concatenate([seen] * GROUP, axis=0)
                piece = jnp.where(seen, s[:, half * HEAD_DIM:(half + 1) * HEAD_DIM], NEG)
                pieces.append(piece)
                top = piece if top is None else jnp.maximum(top, piece)
        top = jnp.max(top, axis=1, keepdims=True)
        total = None
        for n, piece in enumerate(pieces):
            weight = jnp.exp2((piece - top) * SCALE)
            total = weight if total is None else total + weight
            weights[i, :, n * HEAD_DIM:(n + 1) * HEAD_DIM] = weight.astype(jnp.bfloat16)
        total = jnp.sum(total, axis=1, keepdims=True)
        scale[i] = jnp.broadcast_to(1.0 / total, (ROWS, HEAD_DIM))
        return carry

    for n in range(HELD):
        score(n, 0)
        next(v_steps)
    next(v_steps)

    def blend(i):
        block = meta[0, base + 2 * i]
        mixed = jnp.dot(weights[i], rows_of(v_all, block, 0, REACH), preferred_element_type=jnp.float32)
        return (mixed * scale[i]).astype(jnp.bfloat16)

    def place(ref, mixed):
        for j in range(GROUP):
            ref[:, j * HEAD_DIM:(j + 1) * HEAD_DIM] = mixed[j * BLOCK:(j + 1) * BLOCK]

    rows = pl.ds(pl.multiple_of(core * BLOCK, BLOCK), BLOCK)

    def whose(n):
        to_lo = lax.rem(z_lo + 1 - lax.rem(n, 2), 2)
        return RING - 1 - n // 2, to_lo

    def answer(n):
        dx, to_lo = whose(n)
        return pltpu.make_async_remote_copy(
            src_ref=o_all.at[n],
            dst_ref=out_ref.at[rows, columns(x, WIDE)],
            send_sem=o_send.at[n],
            recv_sem=o_recv.at[core * RING + x],
            device_id=at(z_lo, dx, 0, to_lo - z_lo),
            device_id_type=MESH,
        )

    def reply(n):
        dx, to_lo = whose(n)
        mixed = blend(to_lo * RING + turn(x, dx))
        for j in range(GROUP):
            o_all[n, :, j * HEAD_DIM:(j + 1) * HEAD_DIM] = mixed[j * BLOCK:(j + 1) * BLOCK]

    def reply_away(n, carry):
        reply(n)
        answer(n).start()
        return carry

    last = HELD - 1
    lax.fori_loop(0, last, reply_away, 0)
    reply(last)
    pl.when(away)(answer(last).start)
    pl.when(home)(
        pltpu.make_async_copy(
            o_all.at[last], out_ref.at[rows, columns(x, WIDE)], o_recv.at[core * RING + x]
        ).start
    )
    for copy in sent:
        copy.wait_send()
    for copy, mine in firsts:
        if mine is False:
            copy.wait_send()
        else:
            pl.when(jnp.logical_not(mine))(copy.wait_send)
    for b in range(2):
        for j in range(RING):
            ref = out_ref.at[b * BLOCK:(b + 1) * BLOCK, j * WIDE:(j + 1) * WIDE]
            pltpu.make_async_copy(ref, ref, o_recv.at[b * RING + j]).wait()

    def finish(n, carry):
        answer(n).wait_send()
        return carry

    lax.fori_loop(0, last, finish, 0)
    pl.when(away)(answer(last).wait_send)


COPIES = 12 + 16 + 16 + 16
FIRSTS = 24


def shards(queries, keys, values, permutation, segment):
    hbm = pl.BlockSpec(memory_space=pltpu.HBM)
    inputs = (
        *(a.reshape(2, BLOCK, -1) for a in (queries, keys, values)),
        permutation.reshape(1, BLOCKS),
        segment.reshape(SEQ // BLOCKS, BLOCKS),
    )
    return pl.pallas_call(
        episode_kernel,
        out_shape=jax.ShapeDtypeStruct(queries.shape, jnp.bfloat16),
        in_specs=[hbm] * 5,
        out_specs=pl.BlockSpec(memory_space=pltpu.VMEM),
        scratch_shapes=[
            pltpu.VMEM((1, BLOCKS), jnp.int32),
            pltpu.VMEM((SEQ // BLOCKS, BLOCKS), jnp.int32),
            pltpu.VMEM((8, BLOCKS), jnp.int32),
            pltpu.SMEM((8, BLOCKS), jnp.int32),
            pltpu.VMEM((HELD, BLOCK, WIDE), jnp.bfloat16),
            pltpu.VMEM((BLOCKS, BLOCK, HEAD_DIM), jnp.bfloat16),
            pltpu.VMEM((BLOCKS, BLOCK, HEAD_DIM), jnp.bfloat16),
            pltpu.VMEM((HELD, ROWS, WIDTH), jnp.bfloat16),
            pltpu.VMEM((HELD, ROWS, HEAD_DIM), jnp.float32),
            pltpu.VMEM((HELD, BLOCK, WIDE), jnp.bfloat16),
            pltpu.SemaphoreType.DMA((COPIES,)),
            pltpu.SemaphoreType.DMA((COPIES,)),
            pltpu.SemaphoreType.DMA((FIRSTS,)),
            pltpu.SemaphoreType.DMA((32 + HELD,)),
            pltpu.SemaphoreType.DMA((HELD,)),
            pltpu.SemaphoreType.DMA((HELD,)),
            pltpu.SemaphoreType.DMA((3,)),
        ],
        compiler_params=pltpu.CompilerParams(
            collective_id=0, has_side_effects=True, vmem_limit_bytes=40 << 20
        ),
        name="episode",
    )(*(pltpu.with_memory_space_constraint(a, pltpu.HBM) for a in inputs))


def solution(mesh):
    fine = Mesh(mesh.devices.reshape(2, 2, 4, 2, 4), AXES)
    slots = AXES[1:]
    return jax.shard_map(
        shards,
        mesh=fine,
        in_specs=(P(slots, "head"), P(slots, "head"), P(slots, "head"), P(), P()),
        out_specs=P(slots, "head"),
        check_vma=False,
    )
```

```python
import math

import jax
import jax.numpy as jnp
from jax import lax
from jax.experimental import pallas as pl
from jax.experimental.pallas import tpu as pltpu
from jax.sharding import Mesh, PartitionSpec as P

HEAD_DIM = 128
BLOCK = 64
BLOCKS = 128
SEQ = 8192
SEGMENTS = 8
GROUP = 4
RING = 4
LOCAL = 128
ROWS = GROUP * BLOCK
WIDE = GROUP * HEAD_DIM
HELD = 2 * RING
REACH = 34
WIDTH = REACH * BLOCK
SCALE = math.log2(math.e) / math.sqrt(HEAD_DIM)
NEG = -1e30
MESH = pl.DeviceIdType.MESH
AXES = ("head", "z_hi", "y", "z_lo", "x")


def landing(slot):
    z = slot // 64 * 2 + slot // 8 % 2
    y = slot // 16 % 4
    return (z * RING + y) * HELD + slot % 8


def turn(value, shift):
    return lax.rem(value + shift + RING, RING)


def stored(ref, z, y, x, count):
    return ref.at[pl.ds(((z * RING + y) * RING + x) * 2, 2 * count)]


def columns(j, width):
    return pl.ds(pl.multiple_of(j * width, width), width)


def tables(perm, seg):
    lane = lax.broadcasted_iota(jnp.int32, (1, BLOCKS), 1)
    starts = jnp.zeros((1, BLOCKS), jnp.int32)
    for s in range(1, SEGMENTS):
        count = jnp.sum((seg < s).astype(jnp.int32), axis=1, keepdims=True)
        count = jnp.sum(count, axis=0, keepdims=True)
        starts = jnp.where(lane == s, count, starts)
    slot = lax.broadcasted_iota(jnp.int32, (BLOCKS, BLOCKS), 0)
    block = lax.broadcasted_iota(jnp.int32, (BLOCKS, BLOCKS), 1)
    held = jnp.sum(jnp.where(slot == block, perm, 0), axis=1, keepdims=True)
    inverse = jnp.sum(jnp.where(held == block, landing(slot), 0), axis=0, keepdims=True)
    inverse = jnp.minimum(inverse, BLOCKS - 1)
    return jnp.concatenate([perm, starts, inverse, jnp.zeros((5, BLOCKS), jnp.int32)], axis=0)


def episode_kernel(
    q_ref, k_ref, v_ref, perm_ref, seg_ref, out_ref,
    perm, seg, meta_vec, meta, q_all, k_all, v_all, weights, scale, o_all,
    send_sem, recv_sem, first_send, first_recv, o_send, o_recv, local_sem,
):
    core, z_hi, y, z_lo, x = (lax.axis_index(a) for a in AXES)
    z = z_hi * 2 + z_lo
    other = 1 - core
    apart = lax.rem(z_lo + core, 2)
    home = apart == 0
    away = jnp.logical_not(home)
    to_pair = 1 - 2 * z_lo
    pair = apart * to_pair

    def at(to_core, dx=0, dy=0, dz=0):
        far_z = turn(z, dz)
        return (to_core, far_z // 2, turn(y, dy), lax.rem(far_z, 2), turn(x, dx))

    barrier = pltpu.get_barrier_semaphore()

    def tell(device):
        pl.semaphore_signal(barrier, inc=1, device_id=device, device_id_type=MESH)

    left = 2 * core - x
    for dx in (1, 2, 3):
        tell(at(z_lo, dx))
    pl.when(away)(lambda: tell(at(z_lo)))
    for dx in range(RING):
        tell(at(z_lo, dx, 0, to_pair))
        tell(at(1 - z_lo, dx, 0, pair))
    for n in range(2):
        for dz in (2, 2 + to_pair):
            tell(at(z_lo, left + n, 0, dz))
    for dy in (1, 2, 3):
        tell(at(core, 0, dy))
    local = [
        pltpu.make_async_copy(src, dst, local_sem.at[n])
        for n, (src, dst) in enumerate(((perm_ref, perm), (seg_ref, seg)))
    ]
    for copy in local:
        copy.start()
    pl.semaphore_wait(barrier, 18 + apart)

    firsts = []

    def first(src, dst, n, device, own=False):
        copy = pltpu.make_async_remote_copy(
            src_ref=src,
            dst_ref=dst,
            send_sem=first_send.at[len(firsts)],
            recv_sem=first_recv.at[n],
            device_id=device,
            device_id_type=MESH,
        )
        firsts.append((copy, own))
        if own is False:
            copy.start()
        else:
            pl.when(jnp.logical_not(own))(copy.start)
            pl.when(own)(pltpu.make_async_copy(src, dst, first_recv.at[n]).start)

    def landed(ref, n):
        pltpu.make_async_copy(ref, ref, first_recv.at[n]).wait()

    sent = []

    def send(ref, device):
        n = len(sent)
        copy = pltpu.make_async_remote_copy(
            src_ref=ref,
            dst_ref=ref,
            send_sem=send_sem.at[n],
            recv_sem=recv_sem.at[n],
            device_id=device,
            device_id_type=MESH,
        )
        copy.start()
        sent.append(copy)
        return copy

    half = x // 2
    for ref, dst, offset in ((k_ref, k_all, 0), (v_ref, v_all, 16)):
        for k in range(2):
            for dx in (1, 3, 2, 0):
                first(
                    ref.at[:, :, columns(turn(x, dx), HEAD_DIM)],
                    stored(dst, z, y, x, 1),
                    offset + z * RING + x,
                    at(half, dx, 0, apart + 2 * k),
                    home & (half == core) if dx == 0 and k == 0 else False,
                )
    for copy in local:
        copy.wait()
    meta_vec[...] = tables(perm[...], seg[...])
    to_scalars = pltpu.make_async_copy(meta_vec, meta, local_sem.at[2])
    to_scalars.start()

    lines = [turn(z, dz) for dz in (0, 1, 3, 2)]
    shares = ([], [])

    def share(part, ref):
        shares[part].append(send(ref, at(other)))

    def own(part, ref, line):
        offset = 16 * part
        for n in range(2):
            far_x = 2 * core + n
            landed(stored(ref, line, y, far_x, 1), offset + line * RING + far_x)
        return stored(ref, line, y, 2 * core, 2)

    k_along = []
    for line in lines:
        piece = own(0, k_all, line)
        k_along.append([send(piece, at(core, 0, dy)) for dy in (1, 3, 2)])
        share(0, piece)
    for dx in (1, 3, 2, 0):
        for b in range(2):
            first(
                q_ref.at[b, :, columns(turn(x, dx), WIDE)],
                q_all.at[z_lo * RING + x],
                32 + z_lo * RING + x,
                at(b, dx, 0, pair),
                home & (core == b) if dx == 0 else False,
            )
    v_along = []
    for n, line in enumerate(lines):
        for copy, dy in zip(k_along[n], (-1, 1, 2)):
            copy.wait_recv()
            share(0, stored(k_all, line, turn(y, dy), 2 * core, 2))
        piece = own(1, v_all, line)
        v_along.append([send(piece, at(core, 0, dy)) for dy in (1, 3)])
        share(1, piece)
    to_scalars.wait()
    for n in range(HELD):
        landed(q_all.at[n], 32 + n)
    for copy in shares[0]:
        copy.wait_recv()

    def later():
        far = []
        for n, line in enumerate(lines):
            pieces = []
            for copy, dy, part in zip(v_along[n], (-1, 1), (0, 1)):
                copy.wait_recv()
                low = stored(v_all, line, turn(y, dy), 2 * core + part, 1)
                pieces.append(send(low, at(core, 0, -dy)))
                share(1, stored(v_all, line, turn(y, dy), 2 * core, 2))
            far.append(pieces)
            yield
        for n, line in enumerate(lines):
            for copy in far[n]:
                copy.wait_recv()
            share(1, stored(v_all, line, turn(y, 2), 2 * core, 2))
            yield
        for copy in sent:
            copy.wait_send()
        for copy, mine in firsts:
            if mine is False:
                copy.wait_send()
            else:
                pl.when(jnp.logical_not(mine))(copy.wait_send)
        for copy in shares[1]:
            copy.wait_recv()
        yield

    v_steps = later()
    base = (z_hi * RING + y) * 16 + core

    def rows_of(ref, block, start, count):
        parts = []
        for u in range(count):
            there = jnp.clip(block - (REACH - 1) + start + u, 0, BLOCKS - 1)
            parts.append(ref[meta[2, there]])
        return jnp.concatenate(parts, axis=0)

    def score(i):
        block = meta[0, base + 2 * i]
        row_pos = block * BLOCK + lax.broadcasted_iota(jnp.int32, (BLOCK, HEAD_DIM), 0)
        row_low = jnp.zeros((BLOCK, HEAD_DIM), jnp.int32)
        for s in range(1, SEGMENTS):
            row_low = jnp.where(meta[1, s] <= row_pos, meta[1, s], row_low)
        q = jnp.concatenate(
            [q_all[i, :, j * HEAD_DIM:(j + 1) * HEAD_DIM] for j in range(GROUP)], axis=0
        )
        pieces = []
        top = None
        for start in range(-2, REACH - 2, 4):
            begin, count = max(start, 0), 4 + min(start, 0)
            s = lax.dot_general(
                q, rows_of(k_all, block, begin, count), (((1,), (1,)), ((), ())),
                preferred_element_type=jnp.float32,
            )
            for half in range(count // 2):
                index = begin + 2 * half
                col = (block - (REACH - 1) + index) * BLOCK + lax.broadcasted_iota(
                    jnp.int32, (BLOCK, HEAD_DIM), 1
                )
                seen = col >= row_low
                if index == REACH - 2:
                    seen = seen & (col <= row_pos)
                seen = jnp.concatenate([seen] * GROUP, axis=0)
                piece = jnp.where(seen, s[:, half * HEAD_DIM:(half + 1) * HEAD_DIM], NEG)
                pieces.append(piece)
                top = piece if top is None else jnp.maximum(top, piece)
        top = jnp.max(top, axis=1, keepdims=True)
        total = None
        for n, piece in enumerate(pieces):
            weight = jnp.exp2((piece - top) * SCALE)
            total = weight if total is None else total + weight
            weights[i, :, n * HEAD_DIM:(n + 1) * HEAD_DIM] = weight.astype(jnp.bfloat16)
        total = jnp.sum(total, axis=1, keepdims=True)
        scale[i] = jnp.broadcast_to(1.0 / total, (ROWS, HEAD_DIM))

    for n in range(0, HELD, 2):
        score(n)
        score(n + 1)
        next(v_steps)
        next(v_steps)
    next(v_steps)

    def blend(i):
        block = meta[0, base + 2 * i]
        mixed = jnp.dot(weights[i], rows_of(v_all, block, 0, REACH), preferred_element_type=jnp.float32)
        return (mixed * scale[i]).astype(jnp.bfloat16)

    def place(ref, mixed):
        for j in range(GROUP):
            ref[:, j * HEAD_DIM:(j + 1) * HEAD_DIM] = mixed[j * BLOCK:(j + 1) * BLOCK]

    order = ((2, 0), (1, 1), (3, 0), (2, 1), (1, 0), (3, 1), (0, 0), (0, 1))
    rows = pl.ds(pl.multiple_of(core * BLOCK, BLOCK), BLOCK)

    def whose(n):
        dx, same = order[n]
        return dx, z_lo if same else 1 - z_lo

    def answer(n):
        dx, to_lo = whose(n)
        return pltpu.make_async_remote_copy(
            src_ref=o_all.at[n],
            dst_ref=out_ref.at[rows, columns(x, WIDE)],
            send_sem=o_send.at[n],
            recv_sem=o_recv.at[core * RING + x],
            device_id=at(z_lo, dx, 0, to_lo - z_lo),
            device_id_type=MESH,
        )

    def reply(n):
        dx, to_lo = whose(n)
        mixed = blend(to_lo * RING + turn(x, dx))
        for j in range(GROUP):
            o_all[n, :, j * HEAD_DIM:(j + 1) * HEAD_DIM] = mixed[j * BLOCK:(j + 1) * BLOCK]

    last = HELD - 1
    for n in range(HELD):
        reply(n)
        if n < last:
            answer(n).start()
    pl.when(away)(answer(last).start)
    pl.when(home)(
        pltpu.make_async_copy(
            o_all.at[last], out_ref.at[rows, columns(x, WIDE)], o_recv.at[core * RING + x]
        ).start
    )
    for b in range(2):
        for j in range(RING):
            ref = out_ref.at[b * BLOCK:(b + 1) * BLOCK, j * WIDE:(j + 1) * WIDE]
            pltpu.make_async_copy(ref, ref, o_recv.at[b * RING + j]).wait()

    for n in range(last):
        answer(n).wait_send()
    pl.when(away)(answer(last).wait_send)


COPIES = 12 + 16 + 16 + 16
FIRSTS = 24


def shards(queries, keys, values, permutation, segment):
    hbm = pl.BlockSpec(memory_space=pltpu.HBM)
    inputs = (
        *(a.reshape(2, BLOCK, -1) for a in (queries, keys, values)),
        permutation.reshape(1, BLOCKS),
        segment.reshape(SEQ // BLOCKS, BLOCKS),
    )
    return pl.pallas_call(
        episode_kernel,
        out_shape=jax.ShapeDtypeStruct(queries.shape, jnp.bfloat16),
        in_specs=[hbm] * 5,
        out_specs=pl.BlockSpec(memory_space=pltpu.VMEM),
        scratch_shapes=[
            pltpu.VMEM((1, BLOCKS), jnp.int32),
            pltpu.VMEM((SEQ // BLOCKS, BLOCKS), jnp.int32),
            pltpu.VMEM((8, BLOCKS), jnp.int32),
            pltpu.SMEM((8, BLOCKS), jnp.int32),
            pltpu.VMEM((HELD, BLOCK, WIDE), jnp.bfloat16),
            pltpu.VMEM((BLOCKS, BLOCK, HEAD_DIM), jnp.bfloat16),
            pltpu.VMEM((BLOCKS, BLOCK, HEAD_DIM), jnp.bfloat16),
            pltpu.VMEM((HELD, ROWS, WIDTH), jnp.bfloat16),
            pltpu.VMEM((HELD, ROWS, HEAD_DIM), jnp.float32),
            pltpu.VMEM((HELD, BLOCK, WIDE), jnp.bfloat16),
            pltpu.SemaphoreType.DMA((COPIES,)),
            pltpu.SemaphoreType.DMA((COPIES,)),
            pltpu.SemaphoreType.DMA((FIRSTS,)),
            pltpu.SemaphoreType.DMA((32 + HELD,)),
            pltpu.SemaphoreType.DMA((HELD,)),
            pltpu.SemaphoreType.DMA((HELD,)),
            pltpu.SemaphoreType.DMA((3,)),
        ],
        compiler_params=pltpu.CompilerParams(
            collective_id=0, has_side_effects=True, vmem_limit_bytes=40 << 20
        ),
        name="episode",
    )(*(pltpu.with_memory_space_constraint(a, pltpu.HBM) for a in inputs))


def solution(mesh):
    fine = Mesh(mesh.devices.reshape(2, 2, 4, 2, 4), AXES)
    slots = AXES[1:]
    return jax.shard_map(
        shards,
        mesh=fine,
        in_specs=(P(slots, "head"), P(slots, "head"), P(slots, "head"), P(), P()),
        out_specs=P(slots, "head"),
        check_vma=False,
    )
```

```python
import math

import jax
import jax.numpy as jnp
from jax import lax
from jax.experimental import pallas as pl
from jax.experimental.pallas import tpu as pltpu
from jax.sharding import Mesh, PartitionSpec as P

HEAD_DIM = 128
BLOCK = 64
BLOCKS = 128
SEQ = 8192
SEGMENTS = 8
GROUP = 4
RING = 4
LOCAL = 128
ROWS = GROUP * BLOCK
WIDE = GROUP * HEAD_DIM
HELD = 2 * RING
REACH = 34
WIDTH = REACH * BLOCK
SCALE = math.log2(math.e) / math.sqrt(HEAD_DIM)
NEG = -1e30
MESH = pl.DeviceIdType.MESH
AXES = ("head", "z_hi", "y", "z_lo", "x")


def landing(slot):
    z = slot // 64 * 2 + slot // 8 % 2
    y = slot // 16 % 4
    return (z * RING + y) * HELD + slot % 8


def turn(value, shift):
    return lax.rem(value + shift + RING, RING)


def stored(ref, z, y, x, count):
    return ref.at[pl.ds(((z * RING + y) * RING + x) * 2, 2 * count)]


def columns(j, width):
    return pl.ds(pl.multiple_of(j * width, width), width)


def tables(perm, seg):
    lane = lax.broadcasted_iota(jnp.int32, (1, BLOCKS), 1)
    starts = jnp.zeros((1, BLOCKS), jnp.int32)
    for s in range(1, SEGMENTS):
        count = jnp.sum((seg < s).astype(jnp.int32), axis=1, keepdims=True)
        count = jnp.sum(count, axis=0, keepdims=True)
        starts = jnp.where(lane == s, count, starts)
    slot = lax.broadcasted_iota(jnp.int32, (BLOCKS, BLOCKS), 0)
    block = lax.broadcasted_iota(jnp.int32, (BLOCKS, BLOCKS), 1)
    held = jnp.sum(jnp.where(slot == block, perm, 0), axis=1, keepdims=True)
    inverse = jnp.sum(jnp.where(held == block, landing(slot), 0), axis=0, keepdims=True)
    inverse = jnp.minimum(inverse, BLOCKS - 1)
    return jnp.concatenate([perm, starts, inverse, jnp.zeros((5, BLOCKS), jnp.int32)], axis=0)


def episode_kernel(
    q_ref, k_ref, v_ref, perm_ref, seg_ref, out_ref,
    perm, seg, meta_vec, meta, q_all, k_all, v_all, k_part, v_part, weights, scale, o_all,
    send_sem, recv_sem, first_send, first_recv, v_send, v_recv, o_send, o_recv, local_sem,
):
    core, z_hi, y, z_lo, x = (lax.axis_index(a) for a in AXES)
    z = z_hi * 2 + z_lo
    other = 1 - core
    apart = lax.rem(z_lo + core, 2)
    home = apart == 0
    away = jnp.logical_not(home)
    half = x // 2
    x_odd, y_odd = lax.rem(x, 2), lax.rem(y, 2)

    def at(to_core, dx=0, dy=0, dz=0):
        far_z = turn(z, dz)
        return (to_core, far_z // 2, turn(y, dy), lax.rem(far_z, 2), turn(x, dx))

    def cube(b, ex, ey, ez):
        way = 1 - 2 * b
        return ex * way * (1 - 2 * x_odd), ey * way * (1 - 2 * y_odd), ez * way * (1 - 2 * z_lo)

    barrier = pltpu.get_barrier_semaphore()

    def tell(device):
        pl.semaphore_signal(barrier, inc=1, device_id=device, device_id_type=MESH)

    own_key = home & (half == core)
    for dy in range(RING):
        for dx in range(RING):
            if dx or dy:
                tell(at(core, dx, dy))
    for n in range(2):
        for dz in range(RING):
            device = at(z_lo, 2 * core + n - x, 0, dz)
            if dz:
                tell(device)
            else:
                pl.when(jnp.logical_not(home & (x == 2 * core + n)))(lambda device=device: tell(device))
    for dz in (1, 2, 3):
        tell(at(z_lo, 0, 0, dz))
    across = [(ex, ey) for ey in range(2) for ex in range(2)]
    for ex, ey in across:
        tell(at(z_lo, *cube(core, ex, ey, 1)))
        tell(at(other, *cube(other, ex, ey, apart)))

    def tell_more():
        for ex, ey in across:
            tell(at(z_lo, *cube(core, ex, ey, 0)))
            tell(at(core, *cube(core, ex, ey, 1)))

    pl.when(away)(tell_more)
    local = [
        pltpu.make_async_copy(src, dst, local_sem.at[n])
        for n, (src, dst) in enumerate(((perm_ref, perm), (seg_ref, seg)))
    ]
    for copy in local:
        copy.start()
    pl.semaphore_wait(barrier, 33 + 10 * apart - own_key.astype(jnp.int32))

    firsts = []

    def first(src, dst, n, device, own=False):
        copy = pltpu.make_async_remote_copy(
            src_ref=src,
            dst_ref=dst,
            send_sem=first_send.at[len(firsts)],
            recv_sem=first_recv.at[n],
            device_id=device,
            device_id_type=MESH,
        )
        firsts.append((copy, own))
        if own is False:
            copy.start()
        else:
            pl.when(jnp.logical_not(own))(copy.start)
            pl.when(own)(pltpu.make_async_copy(src, dst, first_recv.at[n]).start)

    def landed(ref, sem):
        pltpu.make_async_copy(ref, ref, sem).wait()

    sent = []

    def send(src, dst, device):
        n = len(sent)
        copy = pltpu.make_async_remote_copy(
            src_ref=src,
            dst_ref=dst,
            send_sem=send_sem.at[n],
            recv_sem=recv_sem.at[n],
            device_id=device,
            device_id_type=MESH,
        )
        copy.start()
        sent.append(copy)
        return copy

    def key_part(of_z, odd_x, count=1):
        return k_part.at[pl.ds((of_z * 2 + odd_x) * 2, 2 * count)]

    def value_part(of_y, of_x, count=1):
        return v_part.at[pl.ds((of_y * RING + of_x) * 2, 2 * count)]

    for k in range(2):
        for dx in (1, 3, 2, 0):
            first(
                k_ref.at[:, :, columns(lax.rem(x + dx, 2), 2 * HEAD_DIM)],
                key_part(z, x_odd),
                z * 2 + x_odd,
                at(half, dx, 0, apart + 2 * k),
                own_key if dx == 0 and k == 0 else False,
            )
    for dy in (0, 1, 3, 2):
        for dx in (1, 3, 2, 0):
            src = v_ref.at[:, :, columns(2 * lax.rem(x + dx, 2) + lax.rem(y + dy, 2), HEAD_DIM)]
            n = 8 + y * RING + x
            if dx or dy:
                first(src, value_part(y, x), n, at(core, dx, dy))
            else:
                pltpu.make_async_copy(src, value_part(y, x), first_recv.at[n]).start()
    for copy in local:
        copy.wait()
    meta_vec[...] = tables(perm[...], seg[...])
    to_scalars = pltpu.make_async_copy(meta_vec, meta, local_sem.at[2])
    to_scalars.start()

    lines = [turn(z, dz) for dz in (0, 1, 3, 2)]
    shares = ([], [])

    def share(part, src, dst):
        shares[part].append(send(src, dst, at(other)))

    k_along, k_own = [], []
    for n, line in enumerate(lines):
        for odd in range(2):
            landed(key_part(line, odd), first_recv.at[line * 2 + odd])
        dst = stored(k_all, line, y, 2 * core, 2)

        def piece(dy, line=line):
            return key_part(line, 0, 2).at[:, :, columns(lax.rem(y + dy, 2), HEAD_DIM)]

        k_along.append([send(piece(dy), dst, at(core, 0, dy)) for dy in (1, 3, 2)])
        share(0, piece(0), dst)
        k_own.append(pltpu.make_async_copy(piece(0), dst, local_sem.at[3 + n]))
        k_own[-1].start()
    for b in range(2):
        for ex, ey in ((1, 1), (1, 0), (0, 1), (0, 0)):
            n = apart * 4 + ey * 2 + ex
            first(
                q_ref.at[b, :, columns(2 * lax.rem(x + ex, 2) + lax.rem(y + ey, 2), WIDE)],
                q_all.at[n],
                24 + n,
                at(b, *cube(b, ex, ey, apart)),
                home & (core == b) if not (ex or ey) else False,
            )

    def value_copy(n, src, dst, of_y, device):
        return pltpu.make_async_remote_copy(
            src_ref=src,
            dst_ref=dst,
            send_sem=v_send.at[n],
            recv_sem=v_recv.at[z * RING + of_y],
            device_id=device,
            device_id_type=MESH,
        )

    def halves(n, of_y, dz):
        return [
            value_copy(
                n + c, value_part(of_y, 2 * c, 2), stored(v_all, z, of_y, 2 * c, 2), of_y, at(c, 0, 0, dz)
            )
            for c in range(2)
        ]

    def from_home(m, of_y):
        whole = value_copy(
            4 * m + 2, value_part(of_y, 0, RING), stored(v_all, z, of_y, 0, RING), of_y, at(other)
        )
        return halves(4 * m, of_y, 2) + [whole]

    def from_away(m, of_y):
        return halves(4 * m, of_y, 1) + halves(4 * m + 2, of_y, -1)

    rows_y = [turn(y, dy) for dy in (0, 1, 3, 2)]
    for m, of_y in enumerate(rows_y):
        for of_x in range(RING):
            landed(value_part(of_y, of_x), first_recv.at[8 + of_y * RING + of_x])

        def go_home(m=m, of_y=of_y):
            for copy in from_home(m, of_y):
                copy.start()
            pltpu.make_async_copy(
                value_part(of_y, 0, RING), stored(v_all, z, of_y, 0, RING), v_recv.at[z * RING + of_y]
            ).start()

        def go_away(m=m, of_y=of_y):
            for copy in from_away(m, of_y):
                copy.start()

        pl.when(home)(go_home)
        pl.when(away)(go_away)
    for n, line in enumerate(lines):
        for copy, dy in zip(k_along[n], (-1, 1, 2)):
            copy.wait_recv()
            dst = stored(k_all, line, turn(y, dy), 2 * core, 2)
            share(0, dst, dst)
    to_scalars.wait()
    for n in range(HELD):
        landed(q_all.at[n], first_recv.at[24 + n])
    for copy in k_own:
        copy.wait()
    for copy in shares[0]:
        copy.wait_recv()

    def later():
        for dz in (1, 3, 2):
            line = turn(z, dz)
            for of_y in rows_y:
                piece = stored(v_all, line, of_y, 2 * core, 2)
                landed(piece, v_recv.at[line * RING + of_y])
                share(1, piece, piece)
                yield
        for of_y in rows_y:
            landed(stored(v_all, z, of_y, 0, RING), v_recv.at[z * RING + of_y])
        for copy in sent:
            copy.wait_send()
        for copy, mine in firsts:
            if mine is False:
                copy.wait_send()
            else:
                pl.when(jnp.logical_not(mine))(copy.wait_send)

        def done(copies):
            for m, of_y in enumerate(rows_y):
                for copy in copies(m, of_y):
                    copy.wait_send()

        pl.when(home)(lambda: done(from_home))
        pl.when(away)(lambda: done(from_away))
        for copy in shares[1]:
            copy.wait_recv()
        yield

    v_steps = later()

    def slot(n):
        dx, dy, dz = cube(core, n % 2, n // 2 % 2, n // 4)
        far_z = turn(z, dz)
        return (((far_z // 2 * RING + turn(y, dy)) * 2 + lax.rem(far_z, 2)) * RING + turn(x, dx)) * 2 + core

    def rows_of(ref, block, start, count):
        parts = []
        for u in range(count):
            there = jnp.clip(block - (REACH - 1) + start + u, 0, BLOCKS - 1)
            parts.append(ref[meta[2, there]])
        return jnp.concatenate(parts, axis=0)

    def score(i):
        block = meta[0, slot(i)]
        row_pos = block * BLOCK + lax.broadcasted_iota(jnp.int32, (BLOCK, HEAD_DIM), 0)
        row_low = jnp.zeros((BLOCK, HEAD_DIM), jnp.int32)
        for s in range(1, SEGMENTS):
            row_low = jnp.where(meta[1, s] <= row_pos, meta[1, s], row_low)
        q = jnp.concatenate(
            [q_all[i, :, j * HEAD_DIM:(j + 1) * HEAD_DIM] for j in range(GROUP)], axis=0
        )
        pieces = []
        top = None
        for start in range(-2, REACH - 2, 4):
            begin, count = max(start, 0), 4 + min(start, 0)
            s = lax.dot_general(
                q, rows_of(k_all, block, begin, count), (((1,), (1,)), ((), ())),
                preferred_element_type=jnp.float32,
            )
            for half in range(count // 2):
                index = begin + 2 * half
                col = (block - (REACH - 1) + index) * BLOCK + lax.broadcasted_iota(
                    jnp.int32, (BLOCK, HEAD_DIM), 1
                )
                seen = col >= row_low
                if index == REACH - 2:
                    seen = seen & (col <= row_pos)
                seen = jnp.concatenate([seen] * GROUP, axis=0)
                piece = jnp.where(seen, s[:, half * HEAD_DIM:(half + 1) * HEAD_DIM], NEG)
                pieces.append(piece)
                top = piece if top is None else jnp.maximum(top, piece)
        top = jnp.max(top, axis=1, keepdims=True)
        total = None
        for n, piece in enumerate(pieces):
            weight = jnp.exp2((piece - top) * SCALE)
            total = weight if total is None else total + weight
            weights[i, :, n * HEAD_DIM:(n + 1) * HEAD_DIM] = weight.astype(jnp.bfloat16)
        total = jnp.sum(total, axis=1, keepdims=True)
        scale[i] = jnp.broadcast_to(1.0 / total, (ROWS, HEAD_DIM))

    for n in range(0, HELD, 2):
        score(n)
        score(n + 1)
        for _ in range(3):
            next(v_steps)
    next(v_steps)

    def blend(i):
        block = meta[0, slot(i)]
        mixed = jnp.dot(weights[i], rows_of(v_all, block, 0, REACH), preferred_element_type=jnp.float32)
        return (mixed * scale[i]).astype(jnp.bfloat16)

    def place(ref, mixed):
        for j in range(GROUP):
            ref[:, j * HEAD_DIM:(j + 1) * HEAD_DIM] = mixed[j * BLOCK:(j + 1) * BLOCK]

    rows = pl.ds(pl.multiple_of(core * BLOCK, BLOCK), BLOCK)
    mine = columns(2 * x_odd + y_odd, WIDE)

    def answer(n):
        return pltpu.make_async_remote_copy(
            src_ref=o_all.at[n],
            dst_ref=out_ref.at[rows, mine],
            send_sem=o_send.at[n],
            recv_sem=o_recv.at[core * 4 + n % 4],
            device_id=at(z_lo, *cube(core, n % 2, n // 2 % 2, n // 4)),
            device_id_type=MESH,
        )

    for n in (7, 6, 5, 3, 4, 2, 1, 0):
        mixed = blend(n)
        for j in range(GROUP):
            o_all[n, :, j * HEAD_DIM:(j + 1) * HEAD_DIM] = mixed[j * BLOCK:(j + 1) * BLOCK]
        if n:
            answer(n).start()
    pl.when(away)(answer(0).start)
    pl.when(home)(
        pltpu.make_async_copy(o_all.at[0], out_ref.at[rows, mine], o_recv.at[core * 4]).start
    )
    for b in range(2):
        for n, (ex, ey) in enumerate(across):
            j = 2 * lax.rem(x + ex, 2) + lax.rem(y + ey, 2)
            landed(out_ref.at[b * BLOCK:(b + 1) * BLOCK, columns(j, WIDE)], o_recv.at[b * 4 + n])
    for n in range(1, HELD):
        answer(n).wait_send()
    pl.when(away)(answer(0).wait_send)


COPIES = 12 + 16 + 12
FIRSTS = 8 + 15 + 8


def shards(queries, keys, values, permutation, segment):
    hbm = pl.BlockSpec(memory_space=pltpu.HBM)
    inputs = (
        *(a.reshape(2, BLOCK, -1) for a in (queries, keys, values)),
        permutation.reshape(1, BLOCKS),
        segment.reshape(SEQ // BLOCKS, BLOCKS),
    )
    return pl.pallas_call(
        episode_kernel,
        out_shape=jax.ShapeDtypeStruct(queries.shape, jnp.bfloat16),
        in_specs=[hbm] * 5,
        out_specs=pl.BlockSpec(memory_space=pltpu.VMEM),
        scratch_shapes=[
            pltpu.VMEM((1, BLOCKS), jnp.int32),
            pltpu.VMEM((SEQ // BLOCKS, BLOCKS), jnp.int32),
            pltpu.VMEM((8, BLOCKS), jnp.int32),
            pltpu.SMEM((8, BLOCKS), jnp.int32),
            pltpu.VMEM((HELD, BLOCK, WIDE), jnp.bfloat16),
            pltpu.VMEM((BLOCKS, BLOCK, HEAD_DIM), jnp.bfloat16),
            pltpu.VMEM((BLOCKS, BLOCK, HEAD_DIM), jnp.bfloat16),
            pltpu.VMEM((2 * HELD, BLOCK, 2 * HEAD_DIM), jnp.bfloat16),
            pltpu.VMEM((4 * HELD, BLOCK, HEAD_DIM), jnp.bfloat16),
            pltpu.VMEM((HELD, ROWS, WIDTH), jnp.bfloat16),
            pltpu.VMEM((HELD, ROWS, HEAD_DIM), jnp.float32),
            pltpu.VMEM((HELD, BLOCK, WIDE), jnp.bfloat16),
            pltpu.SemaphoreType.DMA((COPIES,)),
            pltpu.SemaphoreType.DMA((COPIES,)),
            pltpu.SemaphoreType.DMA((FIRSTS,)),
            pltpu.SemaphoreType.DMA((8 + 16 + HELD,)),
            pltpu.SemaphoreType.DMA((16,)),
            pltpu.SemaphoreType.DMA((16,)),
            pltpu.SemaphoreType.DMA((HELD,)),
            pltpu.SemaphoreType.DMA((HELD,)),
            pltpu.SemaphoreType.DMA((7,)),
        ],
        compiler_params=pltpu.CompilerParams(
            collective_id=0, has_side_effects=True, vmem_limit_bytes=40 << 20
        ),
        name="episode",
    )(*(pltpu.with_memory_space_constraint(a, pltpu.HBM) for a in inputs))


def solution(mesh):
    fine = Mesh(mesh.devices.reshape(2, 2, 4, 2, 4), AXES)
    slots = AXES[1:]
    return jax.shard_map(
        shards,
        mesh=fine,
        in_specs=(P(slots, "head"), P(slots, "head"), P(slots, "head"), P(), P()),
        out_specs=P(slots, "head"),
        check_vma=False,
    )
```

```python
import math

import jax
import jax.numpy as jnp
from jax import lax
from jax.experimental import pallas as pl
from jax.experimental.pallas import tpu as pltpu
from jax.sharding import Mesh, PartitionSpec as P

HEAD_DIM = 128
BLOCK = 64
BLOCKS = 128
SEQ = 8192
SEGMENTS = 8
GROUP = 4
RING = 4
LOCAL = 128
ROWS = GROUP * BLOCK
WIDE = GROUP * HEAD_DIM
HELD = 2 * RING
REACH = 34
WIDTH = REACH * BLOCK
SCALE = math.log2(math.e) / math.sqrt(HEAD_DIM)
NEG = -1e30
MESH = pl.DeviceIdType.MESH
AXES = ("head", "z_hi", "y", "z_lo", "x")


def landing(slot):
    z = slot // 64 * 2 + slot // 8 % 2
    y = slot // 16 % 4
    return ((slot % 2 * RING + z) * RING + y) * RING + slot // 2 % 4


def turn(value, shift):
    return lax.rem(value + shift + RING, RING)


def columns(j, width):
    return pl.ds(pl.multiple_of(j * width, width), width)


def tables(perm, seg):
    lane = lax.broadcasted_iota(jnp.int32, (1, BLOCKS), 1)
    starts = jnp.zeros((1, BLOCKS), jnp.int32)
    for s in range(1, SEGMENTS):
        count = jnp.sum((seg < s).astype(jnp.int32), axis=1, keepdims=True)
        count = jnp.sum(count, axis=0, keepdims=True)
        starts = jnp.where(lane == s, count, starts)
    slot = lax.broadcasted_iota(jnp.int32, (BLOCKS, BLOCKS), 0)
    block = lax.broadcasted_iota(jnp.int32, (BLOCKS, BLOCKS), 1)
    held = jnp.sum(jnp.where(slot == block, perm, 0), axis=1, keepdims=True)
    inverse = jnp.sum(jnp.where(held == block, landing(slot), 0), axis=0, keepdims=True)
    inverse = jnp.minimum(inverse, BLOCKS - 1)
    return jnp.concatenate([perm, starts, inverse, jnp.zeros((5, BLOCKS), jnp.int32)], axis=0)


def episode_kernel(
    q_ref, k_ref, v_ref, perm_ref, seg_ref, out_ref,
    perm, seg, meta_vec, meta, q_all, k_all, v_all, k_raw, v_raw, weights, scale, o_all,
    send_sem, recv_sem, first_send, first_recv, o_send, o_recv, local_sem,
):
    core, z_hi, y, z_lo, x = (lax.axis_index(a) for a in AXES)
    z = z_hi * 2 + z_lo
    other = 1 - core
    apart = lax.rem(z_lo + core, 2)
    home = apart == 0
    away = jnp.logical_not(home)
    half = x // 2
    x_odd = lax.rem(x, 2)

    def mate(b):
        return (1 - 2 * z_lo) * (1 - 2 * b)

    def at(to_core, dx=0, dy=0, dz=0):
        far_z = turn(z, dz)
        return (to_core, far_z // 2, turn(y, dy), lax.rem(far_z, 2), turn(x, dx))

    barrier = pltpu.get_barrier_semaphore()

    def tell(device):
        pl.semaphore_signal(barrier, inc=1, device_id=device, device_id_type=MESH)

    def tell_home():
        for dx in range(RING):
            if dx:
                tell(at(core, dx))
            tell(at(other, dx))
        for n in range(2):
            tell(at(core, 2 * core + n - x, 0, -mate(core)))

    def tell_away():
        for dx in range(RING):
            tell(at(other, dx))
            tell(at(other, dx, 0, -mate(core)))
            tell(at(core, dx, 0, mate(core)))

    for dy in (1, 2, 3):
        tell(at(core, 0, dy))
    for dx in range(RING):
        tell(at(z_lo, dx, 0, mate(core)))
    for n in range(2):
        tell(at(z_lo, 2 * core + n - x, 0, 2))
    pl.when(home)(tell_home)
    pl.when(away)(tell_away)
    early = [
        pltpu.make_async_copy(src, dst, local_sem.at[n])
        for n, (src, dst) in enumerate((
            (k_ref.at[1], k_raw.at[y]), (v_ref.at[1], v_raw.at[y]), (perm_ref, perm), (seg_ref, seg),
        ))
    ]
    for copy in early:
        copy.start()
    mine = (half == core).astype(jnp.int32)
    pl.semaphore_wait(barrier, 18 + apart * (1 + 4 * mine))

    firsts = []
    own_key = home & (half == core)

    def first(src, dst, n, device, own=False):
        copy = pltpu.make_async_remote_copy(
            src_ref=src,
            dst_ref=dst,
            send_sem=first_send.at[len(firsts)],
            recv_sem=first_recv.at[n],
            device_id=device,
            device_id_type=MESH,
        )
        firsts.append((copy, own))
        if own is False:
            copy.start()
        else:
            pl.when(jnp.logical_not(own))(copy.start)
            pl.when(own)(pltpu.make_async_copy(src, dst, first_recv.at[n]).start)

    def landed(ref, n):
        pltpu.make_async_copy(ref, ref, first_recv.at[n]).wait()

    def left(copies):
        for copy, own in copies:
            if own is False:
                copy.wait_send()
            else:
                pl.when(jnp.logical_not(own))(copy.wait_send)

    count = [0]

    def send(src, dst, device):
        n = count[0]
        count[0] += 1
        copy = pltpu.make_async_remote_copy(
            src_ref=src,
            dst_ref=dst,
            send_sem=send_sem.at[n],
            recv_sem=recv_sem.at[n],
            device_id=device,
            device_id_type=MESH,
        )
        copy.start()
        return copy

    targets = [(k, dx) for k in range(2) for dx in (1, 3, 2, 0)]
    ways = ((1, -1), (3, 1), (2, 2))
    here_x = pl.ds(2 * core, 2)

    class Spread:
        def __init__(self, ref, raw, everything, offset):
            self.ref, self.raw, self.all, self.offset = ref, raw, everything, offset
            self.shares = []

        def straight(self, source, dst, offset):
            before = len(firsts)
            for k, dx in targets:
                first(
                    source.at[..., columns(turn(x, dx), HEAD_DIM)],
                    dst,
                    self.offset + offset + z * 2 + x_odd,
                    at(half, dx, 0, apart + 2 * k),
                    own_key if k == 0 and dx == 0 else False,
                )
            return firsts[before:]

        def share(self, ref):
            self.shares.append(send(ref, ref, at(other)))

        def start(self):
            self.out = self.straight(self.ref.at[0], self.all.at[z, y, x], 0)
            self.along = [send(self.ref.at[1], self.raw.at[y], at(core, 0, d)) for d, _ in ways]

        def first_lands(self):
            for line in range(RING):
                for odd in range(2):
                    landed(self.all.at[line, y, 2 * core + odd], self.offset + line * 2 + odd)
            piece = self.all.at[0:RING, y, here_x]
            self.far = [send(piece, piece, at(core, 0, d)) for d, _ in ways]
            self.share(piece)

        def second_lands(self):
            for copy in self.along:
                copy.wait_recv()
            self.second = self.straight(self.raw, self.all.at[RING + z, :, x], 8)

        def take_first(self, n):
            self.far[n].wait_recv()
            self.share(self.all.at[0:RING, turn(y, ways[n][1]), here_x])

        def take_second(self, dz):
            line = turn(z, dz)
            for odd in range(2):
                landed(self.all.at[RING + line, :, 2 * core + odd], self.offset + 8 + line * 2 + odd)
            self.share(self.all.at[RING + line, :, here_x])

    keys = Spread(k_ref, k_raw, k_all, 0)
    values = Spread(v_ref, v_raw, v_all, 16)
    keys.start()
    values.start()
    before = len(firsts)
    for dx in (1, 3, 2, 0):
        for b in range(2):
            first(
                q_ref.at[b, :, columns(turn(x, dx), WIDE)],
                q_all.at[z_lo * RING + x],
                32 + z_lo * RING + x,
                at(b, dx, 0, apart * mate(b)),
                home & (core == b) if dx == 0 else False,
            )
    asked = firsts[before:]
    for copy in early:
        copy.wait()
    meta_vec[...] = tables(perm[...], seg[...])
    to_scalars = pltpu.make_async_copy(meta_vec, meta, local_sem.at[4])
    to_scalars.start()

    keys.first_lands()
    keys.second_lands()
    for copy in keys.far:
        copy.wait_send()
    values.first_lands()
    left(keys.second)
    values.second_lands()
    for n in range(3):
        keys.take_first(n)
    for dz in (0, 1, 3, 2):
        keys.take_second(dz)
    to_scalars.wait()
    for n in range(HELD):
        landed(q_all.at[n], 32 + n)
    for copy in keys.shares:
        copy.wait_recv()

    def later():
        left(keys.out + values.out + asked)
        for copy in keys.along + values.along + keys.shares:
            copy.wait_send()
        yield
        for n in range(3):
            values.take_first(n)
            yield
        for dz in (0, 1, 3, 2):
            values.take_second(dz)
            yield
        left(values.second)
        for copy in values.far + values.shares:
            copy.wait_send()
        for copy in values.shares:
            copy.wait_recv()
        yield

    v_steps = later()
    next(v_steps)

    def slot(n):
        far_z = turn(z, jnp.where(z_lo == n // 4, 0, mate(core)))
        return (((far_z // 2 * RING + y) * 2 + lax.rem(far_z, 2)) * RING + n % 4) * 2 + core

    def rows_of(ref, block, start, count):
        parts = []
        for u in range(count):
            there = jnp.clip(block - (REACH - 1) + start + u, 0, BLOCKS - 1)
            place = meta[2, there]
            parts.append(ref[place >> 4, (place >> 2) & 3, place & 3])
        return jnp.concatenate(parts, axis=0)

    def score(i):
        block = meta[0, slot(i)]
        row_pos = block * BLOCK + lax.broadcasted_iota(jnp.int32, (BLOCK, HEAD_DIM), 0)
        row_low = jnp.zeros((BLOCK, HEAD_DIM), jnp.int32)
        for s in range(1, SEGMENTS):
            row_low = jnp.where(meta[1, s] <= row_pos, meta[1, s], row_low)
        q = jnp.concatenate(
            [q_all[i, :, j * HEAD_DIM:(j + 1) * HEAD_DIM] for j in range(GROUP)], axis=0
        )
        pieces = []
        top = None
        for start in range(-2, REACH - 2, 4):
            begin, count = max(start, 0), 4 + min(start, 0)
            s = lax.dot_general(
                q, rows_of(k_all, block, begin, count), (((1,), (1,)), ((), ())),
                preferred_element_type=jnp.float32,
            )
            for half in range(count // 2):
                index = begin + 2 * half
                col = (block - (REACH - 1) + index) * BLOCK + lax.broadcasted_iota(
                    jnp.int32, (BLOCK, HEAD_DIM), 1
                )
                seen = col >= row_low
                if index == REACH - 2:
                    seen = seen & (col <= row_pos)
                seen = jnp.concatenate([seen] * GROUP, axis=0)
                piece = jnp.where(seen, s[:, half * HEAD_DIM:(half + 1) * HEAD_DIM], NEG)
                pieces.append(piece)
                top = piece if top is None else jnp.maximum(top, piece)
        top = jnp.max(top, axis=1, keepdims=True)
        total = None
        for n, piece in enumerate(pieces):
            weight = jnp.exp2((piece - top) * SCALE)
            total = weight if total is None else total + weight
            weights[i, :, n * HEAD_DIM:(n + 1) * HEAD_DIM] = weight.astype(jnp.bfloat16)
        total = jnp.sum(total, axis=1, keepdims=True)
        scale[i] = jnp.broadcast_to(1.0 / total, (ROWS, HEAD_DIM))

    for n in range(0, HELD, 2):
        score(n)
        score(n + 1)
        next(v_steps)
        next(v_steps)

    def blend(i):
        block = meta[0, slot(i)]
        mixed = jnp.dot(weights[i], rows_of(v_all, block, 0, REACH), preferred_element_type=jnp.float32)
        return (mixed * scale[i]).astype(jnp.bfloat16)

    def place(ref, mixed):
        for j in range(GROUP):
            ref[:, j * HEAD_DIM:(j + 1) * HEAD_DIM] = mixed[j * BLOCK:(j + 1) * BLOCK]

    order = ((2, 0), (1, 1), (3, 0), (2, 1), (1, 0), (3, 1), (0, 0), (0, 1))
    rows = pl.ds(pl.multiple_of(core * BLOCK, BLOCK), BLOCK)

    def whose(n):
        dx, same = order[n]
        return dx, z_lo if same else 1 - z_lo

    def answer(n):
        dx, to_lo = whose(n)
        return pltpu.make_async_remote_copy(
            src_ref=o_all.at[n],
            dst_ref=out_ref.at[rows, columns(x, WIDE)],
            send_sem=o_send.at[n],
            recv_sem=o_recv.at[core * RING + x],
            device_id=at(z_lo, dx, 0, jnp.where(to_lo == z_lo, 0, mate(core))),
            device_id_type=MESH,
        )

    def reply(n):
        dx, to_lo = whose(n)
        mixed = blend(to_lo * RING + turn(x, dx))
        for j in range(GROUP):
            o_all[n, :, j * HEAD_DIM:(j + 1) * HEAD_DIM] = mixed[j * BLOCK:(j + 1) * BLOCK]

    last = HELD - 1
    for n in range(HELD):
        reply(n)
        if n < last:
            answer(n).start()
    pl.when(away)(answer(last).start)
    pl.when(home)(
        pltpu.make_async_copy(
            o_all.at[last], out_ref.at[rows, columns(x, WIDE)], o_recv.at[core * RING + x]
        ).start
    )
    for b in range(2):
        for j in range(RING):
            ref = out_ref.at[b * BLOCK:(b + 1) * BLOCK, j * WIDE:(j + 1) * WIDE]
            pltpu.make_async_copy(ref, ref, o_recv.at[b * RING + j]).wait()

    for n in range(last):
        answer(n).wait_send()
    pl.when(away)(answer(last).wait_send)


COPIES = 2 * (3 + 3 + 8)
FIRSTS = 2 * (8 + 8) + 8


def shards(queries, keys, values, permutation, segment):
    hbm = pl.BlockSpec(memory_space=pltpu.HBM)
    inputs = (
        *(a.reshape(2, BLOCK, -1) for a in (queries, keys, values)),
        permutation.reshape(1, BLOCKS),
        segment.reshape(SEQ // BLOCKS, BLOCKS),
    )
    return pl.pallas_call(
        episode_kernel,
        out_shape=jax.ShapeDtypeStruct(queries.shape, jnp.bfloat16),
        in_specs=[hbm] * 5,
        out_specs=pl.BlockSpec(memory_space=pltpu.VMEM),
        scratch_shapes=[
            pltpu.VMEM((1, BLOCKS), jnp.int32),
            pltpu.VMEM((SEQ // BLOCKS, BLOCKS), jnp.int32),
            pltpu.VMEM((8, BLOCKS), jnp.int32),
            pltpu.SMEM((8, BLOCKS), jnp.int32),
            pltpu.VMEM((HELD, BLOCK, WIDE), jnp.bfloat16),
            pltpu.VMEM((2 * RING, RING, RING, BLOCK, HEAD_DIM), jnp.bfloat16),
            pltpu.VMEM((2 * RING, RING, RING, BLOCK, HEAD_DIM), jnp.bfloat16),
            pltpu.VMEM((RING, BLOCK, WIDE), jnp.bfloat16),
            pltpu.VMEM((RING, BLOCK, WIDE), jnp.bfloat16),
            pltpu.VMEM((HELD, ROWS, WIDTH), jnp.bfloat16),
            pltpu.VMEM((HELD, ROWS, HEAD_DIM), jnp.float32),
            pltpu.VMEM((HELD, BLOCK, WIDE), jnp.bfloat16),
            pltpu.SemaphoreType.DMA((COPIES,)),
            pltpu.SemaphoreType.DMA((COPIES,)),
            pltpu.SemaphoreType.DMA((FIRSTS,)),
            pltpu.SemaphoreType.DMA((FIRSTS,)),
            pltpu.SemaphoreType.DMA((HELD,)),
            pltpu.SemaphoreType.DMA((HELD,)),
            pltpu.SemaphoreType.DMA((5,)),
        ],
        compiler_params=pltpu.CompilerParams(
            collective_id=0, has_side_effects=True, vmem_limit_bytes=40 << 20
        ),
        name="episode",
    )(*(pltpu.with_memory_space_constraint(a, pltpu.HBM) for a in inputs))


def solution(mesh):
    fine = Mesh(mesh.devices.reshape(2, 2, 4, 2, 4), AXES)
    slots = AXES[1:]
    return jax.shard_map(
        shards,
        mesh=fine,
        in_specs=(P(slots, "head"), P(slots, "head"), P(slots, "head"), P(), P()),
        out_specs=P(slots, "head"),
        check_vma=False,
    )
```

```python
import math

import jax
import jax.numpy as jnp
from jax import lax
from jax.experimental import pallas as pl
from jax.experimental.pallas import tpu as pltpu
from jax.sharding import Mesh, PartitionSpec as P

HEAD_DIM = 128
BLOCK = 64
BLOCKS = 128
SEQ = 8192
SEGMENTS = 8
GROUP = 4
RING = 4
LOCAL = 128
ROWS = GROUP * BLOCK
WIDE = GROUP * HEAD_DIM
HELD = 2 * RING
REACH = 34
WIDTH = REACH * BLOCK
SCALE = math.log2(math.e) / math.sqrt(HEAD_DIM)
NEG = -1e30
MESH = pl.DeviceIdType.MESH
AXES = ("head", "z_hi", "y", "z_lo", "x")


def landing(slot):
    z = slot // 64 * 2 + slot // 8 % 2
    y = slot // 16 % 4
    return ((slot % 2 * RING + z) * RING + y) * RING + slot // 2 % 4


def turn(value, shift):
    return lax.rem(value + shift + RING, RING)


def columns(j, width):
    return pl.ds(pl.multiple_of(j * width, width), width)


def tables(perm, seg):
    lane = lax.broadcasted_iota(jnp.int32, (1, BLOCKS), 1)
    starts = jnp.zeros((1, BLOCKS), jnp.int32)
    for s in range(1, SEGMENTS):
        count = jnp.sum((seg < s).astype(jnp.int32), axis=1, keepdims=True)
        count = jnp.sum(count, axis=0, keepdims=True)
        starts = jnp.where(lane == s, count, starts)
    slot = lax.broadcasted_iota(jnp.int32, (BLOCKS, BLOCKS), 0)
    block = lax.broadcasted_iota(jnp.int32, (BLOCKS, BLOCKS), 1)
    held = jnp.sum(jnp.where(slot == block, perm, 0), axis=1, keepdims=True)
    inverse = jnp.sum(jnp.where(held == block, landing(slot), 0), axis=0, keepdims=True)
    inverse = jnp.minimum(inverse, BLOCKS - 1)
    return jnp.concatenate([perm, starts, inverse, jnp.zeros((5, BLOCKS), jnp.int32)], axis=0)


def episode_kernel(
    q_ref, k_ref, v_ref, perm_ref, seg_ref, out_ref,
    perm, seg, meta_vec, meta, q_all, k_all, v_all, k_part, v_part, k_raw, v_raw, weights, scale, o_all,
    send_sem, recv_sem, first_send, first_recv, o_send, o_recv, local_sem,
):
    core, z_hi, y, z_lo, x = (lax.axis_index(a) for a in AXES)
    z = z_hi * 2 + z_lo
    other = 1 - core
    apart = lax.rem(z_lo + core, 2)
    home = apart == 0
    away = jnp.logical_not(home)
    half = x // 2
    x_odd, y_odd = lax.rem(x, 2), lax.rem(y, 2)

    def cube(b, ex, ey, ez):
        way = 1 - 2 * b
        return ex * way * (1 - 2 * x_odd), ey * way * (1 - 2 * y_odd), ez * way * (1 - 2 * z_lo)

    def at(to_core, dx=0, dy=0, dz=0):
        far_z = turn(z, dz)
        return (to_core, far_z // 2, turn(y, dy), lax.rem(far_z, 2), turn(x, dx))

    barrier = pltpu.get_barrier_semaphore()

    def tell(device):
        pl.semaphore_signal(barrier, inc=1, device_id=device, device_id_type=MESH)

    own_key = home & (half == core)
    across = [(ex, ey) for ey in range(2) for ex in range(2)]
    for dy in (1, 2, 3):
        tell(at(core, 0, dy))
    for n in range(2):
        for dz in range(RING):
            device = at(z_lo, 2 * core + n - x, 0, dz)
            if dz:
                tell(device)
            else:
                pl.when(jnp.logical_not(home & (x == 2 * core + n)))(lambda device=device: tell(device))
    for ex, ey in across:
        tell(at(z_lo, *cube(core, ex, ey, 1)))
        tell(at(other, *cube(other, ex, ey, apart)))

    def tell_home():
        for ex, ey in across[1:]:
            tell(at(core, *cube(core, ex, ey, 0)))

    def tell_away():
        for ex, ey in across:
            tell(at(z_lo, *cube(core, ex, ey, 0)))
            tell(at(core, *cube(core, ex, ey, 1)))

    pl.when(home)(tell_home)
    pl.when(away)(tell_away)
    early = [
        pltpu.make_async_copy(src, dst, local_sem.at[n])
        for n, (src, dst) in enumerate((
            *(
                (ref.at[1, :, columns(2 * odd + y_odd, HEAD_DIM)], raw.at[y, odd])
                for ref, raw in ((k_ref, k_raw), (v_ref, v_raw))
                for odd in range(2)
            ),
            (perm_ref, perm),
            (seg_ref, seg),
        ))
    ]
    for copy in early:
        copy.start()
    pl.semaphore_wait(barrier, 22 + 5 * apart - own_key.astype(jnp.int32))

    firsts = []

    def first(src, dst, n, device, own=False):
        copy = pltpu.make_async_remote_copy(
            src_ref=src,
            dst_ref=dst,
            send_sem=first_send.at[len(firsts)],
            recv_sem=first_recv.at[n],
            device_id=device,
            device_id_type=MESH,
        )
        firsts.append((copy, own))
        if own is False:
            copy.start()
        else:
            pl.when(jnp.logical_not(own))(copy.start)
            pl.when(own)(pltpu.make_async_copy(src, dst, first_recv.at[n]).start)

    def landed(ref, n):
        pltpu.make_async_copy(ref, ref, first_recv.at[n]).wait()

    def left(copies):
        for copy, own in copies:
            if own is False:
                copy.wait_send()
            else:
                pl.when(jnp.logical_not(own))(copy.wait_send)

    count = [0]

    def send(src, dst, device):
        n = count[0]
        count[0] += 1
        copy = pltpu.make_async_remote_copy(
            src_ref=src,
            dst_ref=dst,
            send_sem=send_sem.at[n],
            recv_sem=recv_sem.at[n],
            device_id=device,
            device_id_type=MESH,
        )
        copy.start()
        return copy

    targets = [(k, dx) for k in range(2) for dx in (1, 3, 2, 0)]
    ways = ((1, -1), (3, 1), (2, 2))
    here_x = pl.ds(2 * core, 2)

    class Spread:
        def __init__(self, ref, part, raw, everything, offset, own_sem):
            self.ref, self.part, self.raw, self.all, self.offset = ref, part, raw, everything, offset
            self.own_sem = own_sem
            self.shares = []

        def straight(self, source, dst, offset):
            before = len(firsts)
            for k, dx in targets:
                first(
                    source(lax.rem(x + dx, 2)),
                    dst,
                    self.offset + offset + z * 2 + x_odd,
                    at(half, dx, 0, apart + 2 * k),
                    own_key if k == 0 and dx == 0 else False,
                )
            return firsts[before:]

        def share(self, src, dst):
            self.shares.append(send(src, dst, at(other)))

        def start(self):
            self.out = self.straight(
                lambda odd: self.ref.at[0, :, columns(odd, 2 * HEAD_DIM)], self.part.at[z, x_odd], 0
            )
            self.along = [
                send(
                    self.ref.at[1, :, columns(2 * odd + lax.rem(y + d, 2), HEAD_DIM)],
                    self.raw.at[y, odd],
                    at(core, 0, d),
                )
                for d, _ in ways
                for odd in range(2)
            ]

        def first_lands(self):
            for line in range(RING):
                for odd in range(2):
                    landed(self.part.at[line, odd], self.offset + line * 2 + odd)
            dst = self.all.at[0:RING, y, here_x]

            def piece(d):
                return self.part.at[:, :, :, columns(lax.rem(y + d, 2), HEAD_DIM)]

            self.far = [send(piece(d), dst, at(core, 0, d)) for d, _ in ways]
            self.share(piece(0), dst)
            self.own = pltpu.make_async_copy(piece(0), dst, self.own_sem)
            self.own.start()

        def second_lands(self):
            for copy in self.along:
                copy.wait_recv()
            self.second = self.straight(
                lambda odd: self.raw.at[:, odd], self.all.at[RING + z, :, x], 8
            )

        def take_first(self, n):
            self.far[n].wait_recv()
            ref = self.all.at[0:RING, turn(y, ways[n][1]), here_x]
            self.share(ref, ref)

        def take_second(self, dz):
            line = turn(z, dz)
            for odd in range(2):
                landed(self.all.at[RING + line, :, 2 * core + odd], self.offset + 8 + line * 2 + odd)
            ref = self.all.at[RING + line, :, here_x]
            self.share(ref, ref)

    keys = Spread(k_ref, k_part, k_raw, k_all, 0, local_sem.at[7])
    values = Spread(v_ref, v_part, v_raw, v_all, 16, local_sem.at[8])
    keys.start()
    values.start()
    before = len(firsts)
    for b in range(2):
        for ex, ey in reversed(across):
            n = apart * 4 + ey * 2 + ex
            first(
                q_ref.at[b, :, columns(2 * lax.rem(x + ex, 2) + lax.rem(y + ey, 2), WIDE)],
                q_all.at[n],
                32 + n,
                at(b, *cube(b, ex, ey, apart)),
                home & (core == b) if not (ex or ey) else False,
            )
    asked = firsts[before:]
    for copy in early:
        copy.wait()
    meta_vec[...] = tables(perm[...], seg[...])
    to_scalars = pltpu.make_async_copy(meta_vec, meta, local_sem.at[6])
    to_scalars.start()

    keys.first_lands()
    keys.second_lands()
    for copy in keys.far:
        copy.wait_send()
    values.first_lands()
    left(keys.second)
    values.second_lands()
    for n in range(3):
        keys.take_first(n)
    for dz in (0, 1, 3, 2):
        keys.take_second(dz)
    to_scalars.wait()
    for n in range(HELD):
        landed(q_all.at[n], 32 + n)
    keys.own.wait()
    for copy in keys.shares:
        copy.wait_recv()

    def later():
        left(keys.out + values.out + asked)
        for copy in keys.along + values.along + keys.shares:
            copy.wait_send()
        yield
        for n in range(3):
            values.take_first(n)
            yield
        for dz in (0, 1, 3, 2):
            values.take_second(dz)
            yield
        left(values.second)
        for copy in values.far + values.shares:
            copy.wait_send()
        values.own.wait()
        for copy in values.shares:
            copy.wait_recv()
        yield

    v_steps = later()
    next(v_steps)

    def slot(n):
        dx, dy, dz = cube(core, n % 2, n // 2 % 2, n // 4)
        far_z = turn(z, dz)
        return (((far_z // 2 * RING + turn(y, dy)) * 2 + lax.rem(far_z, 2)) * RING + turn(x, dx)) * 2 + core

    def rows_of(ref, block, start, count):
        parts = []
        for u in range(count):
            there = jnp.clip(block - (REACH - 1) + start + u, 0, BLOCKS - 1)
            place = meta[2, there]
            parts.append(ref[place >> 4, (place >> 2) & 3, place & 3])
        return jnp.concatenate(parts, axis=0)

    def score(i):
        block = meta[0, slot(i)]
        row_pos = block * BLOCK + lax.broadcasted_iota(jnp.int32, (BLOCK, HEAD_DIM), 0)
        row_low = jnp.zeros((BLOCK, HEAD_DIM), jnp.int32)
        for s in range(1, SEGMENTS):
            row_low = jnp.where(meta[1, s] <= row_pos, meta[1, s], row_low)
        q = jnp.concatenate(
            [q_all[i, :, j * HEAD_DIM:(j + 1) * HEAD_DIM] for j in range(GROUP)], axis=0
        )
        pieces = []
        top = None
        for start in range(-2, REACH - 2, 4):
            begin, count = max(start, 0), 4 + min(start, 0)
            s = lax.dot_general(
                q, rows_of(k_all, block, begin, count), (((1,), (1,)), ((), ())),
                preferred_element_type=jnp.float32,
            )
            for half in range(count // 2):
                index = begin + 2 * half
                col = (block - (REACH - 1) + index) * BLOCK + lax.broadcasted_iota(
                    jnp.int32, (BLOCK, HEAD_DIM), 1
                )
                seen = col >= row_low
                if index == REACH - 2:
                    seen = seen & (col <= row_pos)
                seen = jnp.concatenate([seen] * GROUP, axis=0)
                piece = jnp.where(seen, s[:, half * HEAD_DIM:(half + 1) * HEAD_DIM], NEG)
                pieces.append(piece)
                top = piece if top is None else jnp.maximum(top, piece)
        top = jnp.max(top, axis=1, keepdims=True)
        total = None
        for n, piece in enumerate(pieces):
            weight = jnp.exp2((piece - top) * SCALE)
            total = weight if total is None else total + weight
            weights[i, :, n * HEAD_DIM:(n + 1) * HEAD_DIM] = weight.astype(jnp.bfloat16)
        total = jnp.sum(total, axis=1, keepdims=True)
        scale[i] = jnp.broadcast_to(1.0 / total, (ROWS, HEAD_DIM))

    for n in range(0, HELD, 2):
        score(n)
        score(n + 1)
        next(v_steps)
        next(v_steps)

    def blend(i):
        block = meta[0, slot(i)]
        mixed = jnp.dot(weights[i], rows_of(v_all, block, 0, REACH), preferred_element_type=jnp.float32)
        return (mixed * scale[i]).astype(jnp.bfloat16)

    def place(ref, mixed):
        for j in range(GROUP):
            ref[:, j * HEAD_DIM:(j + 1) * HEAD_DIM] = mixed[j * BLOCK:(j + 1) * BLOCK]

    rows = pl.ds(pl.multiple_of(core * BLOCK, BLOCK), BLOCK)
    mine = columns(2 * x_odd + y_odd, WIDE)

    def answer(n):
        return pltpu.make_async_remote_copy(
            src_ref=o_all.at[n],
            dst_ref=out_ref.at[rows, mine],
            send_sem=o_send.at[n],
            recv_sem=o_recv.at[core * 4 + n % 4],
            device_id=at(z_lo, *cube(core, n % 2, n // 2 % 2, n // 4)),
            device_id_type=MESH,
        )

    for n in (7, 6, 5, 3, 4, 2, 1, 0):
        mixed = blend(n)
        for j in range(GROUP):
            o_all[n, :, j * HEAD_DIM:(j + 1) * HEAD_DIM] = mixed[j * BLOCK:(j + 1) * BLOCK]
        if n:
            answer(n).start()
    pl.when(away)(answer(0).start)
    pl.when(home)(
        pltpu.make_async_copy(o_all.at[0], out_ref.at[rows, mine], o_recv.at[core * 4]).start
    )
    for b in range(2):
        for n, (ex, ey) in enumerate(across):
            j = 2 * lax.rem(x + ex, 2) + lax.rem(y + ey, 2)
            ref = out_ref.at[b * BLOCK:(b + 1) * BLOCK, columns(j, WIDE)]
            pltpu.make_async_copy(ref, ref, o_recv.at[b * 4 + n]).wait()
    for n in range(1, HELD):
        answer(n).wait_send()
    pl.when(away)(answer(0).wait_send)


COPIES = 2 * (6 + 3 + 8)
FIRSTS = 2 * (8 + 8) + 8


def shards(queries, keys, values, permutation, segment):
    hbm = pl.BlockSpec(memory_space=pltpu.HBM)
    inputs = (
        *(a.reshape(2, BLOCK, -1) for a in (queries, keys, values)),
        permutation.reshape(1, BLOCKS),
        segment.reshape(SEQ // BLOCKS, BLOCKS),
    )
    return pl.pallas_call(
        episode_kernel,
        out_shape=jax.ShapeDtypeStruct(queries.shape, jnp.bfloat16),
        in_specs=[hbm] * 5,
        out_specs=pl.BlockSpec(memory_space=pltpu.VMEM),
        scratch_shapes=[
            pltpu.VMEM((1, BLOCKS), jnp.int32),
            pltpu.VMEM((SEQ // BLOCKS, BLOCKS), jnp.int32),
            pltpu.VMEM((8, BLOCKS), jnp.int32),
            pltpu.SMEM((8, BLOCKS), jnp.int32),
            pltpu.VMEM((HELD, BLOCK, WIDE), jnp.bfloat16),
            pltpu.VMEM((2 * RING, RING, RING, BLOCK, HEAD_DIM), jnp.bfloat16),
            pltpu.VMEM((2 * RING, RING, RING, BLOCK, HEAD_DIM), jnp.bfloat16),
            pltpu.VMEM((RING, 2, BLOCK, 2 * HEAD_DIM), jnp.bfloat16),
            pltpu.VMEM((RING, 2, BLOCK, 2 * HEAD_DIM), jnp.bfloat16),
            pltpu.VMEM((RING, 2, BLOCK, HEAD_DIM), jnp.bfloat16),
            pltpu.VMEM((RING, 2, BLOCK, HEAD_DIM), jnp.bfloat16),
            pltpu.VMEM((HELD, ROWS, WIDTH), jnp.bfloat16),
            pltpu.VMEM((HELD, ROWS, HEAD_DIM), jnp.float32),
            pltpu.VMEM((HELD, BLOCK, WIDE), jnp.bfloat16),
            pltpu.SemaphoreType.DMA((COPIES,)),
            pltpu.SemaphoreType.DMA((COPIES,)),
            pltpu.SemaphoreType.DMA((FIRSTS,)),
            pltpu.SemaphoreType.DMA((FIRSTS,)),
            pltpu.SemaphoreType.DMA((HELD,)),
            pltpu.SemaphoreType.DMA((HELD,)),
            pltpu.SemaphoreType.DMA((9,)),
        ],
        compiler_params=pltpu.CompilerParams(
            collective_id=0, has_side_effects=True, vmem_limit_bytes=40 << 20
        ),
        name="episode",
    )(*(pltpu.with_memory_space_constraint(a, pltpu.HBM) for a in inputs))


def solution(mesh):
    fine = Mesh(mesh.devices.reshape(2, 2, 4, 2, 4), AXES)
    slots = AXES[1:]
    return jax.shard_map(
        shards,
        mesh=fine,
        in_specs=(P(slots, "head"), P(slots, "head"), P(slots, "head"), P(), P()),
        out_specs=P(slots, "head"),
        check_vma=False,
    )
```

```python
import math

import jax
import jax.numpy as jnp
from jax import lax
from jax.experimental import pallas as pl
from jax.experimental.pallas import tpu as pltpu
from jax.sharding import Mesh, PartitionSpec as P

HEAD_DIM = 128
BLOCK = 64
BLOCKS = 128
SEQ = 8192
SEGMENTS = 8
GROUP = 4
RING = 4
LOCAL = 128
ROWS = GROUP * BLOCK
WIDE = GROUP * HEAD_DIM
HELD = 2 * RING
REACH = 34
WIDTH = REACH * BLOCK
SCALE = math.log2(math.e) / math.sqrt(HEAD_DIM)
NEG = -1e30
MESH = pl.DeviceIdType.MESH
AXES = ("head", "z_hi", "y", "z_lo", "x")


def landing(slot):
    z = slot // 64 * 2 + slot // 8 % 2
    y = slot // 16 % 4
    return ((slot % 2 * RING + z) * RING + y) * RING + slot // 2 % 4


def turn(value, shift):
    return lax.rem(value + shift + RING, RING)


def columns(j, width):
    return pl.ds(pl.multiple_of(j * width, width), width)


def tables(perm, seg):
    lane = lax.broadcasted_iota(jnp.int32, (1, BLOCKS), 1)
    starts = jnp.zeros((1, BLOCKS), jnp.int32)
    for s in range(1, SEGMENTS):
        count = jnp.sum((seg < s).astype(jnp.int32), axis=1, keepdims=True)
        count = jnp.sum(count, axis=0, keepdims=True)
        starts = jnp.where(lane == s, count, starts)
    slot = lax.broadcasted_iota(jnp.int32, (BLOCKS, BLOCKS), 0)
    block = lax.broadcasted_iota(jnp.int32, (BLOCKS, BLOCKS), 1)
    held = jnp.sum(jnp.where(slot == block, perm, 0), axis=1, keepdims=True)
    inverse = jnp.sum(jnp.where(held == block, landing(slot), 0), axis=0, keepdims=True)
    inverse = jnp.minimum(inverse, BLOCKS - 1)
    return jnp.concatenate([perm, starts, inverse, jnp.zeros((5, BLOCKS), jnp.int32)], axis=0)


def episode_kernel(
    q_ref, k_ref, v_ref, perm_ref, seg_ref, out_ref,
    perm, seg, meta_vec, meta, q_all, k_all, v_all, k_part, v_part, k_raw, v_raw, weights, scale, o_all,
    send_sem, recv_sem, first_send, first_recv, o_send, o_recv, local_sem,
):
    core, z_hi, y, z_lo, x = (lax.axis_index(a) for a in AXES)
    z = z_hi * 2 + z_lo
    other = 1 - core
    apart = lax.rem(z_lo + core, 2)
    home = apart == 0
    away = jnp.logical_not(home)
    half = x // 2
    x_odd, y_odd = lax.rem(x, 2), lax.rem(y, 2)

    def cube(b, ex, ey, ez):
        way = 1 - 2 * b
        return ex * way * (1 - 2 * x_odd), ey * way * (1 - 2 * y_odd), ez * way * (1 - 2 * z_lo)

    def at(to_core, dx=0, dy=0, dz=0):
        far_z = turn(z, dz)
        return (to_core, far_z // 2, turn(y, dy), lax.rem(far_z, 2), turn(x, dx))

    barrier = pltpu.get_barrier_semaphore()

    def tell(device):
        pl.semaphore_signal(barrier, inc=1, device_id=device, device_id_type=MESH)

    own_key = home & (half == core)
    across = [(ex, ey) for ey in range(2) for ex in range(2)]
    for dy in (1, 2, 3):
        tell(at(core, 0, dy))
    for n in range(2):
        for dz in range(RING):
            device = at(z_lo, 2 * core + n - x, 0, dz)
            if dz:
                tell(device)
            else:
                pl.when(jnp.logical_not(home & (x == 2 * core + n)))(lambda device=device: tell(device))
    for ex, ey in across:
        tell(at(z_lo, *cube(core, ex, ey, 1)))
        tell(at(other, *cube(other, ex, ey, apart)))

    def tell_home():
        for ex, ey in across[1:]:
            tell(at(core, *cube(core, ex, ey, 0)))

    def tell_away():
        for ex, ey in across:
            tell(at(z_lo, *cube(core, ex, ey, 0)))
            tell(at(core, *cube(core, ex, ey, 1)))

    pl.when(home)(tell_home)
    pl.when(away)(tell_away)
    early = [
        pltpu.make_async_copy(src, dst, local_sem.at[n])
        for n, (src, dst) in enumerate((
            *(
                (ref.at[1, :, columns(2 * odd + y_odd, HEAD_DIM)], raw.at[y, odd])
                for ref, raw in ((k_ref, k_raw), (v_ref, v_raw))
                for odd in range(2)
            ),
            (perm_ref, perm),
            (seg_ref, seg),
        ))
    ]
    for copy in early:
        copy.start()
    pl.semaphore_wait(barrier, 22 + 5 * apart - own_key.astype(jnp.int32))

    firsts = []

    def first(src, dst, n, device, own=False):
        copy = pltpu.make_async_remote_copy(
            src_ref=src,
            dst_ref=dst,
            send_sem=first_send.at[len(firsts)],
            recv_sem=first_recv.at[n],
            device_id=device,
            device_id_type=MESH,
        )
        firsts.append((copy, own))
        if own is False:
            copy.start()
        else:
            pl.when(jnp.logical_not(own))(copy.start)
            pl.when(own)(pltpu.make_async_copy(src, dst, first_recv.at[n]).start)

    def landed(ref, n):
        pltpu.make_async_copy(ref, ref, first_recv.at[n]).wait()

    def left(copies):
        for copy, own in copies:
            if own is False:
                copy.wait_send()
            else:
                pl.when(jnp.logical_not(own))(copy.wait_send)

    count = [0]

    def send(src, dst, device):
        n = count[0]
        count[0] += 1
        copy = pltpu.make_async_remote_copy(
            src_ref=src,
            dst_ref=dst,
            send_sem=send_sem.at[n],
            recv_sem=recv_sem.at[n],
            device_id=device,
            device_id_type=MESH,
        )
        copy.start()
        return copy

    targets = [(k, dx) for k in range(2) for dx in (1, 3, 2, 0)]
    ways = ((1, -1), (3, 1), (2, 2))
    here_x = pl.ds(2 * core, 2)

    class Spread:
        def __init__(self, ref, part, raw, everything, offset, own_sem):
            self.ref, self.part, self.raw, self.all, self.offset = ref, part, raw, everything, offset
            self.own_sem = own_sem
            self.shares = []

        def straight(self, source, dst, offset):
            before = len(firsts)
            for k, dx in targets:
                first(
                    source(lax.rem(x + dx, 2)),
                    dst,
                    self.offset + offset + z * 2 + x_odd,
                    at(half, dx, 0, apart + 2 * k),
                    own_key if k == 0 and dx == 0 else False,
                )
            return firsts[before:]

        def share(self, src, dst):
            self.shares.append(send(src, dst, at(other)))

        def start(self):
            self.out = self.straight(
                lambda odd: self.ref.at[0, :, columns(odd, 2 * HEAD_DIM)], self.part.at[z, x_odd], 0
            )
            self.along = [
                send(
                    self.ref.at[1, :, columns(2 * odd + lax.rem(y + d, 2), HEAD_DIM)],
                    self.raw.at[y, odd],
                    at(core, 0, d),
                )
                for d, _ in ways
                for odd in range(2)
            ]

        def first_lands(self):
            for line in range(RING):
                for odd in range(2):
                    landed(self.part.at[line, odd], self.offset + line * 2 + odd)
            dst = self.all.at[0:RING, y, here_x]

            def piece(d):
                return self.part.at[:, :, :, columns(lax.rem(y + d, 2), HEAD_DIM)]

            self.far = [send(piece(d), dst, at(core, 0, d)) for d, _ in ways]
            self.share(piece(0), dst)
            self.own = pltpu.make_async_copy(piece(0), dst, self.own_sem)
            self.own.start()

        def second_lands(self):
            for copy in self.along:
                copy.wait_recv()
            self.second = self.straight(
                lambda odd: self.raw.at[:, odd], self.all.at[RING + z, :, x], 8
            )

        def take_first(self, n):
            self.far[n].wait_recv()
            ref = self.all.at[0:RING, turn(y, ways[n][1]), here_x]
            self.share(ref, ref)

        def take_second(self, dz):
            line = turn(z, dz)
            for odd in range(2):
                landed(self.all.at[RING + line, :, 2 * core + odd], self.offset + 8 + line * 2 + odd)
            ref = self.all.at[RING + line, :, here_x]
            self.share(ref, ref)

    keys = Spread(k_ref, k_part, k_raw, k_all, 0, local_sem.at[7])
    values = Spread(v_ref, v_part, v_raw, v_all, 16, local_sem.at[8])
    keys.start()
    before = len(firsts)
    for b in range(2):
        for ex, ey in reversed(across):
            n = apart * 4 + ey * 2 + ex
            first(
                q_ref.at[b, :, columns(2 * lax.rem(x + ex, 2) + lax.rem(y + ey, 2), WIDE)],
                q_all.at[n],
                32 + n,
                at(b, *cube(b, ex, ey, apart)),
                home & (core == b) if not (ex or ey) else False,
            )
    asked = firsts[before:]
    values.start()
    for copy in early:
        copy.wait()
    meta_vec[...] = tables(perm[...], seg[...])
    to_scalars = pltpu.make_async_copy(meta_vec, meta, local_sem.at[6])
    to_scalars.start()

    keys.second_lands()
    keys.first_lands()
    for copy in keys.far:
        copy.wait_send()
    values.first_lands()
    left(keys.second)
    values.second_lands()
    for n in range(3):
        keys.take_first(n)
    for dz in (0, 1, 3, 2):
        keys.take_second(dz)
    to_scalars.wait()
    for n in range(HELD):
        landed(q_all.at[n], 32 + n)
    keys.own.wait()
    for copy in keys.shares:
        copy.wait_recv()

    def later():
        left(keys.out + values.out + asked)
        for copy in keys.along + values.along + keys.shares:
            copy.wait_send()
        yield
        for n in range(3):
            values.take_first(n)
            yield
        for dz in (0, 1, 3, 2):
            values.take_second(dz)
            yield
        left(values.second)
        for copy in values.far + values.shares:
            copy.wait_send()
        values.own.wait()
        for copy in values.shares:
            copy.wait_recv()
        yield

    v_steps = later()
    next(v_steps)

    def slot(n):
        dx, dy, dz = cube(core, n % 2, n // 2 % 2, n // 4)
        far_z = turn(z, dz)
        return (((far_z // 2 * RING + turn(y, dy)) * 2 + lax.rem(far_z, 2)) * RING + turn(x, dx)) * 2 + core

    def rows_of(ref, block, start, count):
        parts = []
        for u in range(count):
            there = jnp.clip(block - (REACH - 1) + start + u, 0, BLOCKS - 1)
            place = meta[2, there]
            parts.append(ref[place >> 4, (place >> 2) & 3, place & 3])
        return jnp.concatenate(parts, axis=0)

    def score(i):
        block = meta[0, slot(i)]
        row_pos = block * BLOCK + lax.broadcasted_iota(jnp.int32, (BLOCK, HEAD_DIM), 0)
        row_low = jnp.zeros((BLOCK, HEAD_DIM), jnp.int32)
        for s in range(1, SEGMENTS):
            row_low = jnp.where(meta[1, s] <= row_pos, meta[1, s], row_low)
        q = jnp.concatenate(
            [q_all[i, :, j * HEAD_DIM:(j + 1) * HEAD_DIM] for j in range(GROUP)], axis=0
        )
        pieces = []
        top = None
        for start in range(-2, REACH - 2, 4):
            begin, count = max(start, 0), 4 + min(start, 0)
            s = lax.dot_general(
                q, rows_of(k_all, block, begin, count), (((1,), (1,)), ((), ())),
                preferred_element_type=jnp.float32,
            )
            for half in range(count // 2):
                index = begin + 2 * half
                col = (block - (REACH - 1) + index) * BLOCK + lax.broadcasted_iota(
                    jnp.int32, (BLOCK, HEAD_DIM), 1
                )
                seen = col >= row_low
                if index == REACH - 2:
                    seen = seen & (col <= row_pos)
                seen = jnp.concatenate([seen] * GROUP, axis=0)
                piece = jnp.where(seen, s[:, half * HEAD_DIM:(half + 1) * HEAD_DIM], NEG)
                pieces.append(piece)
                top = piece if top is None else jnp.maximum(top, piece)
        top = jnp.max(top, axis=1, keepdims=True)
        total = None
        for n, piece in enumerate(pieces):
            weight = jnp.exp2((piece - top) * SCALE)
            total = weight if total is None else total + weight
            weights[i, :, n * HEAD_DIM:(n + 1) * HEAD_DIM] = weight.astype(jnp.bfloat16)
        total = jnp.sum(total, axis=1, keepdims=True)
        scale[i] = jnp.broadcast_to(1.0 / total, (ROWS, HEAD_DIM))

    for n in range(0, HELD, 4):
        for m in range(n, n + 4):
            score(m)
        for _ in range(4):
            next(v_steps)

    def blend(i):
        block = meta[0, slot(i)]
        mixed = jnp.dot(weights[i], rows_of(v_all, block, 0, REACH), preferred_element_type=jnp.float32)
        return (mixed * scale[i]).astype(jnp.bfloat16)

    def place(ref, mixed):
        for j in range(GROUP):
            ref[:, j * HEAD_DIM:(j + 1) * HEAD_DIM] = mixed[j * BLOCK:(j + 1) * BLOCK]

    rows = pl.ds(pl.multiple_of(core * BLOCK, BLOCK), BLOCK)
    mine = columns(2 * x_odd + y_odd, WIDE)

    def answer(n):
        return pltpu.make_async_remote_copy(
            src_ref=o_all.at[n],
            dst_ref=out_ref.at[rows, mine],
            send_sem=o_send.at[n],
            recv_sem=o_recv.at[core * 4 + n % 4],
            device_id=at(z_lo, *cube(core, n % 2, n // 2 % 2, n // 4)),
            device_id_type=MESH,
        )

    for n in (7, 6, 5, 3, 4, 2, 1, 0):
        mixed = blend(n)
        for j in range(GROUP):
            o_all[n, :, j * HEAD_DIM:(j + 1) * HEAD_DIM] = mixed[j * BLOCK:(j + 1) * BLOCK]
        if n:
            answer(n).start()
    pl.when(away)(answer(0).start)
    pl.when(home)(
        pltpu.make_async_copy(o_all.at[0], out_ref.at[rows, mine], o_recv.at[core * 4]).start
    )
    for b in range(2):
        for n, (ex, ey) in enumerate(across):
            j = 2 * lax.rem(x + ex, 2) + lax.rem(y + ey, 2)
            ref = out_ref.at[b * BLOCK:(b + 1) * BLOCK, columns(j, WIDE)]
            pltpu.make_async_copy(ref, ref, o_recv.at[b * 4 + n]).wait()
    for n in range(1, HELD):
        answer(n).wait_send()
    pl.when(away)(answer(0).wait_send)


COPIES = 2 * (6 + 3 + 8)
FIRSTS = 2 * (8 + 8) + 8


def shards(queries, keys, values, permutation, segment):
    hbm = pl.BlockSpec(memory_space=pltpu.HBM)
    inputs = (
        *(a.reshape(2, BLOCK, -1) for a in (queries, keys, values)),
        permutation.reshape(1, BLOCKS),
        segment.reshape(SEQ // BLOCKS, BLOCKS),
    )
    return pl.pallas_call(
        episode_kernel,
        out_shape=jax.ShapeDtypeStruct(queries.shape, jnp.bfloat16),
        in_specs=[hbm] * 5,
        out_specs=pl.BlockSpec(memory_space=pltpu.VMEM),
        scratch_shapes=[
            pltpu.VMEM((1, BLOCKS), jnp.int32),
            pltpu.VMEM((SEQ // BLOCKS, BLOCKS), jnp.int32),
            pltpu.VMEM((8, BLOCKS), jnp.int32),
            pltpu.SMEM((8, BLOCKS), jnp.int32),
            pltpu.VMEM((HELD, BLOCK, WIDE), jnp.bfloat16),
            pltpu.VMEM((2 * RING, RING, RING, BLOCK, HEAD_DIM), jnp.bfloat16),
            pltpu.VMEM((2 * RING, RING, RING, BLOCK, HEAD_DIM), jnp.bfloat16),
            pltpu.VMEM((RING, 2, BLOCK, 2 * HEAD_DIM), jnp.bfloat16),
            pltpu.VMEM((RING, 2, BLOCK, 2 * HEAD_DIM), jnp.bfloat16),
            pltpu.VMEM((RING, 2, BLOCK, HEAD_DIM), jnp.bfloat16),
            pltpu.VMEM((RING, 2, BLOCK, HEAD_DIM), jnp.bfloat16),
            pltpu.VMEM((HELD, ROWS, WIDTH), jnp.bfloat16),
            pltpu.VMEM((HELD, ROWS, HEAD_DIM), jnp.float32),
            pltpu.VMEM((HELD, BLOCK, WIDE), jnp.bfloat16),
            pltpu.SemaphoreType.DMA((COPIES,)),
            pltpu.SemaphoreType.DMA((COPIES,)),
            pltpu.SemaphoreType.DMA((FIRSTS,)),
            pltpu.SemaphoreType.DMA((FIRSTS,)),
            pltpu.SemaphoreType.DMA((HELD,)),
            pltpu.SemaphoreType.DMA((HELD,)),
            pltpu.SemaphoreType.DMA((9,)),
        ],
        compiler_params=pltpu.CompilerParams(
            collective_id=0, has_side_effects=True, vmem_limit_bytes=40 << 20
        ),
        name="episode",
    )(*(pltpu.with_memory_space_constraint(a, pltpu.HBM) for a in inputs))


def solution(mesh):
    fine = Mesh(mesh.devices.reshape(2, 2, 4, 2, 4), AXES)
    slots = AXES[1:]
    return jax.shard_map(
        shards,
        mesh=fine,
        in_specs=(P(slots, "head"), P(slots, "head"), P(slots, "head"), P(), P()),
        out_specs=P(slots, "head"),
        check_vma=False,
    )
```

```python
import math

import jax
import jax.numpy as jnp
from jax import lax
from jax.experimental import pallas as pl
from jax.experimental.pallas import tpu as pltpu
from jax.sharding import Mesh, PartitionSpec as P

HEAD_DIM = 128
BLOCK = 64
BLOCKS = 128
SEQ = 8192
SEGMENTS = 8
GROUP = 4
RING = 4
LOCAL = 128
ROWS = GROUP * BLOCK
WIDE = GROUP * HEAD_DIM
HELD = 2 * RING
REACH = 34
WIDTH = REACH * BLOCK
SCALE = math.log2(math.e) / math.sqrt(HEAD_DIM)
NEG = -1e30
MESH = pl.DeviceIdType.MESH
AXES = ("head", "z_hi", "y", "z_lo", "x")


def landing(slot):
    z = (slot >> 6) * 2 + ((slot >> 3) & 1)
    y = (slot >> 4) & 3
    return (((slot & 1) * RING + z) * RING + y) * RING + ((slot >> 1) & 3)


def turn(value, shift):
    return (value + shift) & (RING - 1)


def columns(j, width):
    return pl.ds(pl.multiple_of(j * width, width), width)


def tables(perm, seg):
    lane = lax.broadcasted_iota(jnp.int32, (1, BLOCKS), 1)
    starts = jnp.zeros((1, BLOCKS), jnp.int32)
    for s in range(1, SEGMENTS):
        count = jnp.sum((seg < s).astype(jnp.int32), axis=1, keepdims=True)
        count = jnp.sum(count, axis=0, keepdims=True)
        starts = jnp.where(lane == s, count, starts)
    slot = lax.broadcasted_iota(jnp.int32, (BLOCKS, BLOCKS), 0)
    block = lax.broadcasted_iota(jnp.int32, (BLOCKS, BLOCKS), 1)
    held = jnp.sum(jnp.where(slot == block, perm, 0), axis=1, keepdims=True)
    inverse = jnp.sum(jnp.where(held == block, landing(slot), 0), axis=0, keepdims=True)
    inverse = jnp.minimum(inverse, BLOCKS - 1)
    return jnp.concatenate([perm, starts, inverse, jnp.zeros((5, BLOCKS), jnp.int32)], axis=0)


def episode_kernel(
    q_ref, k_ref, v_ref, perm_ref, seg_ref, out_ref,
    perm, seg, meta_vec, meta, q_all, k_all, v_all, k_part, v_part, k_raw, v_raw, weights, scale, o_all,
    send_sem, recv_sem, first_send, first_recv, o_send, o_recv, local_sem,
):
    core, z_hi, y, z_lo, x = (lax.axis_index(a) for a in AXES)
    z = z_hi * 2 + z_lo
    other = 1 - core
    apart = (z_lo + core) & 1
    home = apart == 0
    away = jnp.logical_not(home)
    half = x >> 1
    x_odd, y_odd = x & 1, y & 1

    def cube(b, ex, ey, ez):
        way = 1 - 2 * b
        return ex * way * (1 - 2 * x_odd), ey * way * (1 - 2 * y_odd), ez * way * (1 - 2 * z_lo)

    def at(to_core, dx=0, dy=0, dz=0):
        far_z = turn(z, dz)
        return (to_core, far_z >> 1, turn(y, dy), far_z & 1, turn(x, dx))

    barrier = pltpu.get_barrier_semaphore()

    def tell(device):
        pl.semaphore_signal(barrier, inc=1, device_id=device, device_id_type=MESH)

    own_key = home & (half == core)
    across = [(ex, ey) for ey in range(2) for ex in range(2)]
    for dy in (1, 2, 3):
        tell(at(core, 0, dy))
    for n in range(2):
        for dz in range(RING):
            device = at(z_lo, 2 * core + n - x, 0, dz)
            if dz:
                tell(device)
            else:
                pl.when(jnp.logical_not(home & (x == 2 * core + n)))(lambda device=device: tell(device))
    for ex, ey in across:
        tell(at(z_lo, *cube(core, ex, ey, 1)))
        tell(at(other, *cube(other, ex, ey, apart)))

    def tell_home():
        for ex, ey in across[1:]:
            tell(at(core, *cube(core, ex, ey, 0)))

    def tell_away():
        for ex, ey in across:
            tell(at(z_lo, *cube(core, ex, ey, 0)))
            tell(at(core, *cube(core, ex, ey, 1)))

    pl.when(home)(tell_home)
    pl.when(away)(tell_away)
    early = [
        pltpu.make_async_copy(src, dst, local_sem.at[n])
        for n, (src, dst) in enumerate((
            *(
                (ref.at[1, :, columns(2 * odd + y_odd, HEAD_DIM)], raw.at[y, odd])
                for ref, raw in ((k_ref, k_raw), (v_ref, v_raw))
                for odd in range(2)
            ),
            (perm_ref, perm),
            (seg_ref, seg),
        ))
    ]
    for copy in early:
        copy.start()
    pl.semaphore_wait(barrier, 22 + 5 * apart - own_key.astype(jnp.int32))

    firsts = []

    def first(src, dst, n, device, own=False):
        copy = pltpu.make_async_remote_copy(
            src_ref=src,
            dst_ref=dst,
            send_sem=first_send.at[len(firsts)],
            recv_sem=first_recv.at[n],
            device_id=device,
            device_id_type=MESH,
        )
        firsts.append((copy, own))
        if own is False:
            copy.start()
        else:
            pl.when(jnp.logical_not(own))(copy.start)
            pl.when(own)(pltpu.make_async_copy(src, dst, first_recv.at[n]).start)

    def landed(ref, n):
        pltpu.make_async_copy(ref, ref, first_recv.at[n]).wait()

    def left(copies):
        for copy, own in copies:
            if own is False:
                copy.wait_send()
            else:
                pl.when(jnp.logical_not(own))(copy.wait_send)

    count = [0]

    def send(src, dst, device):
        n = count[0]
        count[0] += 1
        copy = pltpu.make_async_remote_copy(
            src_ref=src,
            dst_ref=dst,
            send_sem=send_sem.at[n],
            recv_sem=recv_sem.at[n],
            device_id=device,
            device_id_type=MESH,
        )
        copy.start()
        return copy

    targets = [(k, dx) for k in range(2) for dx in (1, 3, 2, 0)]
    ways = ((1, -1), (3, 1), (2, 2))
    here_x = pl.ds(2 * core, 2)

    class Spread:
        def __init__(self, ref, part, raw, everything, offset, own_sem):
            self.ref, self.part, self.raw, self.all, self.offset = ref, part, raw, everything, offset
            self.own_sem = own_sem
            self.shares = []

        def straight(self, source, dst, offset):
            before = len(firsts)
            for k, dx in targets:
                first(
                    source(((x + dx) & 1)),
                    dst,
                    self.offset + offset + z * 2 + x_odd,
                    at(half, dx, 0, apart + 2 * k),
                    own_key if k == 0 and dx == 0 else False,
                )
            return firsts[before:]

        def share(self, src, dst):
            self.shares.append(send(src, dst, at(other)))

        def start(self):
            self.out = self.straight(
                lambda odd: self.ref.at[0, :, columns(odd, 2 * HEAD_DIM)], self.part.at[z, x_odd], 0
            )
            self.along = [
                send(
                    self.ref.at[1, :, columns(2 * odd + ((y + d) & 1), HEAD_DIM)],
                    self.raw.at[y, odd],
                    at(core, 0, d),
                )
                for d, _ in ways
                for odd in range(2)
            ]

        def first_lands(self):
            for line in range(RING):
                for odd in range(2):
                    landed(self.part.at[line, odd], self.offset + line * 2 + odd)
            dst = self.all.at[0:RING, y, here_x]

            def piece(d):
                return self.part.at[:, :, :, columns(((y + d) & 1), HEAD_DIM)]

            self.far = [send(piece(d), dst, at(core, 0, d)) for d, _ in ways]
            self.share(piece(0), dst)
            self.own = pltpu.make_async_copy(piece(0), dst, self.own_sem)
            self.own.start()

        def second_lands(self):
            for copy in self.along:
                copy.wait_recv()
            self.second = self.straight(
                lambda odd: self.raw.at[:, odd], self.all.at[RING + z, :, x], 8
            )

        def take_first(self, n):
            self.far[n].wait_recv()
            ref = self.all.at[0:RING, turn(y, ways[n][1]), here_x]
            self.share(ref, ref)

        def take_second(self, dz):
            line = turn(z, dz)
            for odd in range(2):
                landed(self.all.at[RING + line, :, 2 * core + odd], self.offset + 8 + line * 2 + odd)
            ref = self.all.at[RING + line, :, here_x]
            self.share(ref, ref)

    keys = Spread(k_ref, k_part, k_raw, k_all, 0, local_sem.at[7])
    values = Spread(v_ref, v_part, v_raw, v_all, 16, local_sem.at[8])
    keys.start()
    before = len(firsts)
    for b in range(2):
        for ex, ey in reversed(across):
            n = apart * 4 + ey * 2 + ex
            first(
                q_ref.at[b, :, columns(2 * ((x + ex) & 1) + ((y + ey) & 1), WIDE)],
                q_all.at[n],
                32 + n,
                at(b, *cube(b, ex, ey, apart)),
                home & (core == b) if not (ex or ey) else False,
            )
    asked = firsts[before:]
    values.start()
    for copy in early:
        copy.wait()
    meta_vec[...] = tables(perm[...], seg[...])
    to_scalars = pltpu.make_async_copy(meta_vec, meta, local_sem.at[6])
    to_scalars.start()

    keys.second_lands()
    keys.first_lands()
    for copy in keys.far:
        copy.wait_send()
    values.first_lands()
    left(keys.second)
    values.second_lands()
    for n in range(3):
        keys.take_first(n)
    for dz in (0, 1, 3, 2):
        keys.take_second(dz)
    to_scalars.wait()
    for n in range(HELD):
        landed(q_all.at[n], 32 + n)
    keys.own.wait()
    for copy in keys.shares:
        copy.wait_recv()

    def later():
        left(keys.out + values.out + asked)
        for copy in keys.along + values.along + keys.shares:
            copy.wait_send()
        yield
        for n in range(3):
            values.take_first(n)
            yield
        for dz in (0, 1, 3, 2):
            values.take_second(dz)
            yield
        left(values.second)
        for copy in values.far + values.shares:
            copy.wait_send()
        values.own.wait()
        for copy in values.shares:
            copy.wait_recv()
        yield

    v_steps = later()
    next(v_steps)

    def slot(n):
        dx, dy, dz = cube(core, n % 2, n // 2 % 2, n // 4)
        far_z = turn(z, dz)
        return ((((far_z >> 1) * RING + turn(y, dy)) * 2 + (far_z & 1)) * RING + turn(x, dx)) * 2 + core

    def rows_of(ref, block, start, count):
        parts = []
        for u in range(count):
            there = jnp.clip(block - (REACH - 1) + start + u, 0, BLOCKS - 1)
            place = meta[2, there]
            parts.append(ref[place >> 4, (place >> 2) & 3, place & 3])
        return jnp.concatenate(parts, axis=0)

    def score(i):
        block = meta[0, slot(i)]
        row_pos = block * BLOCK + lax.broadcasted_iota(jnp.int32, (BLOCK, HEAD_DIM), 0)
        row_low = jnp.zeros((BLOCK, HEAD_DIM), jnp.int32)
        for s in range(1, SEGMENTS):
            row_low = jnp.where(meta[1, s] <= row_pos, meta[1, s], row_low)
        q = jnp.concatenate(
            [q_all[i, :, j * HEAD_DIM:(j + 1) * HEAD_DIM] for j in range(GROUP)], axis=0
        )
        pieces = []
        top = None
        for start in range(-2, REACH - 2, 4):
            begin, count = max(start, 0), 4 + min(start, 0)
            s = lax.dot_general(
                q, rows_of(k_all, block, begin, count), (((1,), (1,)), ((), ())),
                preferred_element_type=jnp.float32,
            )
            for half in range(count // 2):
                index = begin + 2 * half
                col = (block - (REACH - 1) + index) * BLOCK + lax.broadcasted_iota(
                    jnp.int32, (BLOCK, HEAD_DIM), 1
                )
                seen = col >= row_low
                if index == REACH - 2:
                    seen = seen & (col <= row_pos)
                seen = jnp.concatenate([seen] * GROUP, axis=0)
                piece = jnp.where(seen, s[:, half * HEAD_DIM:(half + 1) * HEAD_DIM], NEG)
                pieces.append(piece)
                top = piece if top is None else jnp.maximum(top, piece)
        top = jnp.max(top, axis=1, keepdims=True)
        total = None
        for n, piece in enumerate(pieces):
            weight = jnp.exp2((piece - top) * SCALE)
            total = weight if total is None else total + weight
            weights[i, :, n * HEAD_DIM:(n + 1) * HEAD_DIM] = weight.astype(jnp.bfloat16)
        total = jnp.sum(total, axis=1, keepdims=True)
        scale[i] = jnp.broadcast_to(1.0 / total, (ROWS, HEAD_DIM))

    for n in range(0, HELD, 4):
        for m in range(n, n + 4):
            score(m)
        for _ in range(4):
            next(v_steps)

    def blend(i):
        block = meta[0, slot(i)]
        mixed = jnp.dot(weights[i], rows_of(v_all, block, 0, REACH), preferred_element_type=jnp.float32)
        return (mixed * scale[i]).astype(jnp.bfloat16)

    def place(ref, mixed):
        for j in range(GROUP):
            ref[:, j * HEAD_DIM:(j + 1) * HEAD_DIM] = mixed[j * BLOCK:(j + 1) * BLOCK]

    rows = pl.ds(pl.multiple_of(core * BLOCK, BLOCK), BLOCK)
    mine = columns(2 * x_odd + y_odd, WIDE)

    def answer(n):
        return pltpu.make_async_remote_copy(
            src_ref=o_all.at[n],
            dst_ref=out_ref.at[rows, mine],
            send_sem=o_send.at[n],
            recv_sem=o_recv.at[core * 4 + n % 4],
            device_id=at(z_lo, *cube(core, n % 2, n // 2 % 2, n // 4)),
            device_id_type=MESH,
        )

    for n in (7, 6, 5, 3, 4, 2, 1, 0):
        mixed = blend(n)
        for j in range(GROUP):
            o_all[n, :, j * HEAD_DIM:(j + 1) * HEAD_DIM] = mixed[j * BLOCK:(j + 1) * BLOCK]
        if n:
            answer(n).start()
    pl.when(away)(answer(0).start)
    pl.when(home)(
        pltpu.make_async_copy(o_all.at[0], out_ref.at[rows, mine], o_recv.at[core * 4]).start
    )
    for b in range(2):
        for n, (ex, ey) in enumerate(across):
            j = 2 * ((x + ex) & 1) + ((y + ey) & 1)
            ref = out_ref.at[b * BLOCK:(b + 1) * BLOCK, columns(j, WIDE)]
            pltpu.make_async_copy(ref, ref, o_recv.at[b * 4 + n]).wait()
    for n in range(1, HELD):
        answer(n).wait_send()
    pl.when(away)(answer(0).wait_send)


COPIES = 2 * (6 + 3 + 8)
FIRSTS = 2 * (8 + 8) + 8


def shards(queries, keys, values, permutation, segment):
    hbm = pl.BlockSpec(memory_space=pltpu.HBM)
    inputs = (
        *(a.reshape(2, BLOCK, -1) for a in (queries, keys, values)),
        permutation.reshape(1, BLOCKS),
        segment.reshape(SEQ // BLOCKS, BLOCKS),
    )
    return pl.pallas_call(
        episode_kernel,
        out_shape=jax.ShapeDtypeStruct(queries.shape, jnp.bfloat16),
        in_specs=[hbm] * 5,
        out_specs=pl.BlockSpec(memory_space=pltpu.VMEM),
        scratch_shapes=[
            pltpu.VMEM((1, BLOCKS), jnp.int32),
            pltpu.VMEM((SEQ // BLOCKS, BLOCKS), jnp.int32),
            pltpu.VMEM((8, BLOCKS), jnp.int32),
            pltpu.SMEM((8, BLOCKS), jnp.int32),
            pltpu.VMEM((HELD, BLOCK, WIDE), jnp.bfloat16),
            pltpu.VMEM((2 * RING, RING, RING, BLOCK, HEAD_DIM), jnp.bfloat16),
            pltpu.VMEM((2 * RING, RING, RING, BLOCK, HEAD_DIM), jnp.bfloat16),
            pltpu.VMEM((RING, 2, BLOCK, 2 * HEAD_DIM), jnp.bfloat16),
            pltpu.VMEM((RING, 2, BLOCK, 2 * HEAD_DIM), jnp.bfloat16),
            pltpu.VMEM((RING, 2, BLOCK, HEAD_DIM), jnp.bfloat16),
            pltpu.VMEM((RING, 2, BLOCK, HEAD_DIM), jnp.bfloat16),
            pltpu.VMEM((HELD, ROWS, WIDTH), jnp.bfloat16),
            pltpu.VMEM((HELD, ROWS, HEAD_DIM), jnp.float32),
            pltpu.VMEM((HELD, BLOCK, WIDE), jnp.bfloat16),
            pltpu.SemaphoreType.DMA((COPIES,)),
            pltpu.SemaphoreType.DMA((COPIES,)),
            pltpu.SemaphoreType.DMA((FIRSTS,)),
            pltpu.SemaphoreType.DMA((FIRSTS,)),
            pltpu.SemaphoreType.DMA((HELD,)),
            pltpu.SemaphoreType.DMA((HELD,)),
            pltpu.SemaphoreType.DMA((9,)),
        ],
        compiler_params=pltpu.CompilerParams(
            collective_id=0, has_side_effects=True, vmem_limit_bytes=40 << 20
        ),
        name="episode",
    )(*(pltpu.with_memory_space_constraint(a, pltpu.HBM) for a in inputs))


def solution(mesh):
    fine = Mesh(mesh.devices.reshape(2, 2, 4, 2, 4), AXES)
    slots = AXES[1:]
    return jax.shard_map(
        shards,
        mesh=fine,
        in_specs=(P(slots, "head"), P(slots, "head"), P(slots, "head"), P(), P()),
        out_specs=P(slots, "head"),
        check_vma=False,
    )
```

```python
import math

import jax
import jax.numpy as jnp
from jax import lax
from jax.experimental import pallas as pl
from jax.experimental.pallas import tpu as pltpu
from jax.sharding import Mesh, PartitionSpec as P

HEAD_DIM = 128
BLOCK = 64
BLOCKS = 128
SEQ = 8192
SEGMENTS = 8
GROUP = 4
RING = 4
LOCAL = 128
ROWS = GROUP * BLOCK
WIDE = GROUP * HEAD_DIM
HELD = 2 * RING
REACH = 34
WIDTH = REACH * BLOCK
SCALE = math.log2(math.e) / math.sqrt(HEAD_DIM)
NEG = -1e30
MESH = pl.DeviceIdType.MESH
AXES = ("head", "z_hi", "y", "z_lo", "x")


def landing(slot):
    z = (slot >> 6) * 2 + ((slot >> 3) & 1)
    y = (slot >> 4) & 3
    return (((slot & 1) * RING + z) * RING + y) * RING + ((slot >> 1) & 3)


def turn(value, shift):
    return (value + shift) & (RING - 1)


def columns(j, width):
    return pl.ds(pl.multiple_of(j * width, width), width)


def tables(perm, seg):
    lane = lax.broadcasted_iota(jnp.int32, (1, BLOCKS), 1)
    starts = jnp.zeros((1, BLOCKS), jnp.int32)
    for s in range(1, SEGMENTS):
        count = jnp.sum((seg < s).astype(jnp.int32), axis=1, keepdims=True)
        count = jnp.sum(count, axis=0, keepdims=True)
        starts = jnp.where(lane == s, count, starts)
    slot = lax.broadcasted_iota(jnp.int32, (BLOCKS, BLOCKS), 0)
    block = lax.broadcasted_iota(jnp.int32, (BLOCKS, BLOCKS), 1)
    held = jnp.sum(jnp.where(slot == block, perm, 0), axis=1, keepdims=True)
    inverse = jnp.sum(jnp.where(held == block, landing(slot), 0), axis=0, keepdims=True)
    inverse = jnp.minimum(inverse, BLOCKS - 1)
    return jnp.concatenate([perm, starts, inverse, jnp.zeros((5, BLOCKS), jnp.int32)], axis=0)


def episode_kernel(
    q_ref, k_ref, v_ref, perm_ref, seg_ref, out_ref,
    perm, seg, meta_vec, meta, q_all, k_all, v_all, k_part, v_part, k_raw, v_raw, weights, scale, o_all,
    send_sem, recv_sem, first_send, first_recv, o_send, o_recv, local_sem,
):
    core, z_hi, y, z_lo, x = (lax.axis_index(a) for a in AXES)
    z = z_hi * 2 + z_lo
    other = 1 - core
    apart = (z_lo + core) & 1
    home = apart == 0
    away = jnp.logical_not(home)
    half = x >> 1
    x_odd, y_odd = x & 1, y & 1

    def cube(b, ex, ey, ez):
        way = 1 - 2 * b
        return ex * way * (1 - 2 * x_odd), ey * way * (1 - 2 * y_odd), ez * way * (1 - 2 * z_lo)

    def at(to_core, dx=0, dy=0, dz=0):
        far_z = turn(z, dz)
        return (to_core, far_z >> 1, turn(y, dy), far_z & 1, turn(x, dx))

    barrier = pltpu.get_barrier_semaphore()

    def tell(device):
        pl.semaphore_signal(barrier, inc=1, device_id=device, device_id_type=MESH)

    own_key = home & (half == core)
    across = [(ex, ey) for ey in range(2) for ex in range(2)]
    for dy in (1, 2, 3):
        tell(at(core, 0, dy))
    for n in range(2):
        for dz in range(RING):
            device = at(z_lo, 2 * core + n - x, 0, dz)
            if dz:
                tell(device)
            else:
                pl.when(jnp.logical_not(home & (x == 2 * core + n)))(lambda device=device: tell(device))
    for ex, ey in across:
        tell(at(z_lo, *cube(core, ex, ey, 1)))
        tell(at(other, *cube(other, ex, ey, apart)))

    def tell_home():
        for ex, ey in across[1:]:
            tell(at(core, *cube(core, ex, ey, 0)))

    def tell_away():
        for ex, ey in across:
            tell(at(z_lo, *cube(core, ex, ey, 0)))
            tell(at(core, *cube(core, ex, ey, 1)))

    pl.when(home)(tell_home)
    pl.when(away)(tell_away)
    early = [
        pltpu.make_async_copy(src, dst, local_sem.at[n])
        for n, (src, dst) in enumerate((
            *(
                (ref.at[1, :, columns(2 * odd + y_odd, HEAD_DIM)], raw.at[y, odd])
                for ref, raw in ((k_ref, k_raw), (v_ref, v_raw))
                for odd in range(2)
            ),
            (perm_ref, perm),
            (seg_ref, seg),
        ))
    ]
    for copy in early:
        copy.start()
    pl.semaphore_wait(barrier, 22 + 5 * apart - own_key.astype(jnp.int32))

    firsts = []

    def first(src, dst, n, device, own=False):
        copy = pltpu.make_async_remote_copy(
            src_ref=src,
            dst_ref=dst,
            send_sem=first_send.at[len(firsts)],
            recv_sem=first_recv.at[n],
            device_id=device,
            device_id_type=MESH,
        )
        firsts.append((copy, own))
        if own is False:
            copy.start()
        else:
            pl.when(jnp.logical_not(own))(copy.start)
            pl.when(own)(pltpu.make_async_copy(src, dst, first_recv.at[n]).start)

    def landed(ref, n):
        pltpu.make_async_copy(ref, ref, first_recv.at[n]).wait()

    def left(copies):
        for copy, own in copies:
            if own is False:
                copy.wait_send()
            else:
                pl.when(jnp.logical_not(own))(copy.wait_send)

    count = [0]

    def send(src, dst, device):
        n = count[0]
        count[0] += 1
        copy = pltpu.make_async_remote_copy(
            src_ref=src,
            dst_ref=dst,
            send_sem=send_sem.at[n],
            recv_sem=recv_sem.at[n],
            device_id=device,
            device_id_type=MESH,
        )
        copy.start()
        return copy

    targets = [(k, dx) for k in range(2) for dx in (1, 3, 2, 0)]
    ways = ((1, -1), (3, 1), (2, 2))
    here_x = pl.ds(2 * core, 2)

    class Spread:
        def __init__(self, ref, part, raw, everything, offset, own_sem):
            self.ref, self.part, self.raw, self.all, self.offset = ref, part, raw, everything, offset
            self.own_sem = own_sem
            self.shares = []

        def straight(self, source, dst, offset):
            before = len(firsts)
            for k, dx in targets:
                first(
                    source(((x + dx) & 1)),
                    dst,
                    self.offset + offset + z * 2 + x_odd,
                    at(half, dx, 0, apart + 2 * k),
                    own_key if k == 0 and dx == 0 else False,
                )
            return firsts[before:]

        def share(self, src, dst):
            self.shares.append(send(src, dst, at(other)))

        def start(self):
            self.along = [
                send(
                    self.ref.at[1, :, columns(2 * odd + ((y + d) & 1), HEAD_DIM)],
                    self.raw.at[y, odd],
                    at(core, 0, d),
                )
                for d, _ in ways
                for odd in range(2)
            ]
            self.out = self.straight(
                lambda odd: self.ref.at[0, :, columns(odd, 2 * HEAD_DIM)], self.part.at[z, x_odd], 0
            )

        def first_lands(self):
            for line in range(RING):
                for odd in range(2):
                    landed(self.part.at[line, odd], self.offset + line * 2 + odd)
            dst = self.all.at[0:RING, y, here_x]

            def piece(d):
                return self.part.at[:, :, :, columns(((y + d) & 1), HEAD_DIM)]

            self.far = [send(piece(d), dst, at(core, 0, d)) for d, _ in ways]
            self.share(piece(0), dst)
            self.own = pltpu.make_async_copy(piece(0), dst, self.own_sem)
            self.own.start()

        def second_lands(self):
            for copy in self.along:
                copy.wait_recv()
            self.second = self.straight(
                lambda odd: self.raw.at[:, odd], self.all.at[RING + z, :, x], 8
            )

        def take_first(self, n):
            self.far[n].wait_recv()
            ref = self.all.at[0:RING, turn(y, ways[n][1]), here_x]
            self.share(ref, ref)

        def take_second(self, dz):
            line = turn(z, dz)
            for odd in range(2):
                landed(self.all.at[RING + line, :, 2 * core + odd], self.offset + 8 + line * 2 + odd)
            ref = self.all.at[RING + line, :, here_x]
            self.share(ref, ref)

    keys = Spread(k_ref, k_part, k_raw, k_all, 0, local_sem.at[7])
    values = Spread(v_ref, v_part, v_raw, v_all, 16, local_sem.at[8])
    keys.start()
    before = len(firsts)
    for b in range(2):
        for ex, ey in reversed(across):
            n = apart * 4 + ey * 2 + ex
            first(
                q_ref.at[b, :, columns(2 * ((x + ex) & 1) + ((y + ey) & 1), WIDE)],
                q_all.at[n],
                32 + n,
                at(b, *cube(b, ex, ey, apart)),
                home & (core == b) if not (ex or ey) else False,
            )
    asked = firsts[before:]
    values.start()
    for copy in early:
        copy.wait()
    meta_vec[...] = tables(perm[...], seg[...])
    to_scalars = pltpu.make_async_copy(meta_vec, meta, local_sem.at[6])
    to_scalars.start()

    keys.second_lands()
    keys.first_lands()
    for copy in keys.far:
        copy.wait_send()
    values.first_lands()
    left(keys.second)
    values.second_lands()
    for n in range(3):
        keys.take_first(n)
    for dz in (0, 1, 3, 2):
        keys.take_second(dz)
    to_scalars.wait()
    for n in range(HELD):
        landed(q_all.at[n], 32 + n)
    keys.own.wait()
    for copy in keys.shares:
        copy.wait_recv()

    def later():
        left(keys.out + values.out + asked)
        for copy in keys.along + values.along + keys.shares:
            copy.wait_send()
        yield
        for n in range(3):
            values.take_first(n)
            yield
        for dz in (0, 1, 3, 2):
            values.take_second(dz)
            yield
        left(values.second)
        for copy in values.far + values.shares:
            copy.wait_send()
        values.own.wait()
        for copy in values.shares:
            copy.wait_recv()
        yield

    v_steps = later()
    next(v_steps)

    def slot(n):
        dx, dy, dz = cube(core, n % 2, n // 2 % 2, n // 4)
        far_z = turn(z, dz)
        return ((((far_z >> 1) * RING + turn(y, dy)) * 2 + (far_z & 1)) * RING + turn(x, dx)) * 2 + core

    def rows_of(ref, block, start, count):
        parts = []
        for u in range(count):
            there = jnp.clip(block - (REACH - 1) + start + u, 0, BLOCKS - 1)
            place = meta[2, there]
            parts.append(ref[place >> 4, (place >> 2) & 3, place & 3])
        return jnp.concatenate(parts, axis=0)

    def score(i):
        block = meta[0, slot(i)]
        row_pos = block * BLOCK + lax.broadcasted_iota(jnp.int32, (BLOCK, HEAD_DIM), 0)
        row_low = jnp.zeros((BLOCK, HEAD_DIM), jnp.int32)
        for s in range(1, SEGMENTS):
            row_low = jnp.where(meta[1, s] <= row_pos, meta[1, s], row_low)
        q = jnp.concatenate(
            [q_all[i, :, j * HEAD_DIM:(j + 1) * HEAD_DIM] for j in range(GROUP)], axis=0
        )
        pieces = []
        top = None
        for start in range(-2, REACH - 2, 4):
            begin, count = max(start, 0), 4 + min(start, 0)
            s = lax.dot_general(
                q, rows_of(k_all, block, begin, count), (((1,), (1,)), ((), ())),
                preferred_element_type=jnp.float32,
            )
            for half in range(count // 2):
                index = begin + 2 * half
                col = (block - (REACH - 1) + index) * BLOCK + lax.broadcasted_iota(
                    jnp.int32, (BLOCK, HEAD_DIM), 1
                )
                seen = col >= row_low
                if index == REACH - 2:
                    seen = seen & (col <= row_pos)
                seen = jnp.concatenate([seen] * GROUP, axis=0)
                piece = jnp.where(seen, s[:, half * HEAD_DIM:(half + 1) * HEAD_DIM], NEG)
                pieces.append(piece)
                top = piece if top is None else jnp.maximum(top, piece)
        top = jnp.max(top, axis=1, keepdims=True)
        total = None
        for n, piece in enumerate(pieces):
            weight = jnp.exp2((piece - top) * SCALE)
            total = weight if total is None else total + weight
            weights[i, :, n * HEAD_DIM:(n + 1) * HEAD_DIM] = weight.astype(jnp.bfloat16)
        total = jnp.sum(total, axis=1, keepdims=True)
        scale[i] = jnp.broadcast_to(1.0 / total, (ROWS, HEAD_DIM))

    for n in range(0, HELD, 4):
        for m in range(n, n + 4):
            score(m)
        for _ in range(4):
            next(v_steps)

    def blend(i):
        block = meta[0, slot(i)]
        mixed = jnp.dot(weights[i], rows_of(v_all, block, 0, REACH), preferred_element_type=jnp.float32)
        return (mixed * scale[i]).astype(jnp.bfloat16)

    def place(ref, mixed):
        for j in range(GROUP):
            ref[:, j * HEAD_DIM:(j + 1) * HEAD_DIM] = mixed[j * BLOCK:(j + 1) * BLOCK]

    rows = pl.ds(pl.multiple_of(core * BLOCK, BLOCK), BLOCK)
    mine = columns(2 * x_odd + y_odd, WIDE)

    def answer(n):
        return pltpu.make_async_remote_copy(
            src_ref=o_all.at[n],
            dst_ref=out_ref.at[rows, mine],
            send_sem=o_send.at[n],
            recv_sem=o_recv.at[core * 4 + n % 4],
            device_id=at(z_lo, *cube(core, n % 2, n // 2 % 2, n // 4)),
            device_id_type=MESH,
        )

    for n in (7, 6, 5, 3, 4, 2, 1, 0):
        mixed = blend(n)
        for j in range(GROUP):
            o_all[n, :, j * HEAD_DIM:(j + 1) * HEAD_DIM] = mixed[j * BLOCK:(j + 1) * BLOCK]
        if n:
            answer(n).start()
    pl.when(away)(answer(0).start)
    pl.when(home)(
        pltpu.make_async_copy(o_all.at[0], out_ref.at[rows, mine], o_recv.at[core * 4]).start
    )
    for b in range(2):
        for n, (ex, ey) in enumerate(across):
            j = 2 * ((x + ex) & 1) + ((y + ey) & 1)
            ref = out_ref.at[b * BLOCK:(b + 1) * BLOCK, columns(j, WIDE)]
            pltpu.make_async_copy(ref, ref, o_recv.at[b * 4 + n]).wait()
    for n in range(1, HELD):
        answer(n).wait_send()
    pl.when(away)(answer(0).wait_send)


COPIES = 2 * (6 + 3 + 8)
FIRSTS = 2 * (8 + 8) + 8


def shards(queries, keys, values, permutation, segment):
    hbm = pl.BlockSpec(memory_space=pltpu.HBM)
    inputs = (
        *(a.reshape(2, BLOCK, -1) for a in (queries, keys, values)),
        permutation.reshape(1, BLOCKS),
        segment.reshape(SEQ // BLOCKS, BLOCKS),
    )
    return pl.pallas_call(
        episode_kernel,
        out_shape=jax.ShapeDtypeStruct(queries.shape, jnp.bfloat16),
        in_specs=[hbm] * 5,
        out_specs=pl.BlockSpec(memory_space=pltpu.VMEM),
        scratch_shapes=[
            pltpu.VMEM((1, BLOCKS), jnp.int32),
            pltpu.VMEM((SEQ // BLOCKS, BLOCKS), jnp.int32),
            pltpu.VMEM((8, BLOCKS), jnp.int32),
            pltpu.SMEM((8, BLOCKS), jnp.int32),
            pltpu.VMEM((HELD, BLOCK, WIDE), jnp.bfloat16),
            pltpu.VMEM((2 * RING, RING, RING, BLOCK, HEAD_DIM), jnp.bfloat16),
            pltpu.VMEM((2 * RING, RING, RING, BLOCK, HEAD_DIM), jnp.bfloat16),
            pltpu.VMEM((RING, 2, BLOCK, 2 * HEAD_DIM), jnp.bfloat16),
            pltpu.VMEM((RING, 2, BLOCK, 2 * HEAD_DIM), jnp.bfloat16),
            pltpu.VMEM((RING, 2, BLOCK, HEAD_DIM), jnp.bfloat16),
            pltpu.VMEM((RING, 2, BLOCK, HEAD_DIM), jnp.bfloat16),
            pltpu.VMEM((HELD, ROWS, WIDTH), jnp.bfloat16),
            pltpu.VMEM((HELD, ROWS, HEAD_DIM), jnp.float32),
            pltpu.VMEM((HELD, BLOCK, WIDE), jnp.bfloat16),
            pltpu.SemaphoreType.DMA((COPIES,)),
            pltpu.SemaphoreType.DMA((COPIES,)),
            pltpu.SemaphoreType.DMA((FIRSTS,)),
            pltpu.SemaphoreType.DMA((FIRSTS,)),
            pltpu.SemaphoreType.DMA((HELD,)),
            pltpu.SemaphoreType.DMA((HELD,)),
            pltpu.SemaphoreType.DMA((9,)),
        ],
        compiler_params=pltpu.CompilerParams(
            collective_id=0, has_side_effects=True, vmem_limit_bytes=40 << 20
        ),
        name="episode",
    )(*(pltpu.with_memory_space_constraint(a, pltpu.HBM) for a in inputs))


def solution(mesh):
    fine = Mesh(mesh.devices.reshape(2, 2, 4, 2, 4), AXES)
    slots = AXES[1:]
    return jax.shard_map(
        shards,
        mesh=fine,
        in_specs=(P(slots, "head"), P(slots, "head"), P(slots, "head"), P(), P()),
        out_specs=P(slots, "head"),
        check_vma=False,
    )
```

```python
import math

import jax
import jax.numpy as jnp
from jax import lax
from jax.experimental import pallas as pl
from jax.experimental.pallas import tpu as pltpu
from jax.sharding import Mesh, PartitionSpec as P

HEAD_DIM = 128
BLOCK = 64
BLOCKS = 128
SEQ = 8192
SEGMENTS = 8
GROUP = 4
RING = 4
LOCAL = 128
ROWS = GROUP * BLOCK
WIDE = GROUP * HEAD_DIM
HELD = 2 * RING
REACH = 34
WIDTH = REACH * BLOCK
SCALE = math.log2(math.e) / math.sqrt(HEAD_DIM)
NEG = -1e30
MESH = pl.DeviceIdType.MESH
AXES = ("head", "z_hi", "y", "z_lo", "x")


def landing(slot):
    z = (slot >> 6) * 2 + ((slot >> 3) & 1)
    y = (slot >> 4) & 3
    return (((slot & 1) * RING + z) * RING + y) * RING + ((slot >> 1) & 3)


def turn(value, shift):
    return (value + shift) & (RING - 1)


def columns(j, width):
    return pl.ds(pl.multiple_of(j * width, width), width)


def tables(perm, seg):
    lane = lax.broadcasted_iota(jnp.int32, (1, BLOCKS), 1)
    starts = jnp.zeros((1, BLOCKS), jnp.int32)
    for s in range(1, SEGMENTS):
        count = jnp.sum((seg < s).astype(jnp.int32), axis=1, keepdims=True)
        count = jnp.sum(count, axis=0, keepdims=True)
        starts = jnp.where(lane == s, count, starts)
    slot = lax.broadcasted_iota(jnp.int32, (BLOCKS, BLOCKS), 0)
    block = lax.broadcasted_iota(jnp.int32, (BLOCKS, BLOCKS), 1)
    held = jnp.sum(jnp.where(slot == block, perm, 0), axis=1, keepdims=True)
    inverse = jnp.sum(jnp.where(held == block, landing(slot), 0), axis=0, keepdims=True)
    inverse = jnp.minimum(inverse, BLOCKS - 1)
    return jnp.concatenate([perm, starts, inverse, jnp.zeros((5, BLOCKS), jnp.int32)], axis=0)


def episode_kernel(
    q_ref, k_ref, v_ref, perm_ref, seg_ref, out_ref,
    perm, seg, meta_vec, meta, q_all, k_all, v_all, k_part, v_part, k_raw, v_raw, weights, scale, o_all,
    send_sem, recv_sem, first_send, first_recv, o_send, o_recv, local_sem,
):
    core, z_hi, y, z_lo, x = (lax.axis_index(a) for a in AXES)
    z = z_hi * 2 + z_lo
    other = 1 - core
    apart = (z_lo + core) & 1
    home = apart == 0
    away = jnp.logical_not(home)
    half = x >> 1
    x_odd, y_odd = x & 1, y & 1

    def cube(b, ex, ey, ez):
        way = 1 - 2 * b
        return ex * way * (1 - 2 * x_odd), ey * way * (1 - 2 * y_odd), ez * way * (1 - 2 * z_lo)

    def at(to_core, dx=0, dy=0, dz=0):
        far_z = turn(z, dz)
        return (to_core, far_z >> 1, turn(y, dy), far_z & 1, turn(x, dx))

    barrier = pltpu.get_barrier_semaphore()

    def tell(device):
        pl.semaphore_signal(barrier, inc=1, device_id=device, device_id_type=MESH)

    own_key = home & (half == core)
    across = [(ex, ey) for ey in range(2) for ex in range(2)]
    for dy in (1, 2, 3):
        tell(at(core, 0, dy))
    for n in range(2):
        for dz in range(RING):
            device = at(z_lo, 2 * core + n - x, 0, dz)
            if dz:
                tell(device)
            else:
                pl.when(jnp.logical_not(home & (x == 2 * core + n)))(lambda device=device: tell(device))
    for ex, ey in across:
        tell(at(z_lo, *cube(core, ex, ey, 1)))
        tell(at(other, *cube(other, ex, ey, apart)))

    def tell_home():
        for ex, ey in across[1:]:
            tell(at(core, *cube(core, ex, ey, 0)))

    def tell_away():
        for ex, ey in across:
            tell(at(z_lo, *cube(core, ex, ey, 0)))
            tell(at(core, *cube(core, ex, ey, 1)))

    pl.when(home)(tell_home)
    pl.when(away)(tell_away)
    early = [
        pltpu.make_async_copy(src, dst, local_sem.at[n])
        for n, (src, dst) in enumerate((
            *(
                (ref.at[1, :, columns(2 * odd + y_odd, HEAD_DIM)], raw.at[y, odd])
                for ref, raw in ((k_ref, k_raw), (v_ref, v_raw))
                for odd in range(2)
            ),
            (perm_ref, perm),
            (seg_ref, seg),
        ))
    ]
    for copy in early:
        copy.start()
    pl.semaphore_wait(barrier, 22 + 5 * apart - own_key.astype(jnp.int32))

    firsts = []

    def first(src, dst, n, device, own=False):
        copy = pltpu.make_async_remote_copy(
            src_ref=src,
            dst_ref=dst,
            send_sem=first_send.at[len(firsts)],
            recv_sem=first_recv.at[n],
            device_id=device,
            device_id_type=MESH,
        )
        firsts.append((copy, own))
        if own is False:
            copy.start()
        else:
            pl.when(jnp.logical_not(own))(copy.start)
            pl.when(own)(pltpu.make_async_copy(src, dst, first_recv.at[n]).start)

    def landed(ref, n):
        pltpu.make_async_copy(ref, ref, first_recv.at[n]).wait()

    def left(copies):
        for copy, own in copies:
            if own is False:
                copy.wait_send()
            else:
                pl.when(jnp.logical_not(own))(copy.wait_send)

    count = [0]

    def send(src, dst, device):
        n = count[0]
        count[0] += 1
        copy = pltpu.make_async_remote_copy(
            src_ref=src,
            dst_ref=dst,
            send_sem=send_sem.at[n],
            recv_sem=recv_sem.at[n],
            device_id=device,
            device_id_type=MESH,
        )
        copy.start()
        return copy

    targets = [(k, dx) for k in range(2) for dx in (1, 3, 2, 0)]
    ways = ((1, -1), (3, 1), (2, 2))
    here_x = pl.ds(2 * core, 2)

    class Spread:
        def __init__(self, ref, part, raw, everything, offset, own_sem):
            self.ref, self.part, self.raw, self.all, self.offset = ref, part, raw, everything, offset
            self.own_sem = own_sem
            self.shares = []

        def straight(self, source, dst, offset):
            before = len(firsts)
            for k, dx in targets:
                first(
                    source(((x + dx) & 1)),
                    dst,
                    self.offset + offset + z * 2 + x_odd,
                    at(half, dx, 0, apart + 2 * k),
                    own_key if k == 0 and dx == 0 else False,
                )
            return firsts[before:]

        def share(self, src, dst):
            self.shares.append(send(src, dst, at(other)))

        def start(self):
            self.out = self.straight(
                lambda odd: self.ref.at[0, :, columns(odd, 2 * HEAD_DIM)], self.part.at[z, x_odd], 0
            )
            self.along = [
                send(
                    self.ref.at[1, :, columns(2 * odd + ((y + d) & 1), HEAD_DIM)],
                    self.raw.at[y, odd],
                    at(core, 0, d),
                )
                for d, _ in ways
                for odd in range(2)
            ]

        def first_lands(self):
            for line in range(RING):
                for odd in range(2):
                    landed(self.part.at[line, odd], self.offset + line * 2 + odd)
            dst = self.all.at[0:RING, y, here_x]

            def piece(d):
                return self.part.at[:, :, :, columns(((y + d) & 1), HEAD_DIM)]

            self.far = [send(piece(d), dst, at(core, 0, d)) for d, _ in ways]
            self.share(piece(0), dst)
            self.own = pltpu.make_async_copy(piece(0), dst, self.own_sem)
            self.own.start()

        def second_lands(self):
            for copy in self.along:
                copy.wait_recv()
            self.second = self.straight(
                lambda odd: self.raw.at[:, odd], self.all.at[RING + z, :, x], 8
            )

        def take_first(self, n):
            self.far[n].wait_recv()
            ref = self.all.at[0:RING, turn(y, ways[n][1]), here_x]
            self.share(ref, ref)

        def take_second(self, dz):
            line = turn(z, dz)
            for odd in range(2):
                landed(self.all.at[RING + line, :, 2 * core + odd], self.offset + 8 + line * 2 + odd)
            ref = self.all.at[RING + line, :, here_x]
            self.share(ref, ref)

    keys = Spread(k_ref, k_part, k_raw, k_all, 0, local_sem.at[7])
    values = Spread(v_ref, v_part, v_raw, v_all, 16, local_sem.at[8])
    keys.start()
    before = len(firsts)
    for b in range(2):
        for ex, ey in reversed(across):
            n = apart * 4 + ey * 2 + ex
            first(
                q_ref.at[b, :, columns(2 * ((x + ex) & 1) + ((y + ey) & 1), WIDE)],
                q_all.at[n],
                32 + n,
                at(b, *cube(b, ex, ey, apart)),
                home & (core == b) if not (ex or ey) else False,
            )
    asked = firsts[before:]
    values.start()
    for copy in early:
        copy.wait()
    meta_vec[...] = tables(perm[...], seg[...])
    to_scalars = pltpu.make_async_copy(meta_vec, meta, local_sem.at[6])
    to_scalars.start()

    keys.second_lands()
    keys.first_lands()
    left(keys.second)
    values.second_lands()
    for copy in keys.far:
        copy.wait_send()
    values.first_lands()
    for n in range(3):
        keys.take_first(n)
    for dz in (0, 1, 3, 2):
        keys.take_second(dz)
    to_scalars.wait()
    for n in range(HELD):
        landed(q_all.at[n], 32 + n)
    keys.own.wait()
    for copy in keys.shares:
        copy.wait_recv()

    def later():
        left(keys.out + values.out + asked)
        for copy in keys.along + values.along + keys.shares:
            copy.wait_send()
        yield
        for n in range(3):
            values.take_first(n)
            yield
        for dz in (0, 1, 3, 2):
            values.take_second(dz)
            yield
        left(values.second)
        for copy in values.far + values.shares:
            copy.wait_send()
        values.own.wait()
        for copy in values.shares:
            copy.wait_recv()
        yield

    v_steps = later()
    next(v_steps)

    def slot(n):
        dx, dy, dz = cube(core, n % 2, n // 2 % 2, n // 4)
        far_z = turn(z, dz)
        return ((((far_z >> 1) * RING + turn(y, dy)) * 2 + (far_z & 1)) * RING + turn(x, dx)) * 2 + core

    def rows_of(ref, block, start, count):
        parts = []
        for u in range(count):
            there = jnp.clip(block - (REACH - 1) + start + u, 0, BLOCKS - 1)
            place = meta[2, there]
            parts.append(ref[place >> 4, (place >> 2) & 3, place & 3])
        return jnp.concatenate(parts, axis=0)

    def score(i):
        block = meta[0, slot(i)]
        row_pos = block * BLOCK + lax.broadcasted_iota(jnp.int32, (BLOCK, HEAD_DIM), 0)
        row_low = jnp.zeros((BLOCK, HEAD_DIM), jnp.int32)
        for s in range(1, SEGMENTS):
            row_low = jnp.where(meta[1, s] <= row_pos, meta[1, s], row_low)
        q = jnp.concatenate(
            [q_all[i, :, j * HEAD_DIM:(j + 1) * HEAD_DIM] for j in range(GROUP)], axis=0
        )
        pieces = []
        top = None
        for start in range(-2, REACH - 2, 4):
            begin, count = max(start, 0), 4 + min(start, 0)
            s = lax.dot_general(
                q, rows_of(k_all, block, begin, count), (((1,), (1,)), ((), ())),
                preferred_element_type=jnp.float32,
            )
            for half in range(count // 2):
                index = begin + 2 * half
                col = (block - (REACH - 1) + index) * BLOCK + lax.broadcasted_iota(
                    jnp.int32, (BLOCK, HEAD_DIM), 1
                )
                seen = col >= row_low
                if index == REACH - 2:
                    seen = seen & (col <= row_pos)
                seen = jnp.concatenate([seen] * GROUP, axis=0)
                piece = jnp.where(seen, s[:, half * HEAD_DIM:(half + 1) * HEAD_DIM], NEG)
                pieces.append(piece)
                top = piece if top is None else jnp.maximum(top, piece)
        top = jnp.max(top, axis=1, keepdims=True)
        total = None
        for n, piece in enumerate(pieces):
            weight = jnp.exp2((piece - top) * SCALE)
            total = weight if total is None else total + weight
            weights[i, :, n * HEAD_DIM:(n + 1) * HEAD_DIM] = weight.astype(jnp.bfloat16)
        total = jnp.sum(total, axis=1, keepdims=True)
        scale[i] = jnp.broadcast_to(1.0 / total, (ROWS, HEAD_DIM))

    for n in range(0, HELD, 4):
        for m in range(n, n + 4):
            score(m)
        for _ in range(4):
            next(v_steps)

    def blend(i):
        block = meta[0, slot(i)]
        mixed = jnp.dot(weights[i], rows_of(v_all, block, 0, REACH), preferred_element_type=jnp.float32)
        return (mixed * scale[i]).astype(jnp.bfloat16)

    def place(ref, mixed):
        for j in range(GROUP):
            ref[:, j * HEAD_DIM:(j + 1) * HEAD_DIM] = mixed[j * BLOCK:(j + 1) * BLOCK]

    rows = pl.ds(pl.multiple_of(core * BLOCK, BLOCK), BLOCK)
    mine = columns(2 * x_odd + y_odd, WIDE)

    def answer(n):
        return pltpu.make_async_remote_copy(
            src_ref=o_all.at[n],
            dst_ref=out_ref.at[rows, mine],
            send_sem=o_send.at[n],
            recv_sem=o_recv.at[core * 4 + n % 4],
            device_id=at(z_lo, *cube(core, n % 2, n // 2 % 2, n // 4)),
            device_id_type=MESH,
        )

    for n in (7, 6, 5, 3, 4, 2, 1, 0):
        mixed = blend(n)
        for j in range(GROUP):
            o_all[n, :, j * HEAD_DIM:(j + 1) * HEAD_DIM] = mixed[j * BLOCK:(j + 1) * BLOCK]
        if n:
            answer(n).start()
    pl.when(away)(answer(0).start)
    pl.when(home)(
        pltpu.make_async_copy(o_all.at[0], out_ref.at[rows, mine], o_recv.at[core * 4]).start
    )
    for b in range(2):
        for n, (ex, ey) in enumerate(across):
            j = 2 * ((x + ex) & 1) + ((y + ey) & 1)
            ref = out_ref.at[b * BLOCK:(b + 1) * BLOCK, columns(j, WIDE)]
            pltpu.make_async_copy(ref, ref, o_recv.at[b * 4 + n]).wait()
    for n in range(1, HELD):
        answer(n).wait_send()
    pl.when(away)(answer(0).wait_send)


COPIES = 2 * (6 + 3 + 8)
FIRSTS = 2 * (8 + 8) + 8


def shards(queries, keys, values, permutation, segment):
    hbm = pl.BlockSpec(memory_space=pltpu.HBM)
    inputs = (
        *(a.reshape(2, BLOCK, -1) for a in (queries, keys, values)),
        permutation.reshape(1, BLOCKS),
        segment.reshape(SEQ // BLOCKS, BLOCKS),
    )
    return pl.pallas_call(
        episode_kernel,
        out_shape=jax.ShapeDtypeStruct(queries.shape, jnp.bfloat16),
        in_specs=[hbm] * 5,
        out_specs=pl.BlockSpec(memory_space=pltpu.VMEM),
        scratch_shapes=[
            pltpu.VMEM((1, BLOCKS), jnp.int32),
            pltpu.VMEM((SEQ // BLOCKS, BLOCKS), jnp.int32),
            pltpu.VMEM((8, BLOCKS), jnp.int32),
            pltpu.SMEM((8, BLOCKS), jnp.int32),
            pltpu.VMEM((HELD, BLOCK, WIDE), jnp.bfloat16),
            pltpu.VMEM((2 * RING, RING, RING, BLOCK, HEAD_DIM), jnp.bfloat16),
            pltpu.VMEM((2 * RING, RING, RING, BLOCK, HEAD_DIM), jnp.bfloat16),
            pltpu.VMEM((RING, 2, BLOCK, 2 * HEAD_DIM), jnp.bfloat16),
            pltpu.VMEM((RING, 2, BLOCK, 2 * HEAD_DIM), jnp.bfloat16),
            pltpu.VMEM((RING, 2, BLOCK, HEAD_DIM), jnp.bfloat16),
            pltpu.VMEM((RING, 2, BLOCK, HEAD_DIM), jnp.bfloat16),
            pltpu.VMEM((HELD, ROWS, WIDTH), jnp.bfloat16),
            pltpu.VMEM((HELD, ROWS, HEAD_DIM), jnp.float32),
            pltpu.VMEM((HELD, BLOCK, WIDE), jnp.bfloat16),
            pltpu.SemaphoreType.DMA((COPIES,)),
            pltpu.SemaphoreType.DMA((COPIES,)),
            pltpu.SemaphoreType.DMA((FIRSTS,)),
            pltpu.SemaphoreType.DMA((FIRSTS,)),
            pltpu.SemaphoreType.DMA((HELD,)),
            pltpu.SemaphoreType.DMA((HELD,)),
            pltpu.SemaphoreType.DMA((9,)),
        ],
        compiler_params=pltpu.CompilerParams(
            collective_id=0, has_side_effects=True, vmem_limit_bytes=40 << 20
        ),
        name="episode",
    )(*(pltpu.with_memory_space_constraint(a, pltpu.HBM) for a in inputs))


def solution(mesh):
    fine = Mesh(mesh.devices.reshape(2, 2, 4, 2, 4), AXES)
    slots = AXES[1:]
    return jax.shard_map(
        shards,
        mesh=fine,
        in_specs=(P(slots, "head"), P(slots, "head"), P(slots, "head"), P(), P()),
        out_specs=P(slots, "head"),
        check_vma=False,
    )
```

```python
import math

import jax
import jax.numpy as jnp
from jax import lax
from jax.experimental import pallas as pl
from jax.experimental.pallas import tpu as pltpu
from jax.sharding import Mesh, PartitionSpec as P

HEAD_DIM = 128
BLOCK = 64
BLOCKS = 128
SEQ = 8192
SEGMENTS = 8
GROUP = 4
RING = 4
LOCAL = 128
ROWS = GROUP * BLOCK
WIDE = GROUP * HEAD_DIM
HELD = 2 * RING
REACH = 34
WIDTH = REACH * BLOCK
SCALE = math.log2(math.e) / math.sqrt(HEAD_DIM)
NEG = -1e30
MESH = pl.DeviceIdType.MESH
AXES = ("head", "z_hi", "y", "z_lo", "x")


def landing(slot):
    z = (slot >> 6) * 2 + ((slot >> 3) & 1)
    y = (slot >> 4) & 3
    return (((slot & 1) * RING + z) * RING + y) * RING + ((slot >> 1) & 3)


def turn(value, shift):
    return (value + shift) & (RING - 1)


def columns(j, width):
    return pl.ds(pl.multiple_of(j * width, width), width)


def tables(perm, seg):
    lane = lax.broadcasted_iota(jnp.int32, (1, BLOCKS), 1)
    starts = jnp.zeros((1, BLOCKS), jnp.int32)
    for s in range(1, SEGMENTS):
        count = jnp.sum((seg < s).astype(jnp.int32), axis=1, keepdims=True)
        count = jnp.sum(count, axis=0, keepdims=True)
        starts = jnp.where(lane == s, count, starts)
    slot = lax.broadcasted_iota(jnp.int32, (BLOCKS, BLOCKS), 0)
    block = lax.broadcasted_iota(jnp.int32, (BLOCKS, BLOCKS), 1)
    held = jnp.sum(jnp.where(slot == block, perm, 0), axis=1, keepdims=True)
    inverse = jnp.sum(jnp.where(held == block, landing(slot), 0), axis=0, keepdims=True)
    inverse = jnp.minimum(inverse, BLOCKS - 1)
    return jnp.concatenate([perm, starts, inverse, jnp.zeros((5, BLOCKS), jnp.int32)], axis=0)


def episode_kernel(
    q_ref, k_ref, v_ref, perm_ref, seg_ref, out_ref,
    perm, seg, meta_vec, meta, q_all, k_all, v_all, k_part, v_part, k_raw, v_raw, weights, scale, o_all,
    send_sem, recv_sem, first_send, first_recv, o_send, o_recv, local_sem,
):
    core, z_hi, y, z_lo, x = (lax.axis_index(a) for a in AXES)
    z = z_hi * 2 + z_lo
    other = 1 - core
    apart = (z_lo + core) & 1
    home = apart == 0
    away = jnp.logical_not(home)
    half = x >> 1
    x_odd, y_odd = x & 1, y & 1

    def cube(b, ex, ey, ez):
        way = 1 - 2 * b
        return ex * way * (1 - 2 * x_odd), ey * way * (1 - 2 * y_odd), ez * way * (1 - 2 * z_lo)

    def at(to_core, dx=0, dy=0, dz=0):
        far_z = turn(z, dz)
        return (to_core, far_z >> 1, turn(y, dy), far_z & 1, turn(x, dx))

    barrier = pltpu.get_barrier_semaphore()

    def tell(device):
        pl.semaphore_signal(barrier, inc=1, device_id=device, device_id_type=MESH)

    own_key = home & (half == core)
    across = [(ex, ey) for ey in range(2) for ex in range(2)]
    for dy in (1, 2, 3):
        tell(at(core, 0, dy))
    for n in range(2):
        for dz in range(RING):
            device = at(z_lo, 2 * core + n - x, 0, dz)
            if dz:
                tell(device)
            else:
                pl.when(jnp.logical_not(home & (x == 2 * core + n)))(lambda device=device: tell(device))
    for ex, ey in across:
        tell(at(z_lo, *cube(core, ex, ey, 1)))
        tell(at(other, *cube(other, ex, ey, apart)))

    def tell_home():
        for ex, ey in across[1:]:
            tell(at(core, *cube(core, ex, ey, 0)))

    def tell_away():
        for ex, ey in across:
            tell(at(z_lo, *cube(core, ex, ey, 0)))
            tell(at(core, *cube(core, ex, ey, 1)))

    pl.when(home)(tell_home)
    pl.when(away)(tell_away)
    early = [
        pltpu.make_async_copy(src, dst, local_sem.at[n])
        for n, (src, dst) in enumerate((
            *(
                (ref.at[1, :, columns(2 * odd + y_odd, HEAD_DIM)], raw.at[y, odd])
                for ref, raw in ((k_ref, k_raw), (v_ref, v_raw))
                for odd in range(2)
            ),
            (perm_ref, perm),
            (seg_ref, seg),
        ))
    ]
    for copy in early:
        copy.start()
    pl.semaphore_wait(barrier, 22 + 5 * apart - own_key.astype(jnp.int32))

    firsts = []

    def first(src, dst, n, device, own=False):
        copy = pltpu.make_async_remote_copy(
            src_ref=src,
            dst_ref=dst,
            send_sem=first_send.at[len(firsts)],
            recv_sem=first_recv.at[n],
            device_id=device,
            device_id_type=MESH,
        )
        firsts.append((copy, own))
        if own is False:
            copy.start()
        else:
            pl.when(jnp.logical_not(own))(copy.start)
            pl.when(own)(pltpu.make_async_copy(src, dst, first_recv.at[n]).start)

    def landed(ref, n):
        pltpu.make_async_copy(ref, ref, first_recv.at[n]).wait()

    def left(copies):
        for copy, own in copies:
            if own is False:
                copy.wait_send()
            else:
                pl.when(jnp.logical_not(own))(copy.wait_send)

    count = [0]

    def send(src, dst, device):
        n = count[0]
        count[0] += 1
        copy = pltpu.make_async_remote_copy(
            src_ref=src,
            dst_ref=dst,
            send_sem=send_sem.at[n],
            recv_sem=recv_sem.at[n],
            device_id=device,
            device_id_type=MESH,
        )
        copy.start()
        return copy

    targets = [(k, dx) for k in range(2) for dx in (1, 3, 2, 0)]
    ways = ((1, -1), (3, 1), (2, 2))
    here_x = pl.ds(2 * core, 2)

    class Spread:
        def __init__(self, ref, part, raw, everything, offset, own_sem):
            self.ref, self.part, self.raw, self.all, self.offset = ref, part, raw, everything, offset
            self.own_sem = own_sem
            self.shares = []

        def straight(self, source, dst, offset):
            before = len(firsts)
            for k, dx in targets:
                first(
                    source(((x + dx) & 1)),
                    dst,
                    self.offset + offset + z * 2 + x_odd,
                    at(half, dx, 0, apart + 2 * k),
                    own_key if k == 0 and dx == 0 else False,
                )
            return firsts[before:]

        def share(self, src, dst):
            self.shares.append(send(src, dst, at(other)))

        def start(self):
            self.out = self.straight(
                lambda odd: self.ref.at[0, :, columns(odd, 2 * HEAD_DIM)], self.part.at[z, x_odd], 0
            )
            self.along = [
                send(
                    self.ref.at[1, :, columns(2 * odd + ((y + d) & 1), HEAD_DIM)],
                    self.raw.at[y, odd],
                    at(core, 0, d),
                )
                for d, _ in ways
                for odd in range(2)
            ]

        def first_lands(self):
            for line in range(RING):
                for odd in range(2):
                    landed(self.part.at[line, odd], self.offset + line * 2 + odd)
            dst = self.all.at[0:RING, y, here_x]

            def piece(d):
                return self.part.at[:, :, :, columns(((y + d) & 1), HEAD_DIM)]

            self.far = [send(piece(d), dst, at(core, 0, d)) for d, _ in ways]
            self.share(piece(0), dst)
            self.own = pltpu.make_async_copy(piece(0), dst, self.own_sem)
            self.own.start()

        def second_lands(self):
            for copy in self.along:
                copy.wait_recv()
            self.second = self.straight(
                lambda odd: self.raw.at[:, odd], self.all.at[RING + z, :, x], 8
            )

        def take_first(self, n):
            self.far[n].wait_recv()
            ref = self.all.at[0:RING, turn(y, ways[n][1]), here_x]
            self.share(ref, ref)

        def take_second(self, dz):
            line = turn(z, dz)
            for odd in range(2):
                landed(self.all.at[RING + line, :, 2 * core + odd], self.offset + 8 + line * 2 + odd)
            ref = self.all.at[RING + line, :, here_x]
            self.share(ref, ref)

    keys = Spread(k_ref, k_part, k_raw, k_all, 0, local_sem.at[7])
    values = Spread(v_ref, v_part, v_raw, v_all, 16, local_sem.at[8])
    keys.start()
    values.start()
    for copy in early:
        copy.wait()
    meta_vec[...] = tables(perm[...], seg[...])
    to_scalars = pltpu.make_async_copy(meta_vec, meta, local_sem.at[6])
    to_scalars.start()

    keys.second_lands()
    keys.first_lands()
    before = len(firsts)
    for b in range(2):
        for ex, ey in reversed(across):
            n = apart * 4 + ey * 2 + ex
            first(
                q_ref.at[b, :, columns(2 * ((x + ex) & 1) + ((y + ey) & 1), WIDE)],
                q_all.at[n],
                32 + n,
                at(b, *cube(b, ex, ey, apart)),
                home & (core == b) if not (ex or ey) else False,
            )
    asked = firsts[before:]
    for copy in keys.far:
        copy.wait_send()
    values.first_lands()
    left(keys.second)
    values.second_lands()
    for n in range(3):
        keys.take_first(n)
    for dz in (0, 1, 3, 2):
        keys.take_second(dz)
    to_scalars.wait()
    for n in range(HELD):
        landed(q_all.at[n], 32 + n)
    keys.own.wait()
    for copy in keys.shares:
        copy.wait_recv()

    def later():
        left(keys.out + values.out + asked)
        for copy in keys.along + values.along + keys.shares:
            copy.wait_send()
        yield
        for n in range(3):
            values.take_first(n)
            yield
        for dz in (0, 1, 3, 2):
            values.take_second(dz)
            yield
        left(values.second)
        for copy in values.far + values.shares:
            copy.wait_send()
        values.own.wait()
        for copy in values.shares:
            copy.wait_recv()
        yield

    v_steps = later()
    next(v_steps)

    def slot(n):
        dx, dy, dz = cube(core, n % 2, n // 2 % 2, n // 4)
        far_z = turn(z, dz)
        return ((((far_z >> 1) * RING + turn(y, dy)) * 2 + (far_z & 1)) * RING + turn(x, dx)) * 2 + core

    def rows_of(ref, block, start, count):
        parts = []
        for u in range(count):
            there = jnp.clip(block - (REACH - 1) + start + u, 0, BLOCKS - 1)
            place = meta[2, there]
            parts.append(ref[place >> 4, (place >> 2) & 3, place & 3])
        return jnp.concatenate(parts, axis=0)

    def score(i):
        block = meta[0, slot(i)]
        row_pos = block * BLOCK + lax.broadcasted_iota(jnp.int32, (BLOCK, HEAD_DIM), 0)
        row_low = jnp.zeros((BLOCK, HEAD_DIM), jnp.int32)
        for s in range(1, SEGMENTS):
            row_low = jnp.where(meta[1, s] <= row_pos, meta[1, s], row_low)
        q = jnp.concatenate(
            [q_all[i, :, j * HEAD_DIM:(j + 1) * HEAD_DIM] for j in range(GROUP)], axis=0
        )
        pieces = []
        top = None
        for start in range(-2, REACH - 2, 4):
            begin, count = max(start, 0), 4 + min(start, 0)
            s = lax.dot_general(
                q, rows_of(k_all, block, begin, count), (((1,), (1,)), ((), ())),
                preferred_element_type=jnp.float32,
            )
            for half in range(count // 2):
                index = begin + 2 * half
                col = (block - (REACH - 1) + index) * BLOCK + lax.broadcasted_iota(
                    jnp.int32, (BLOCK, HEAD_DIM), 1
                )
                seen = col >= row_low
                if index == REACH - 2:
                    seen = seen & (col <= row_pos)
                seen = jnp.concatenate([seen] * GROUP, axis=0)
                piece = jnp.where(seen, s[:, half * HEAD_DIM:(half + 1) * HEAD_DIM], NEG)
                pieces.append(piece)
                top = piece if top is None else jnp.maximum(top, piece)
        top = jnp.max(top, axis=1, keepdims=True)
        total = None
        for n, piece in enumerate(pieces):
            weight = jnp.exp2((piece - top) * SCALE)
            total = weight if total is None else total + weight
            weights[i, :, n * HEAD_DIM:(n + 1) * HEAD_DIM] = weight.astype(jnp.bfloat16)
        total = jnp.sum(total, axis=1, keepdims=True)
        scale[i] = jnp.broadcast_to(1.0 / total, (ROWS, HEAD_DIM))

    for n in range(0, HELD, 4):
        for m in range(n, n + 4):
            score(m)
        for _ in range(4):
            next(v_steps)

    def blend(i):
        block = meta[0, slot(i)]
        mixed = jnp.dot(weights[i], rows_of(v_all, block, 0, REACH), preferred_element_type=jnp.float32)
        return (mixed * scale[i]).astype(jnp.bfloat16)

    def place(ref, mixed):
        for j in range(GROUP):
            ref[:, j * HEAD_DIM:(j + 1) * HEAD_DIM] = mixed[j * BLOCK:(j + 1) * BLOCK]

    rows = pl.ds(pl.multiple_of(core * BLOCK, BLOCK), BLOCK)
    mine = columns(2 * x_odd + y_odd, WIDE)

    def answer(n):
        return pltpu.make_async_remote_copy(
            src_ref=o_all.at[n],
            dst_ref=out_ref.at[rows, mine],
            send_sem=o_send.at[n],
            recv_sem=o_recv.at[core * 4 + n % 4],
            device_id=at(z_lo, *cube(core, n % 2, n // 2 % 2, n // 4)),
            device_id_type=MESH,
        )

    for n in (7, 6, 5, 3, 4, 2, 1, 0):
        mixed = blend(n)
        for j in range(GROUP):
            o_all[n, :, j * HEAD_DIM:(j + 1) * HEAD_DIM] = mixed[j * BLOCK:(j + 1) * BLOCK]
        if n:
            answer(n).start()
    pl.when(away)(answer(0).start)
    pl.when(home)(
        pltpu.make_async_copy(o_all.at[0], out_ref.at[rows, mine], o_recv.at[core * 4]).start
    )
    for b in range(2):
        for n, (ex, ey) in enumerate(across):
            j = 2 * ((x + ex) & 1) + ((y + ey) & 1)
            ref = out_ref.at[b * BLOCK:(b + 1) * BLOCK, columns(j, WIDE)]
            pltpu.make_async_copy(ref, ref, o_recv.at[b * 4 + n]).wait()
    for n in range(1, HELD):
        answer(n).wait_send()
    pl.when(away)(answer(0).wait_send)


COPIES = 2 * (6 + 3 + 8)
FIRSTS = 2 * (8 + 8) + 8


def shards(queries, keys, values, permutation, segment):
    hbm = pl.BlockSpec(memory_space=pltpu.HBM)
    inputs = (
        *(a.reshape(2, BLOCK, -1) for a in (queries, keys, values)),
        permutation.reshape(1, BLOCKS),
        segment.reshape(SEQ // BLOCKS, BLOCKS),
    )
    return pl.pallas_call(
        episode_kernel,
        out_shape=jax.ShapeDtypeStruct(queries.shape, jnp.bfloat16),
        in_specs=[hbm] * 5,
        out_specs=pl.BlockSpec(memory_space=pltpu.VMEM),
        scratch_shapes=[
            pltpu.VMEM((1, BLOCKS), jnp.int32),
            pltpu.VMEM((SEQ // BLOCKS, BLOCKS), jnp.int32),
            pltpu.VMEM((8, BLOCKS), jnp.int32),
            pltpu.SMEM((8, BLOCKS), jnp.int32),
            pltpu.VMEM((HELD, BLOCK, WIDE), jnp.bfloat16),
            pltpu.VMEM((2 * RING, RING, RING, BLOCK, HEAD_DIM), jnp.bfloat16),
            pltpu.VMEM((2 * RING, RING, RING, BLOCK, HEAD_DIM), jnp.bfloat16),
            pltpu.VMEM((RING, 2, BLOCK, 2 * HEAD_DIM), jnp.bfloat16),
            pltpu.VMEM((RING, 2, BLOCK, 2 * HEAD_DIM), jnp.bfloat16),
            pltpu.VMEM((RING, 2, BLOCK, HEAD_DIM), jnp.bfloat16),
            pltpu.VMEM((RING, 2, BLOCK, HEAD_DIM), jnp.bfloat16),
            pltpu.VMEM((HELD, ROWS, WIDTH), jnp.bfloat16),
            pltpu.VMEM((HELD, ROWS, HEAD_DIM), jnp.float32),
            pltpu.VMEM((HELD, BLOCK, WIDE), jnp.bfloat16),
            pltpu.SemaphoreType.DMA((COPIES,)),
            pltpu.SemaphoreType.DMA((COPIES,)),
            pltpu.SemaphoreType.DMA((FIRSTS,)),
            pltpu.SemaphoreType.DMA((FIRSTS,)),
            pltpu.SemaphoreType.DMA((HELD,)),
            pltpu.SemaphoreType.DMA((HELD,)),
            pltpu.SemaphoreType.DMA((9,)),
        ],
        compiler_params=pltpu.CompilerParams(
            collective_id=0, has_side_effects=True, vmem_limit_bytes=40 << 20
        ),
        name="episode",
    )(*(pltpu.with_memory_space_constraint(a, pltpu.HBM) for a in inputs))


def solution(mesh):
    fine = Mesh(mesh.devices.reshape(2, 2, 4, 2, 4), AXES)
    slots = AXES[1:]
    return jax.shard_map(
        shards,
        mesh=fine,
        in_specs=(P(slots, "head"), P(slots, "head"), P(slots, "head"), P(), P()),
        out_specs=P(slots, "head"),
        check_vma=False,
    )
```

```python
import math

import jax
import jax.numpy as jnp
from jax import lax
from jax.experimental import pallas as pl
from jax.experimental.pallas import tpu as pltpu
from jax.sharding import Mesh, PartitionSpec as P

HEAD_DIM = 128
BLOCK = 64
BLOCKS = 128
SEQ = 8192
SEGMENTS = 8
GROUP = 4
RING = 4
LOCAL = 128
ROWS = GROUP * BLOCK
WIDE = GROUP * HEAD_DIM
HELD = 2 * RING
REACH = 34
WIDTH = REACH * BLOCK
SCALE = math.log2(math.e) / math.sqrt(HEAD_DIM)
NEG = -1e30
MESH = pl.DeviceIdType.MESH
AXES = ("head", "z_hi", "y", "z_lo", "x")


def landing(slot):
    z = (slot >> 6) * 2 + ((slot >> 3) & 1)
    y = (slot >> 4) & 3
    return (((slot & 1) * RING + z) * RING + y) * RING + ((slot >> 1) & 3)


def turn(value, shift):
    return (value + shift) & (RING - 1)


def columns(j, width):
    return pl.ds(pl.multiple_of(j * width, width), width)


def tables(perm, seg):
    lane = lax.broadcasted_iota(jnp.int32, (1, BLOCKS), 1)
    starts = jnp.zeros((1, BLOCKS), jnp.int32)
    for s in range(1, SEGMENTS):
        count = jnp.sum((seg < s).astype(jnp.int32), axis=1, keepdims=True)
        count = jnp.sum(count, axis=0, keepdims=True)
        starts = jnp.where(lane == s, count, starts)
    slot = lax.broadcasted_iota(jnp.int32, (BLOCKS, BLOCKS), 0)
    block = lax.broadcasted_iota(jnp.int32, (BLOCKS, BLOCKS), 1)
    held = jnp.sum(jnp.where(slot == block, perm, 0), axis=1, keepdims=True)
    inverse = jnp.sum(jnp.where(held == block, landing(slot), 0), axis=0, keepdims=True)
    inverse = jnp.minimum(inverse, BLOCKS - 1)
    return jnp.concatenate([perm, starts, inverse, jnp.zeros((5, BLOCKS), jnp.int32)], axis=0)


def episode_kernel(
    q_ref, k_ref, v_ref, perm_ref, seg_ref, out_ref,
    perm, seg, meta_vec, meta, q_all, k_all, v_all, k_part, v_part, k_raw, v_raw, weights, scale, o_all,
    send_sem, recv_sem, first_send, first_recv, o_send, o_recv, local_sem,
):
    core, z_hi, y, z_lo, x = (lax.axis_index(a) for a in AXES)
    z = z_hi * 2 + z_lo
    other = 1 - core
    apart = (z_lo + core) & 1
    home = apart == 0
    away = jnp.logical_not(home)
    half = x >> 1
    x_odd, y_odd = x & 1, y & 1

    def cube(b, ex, ey, ez):
        way = 1 - 2 * b
        return ex * way * (1 - 2 * x_odd), ey * way * (1 - 2 * y_odd), ez * way * (1 - 2 * z_lo)

    def at(to_core, dx=0, dy=0, dz=0):
        far_z = turn(z, dz)
        return (to_core, far_z >> 1, turn(y, dy), far_z & 1, turn(x, dx))

    barrier = pltpu.get_barrier_semaphore()

    def tell(device):
        pl.semaphore_signal(barrier, inc=1, device_id=device, device_id_type=MESH)

    own_key = home & (half == core)
    across = [(ex, ey) for ey in range(2) for ex in range(2)]
    for dy in (1, 2, 3):
        tell(at(core, 0, dy))
    for n in range(2):
        for dz in range(RING):
            device = at(z_lo, 2 * core + n - x, 0, dz)
            if dz:
                tell(device)
            else:
                pl.when(jnp.logical_not(home & (x == 2 * core + n)))(lambda device=device: tell(device))
    for ex, ey in across:
        tell(at(z_lo, *cube(core, ex, ey, 1)))
        tell(at(other, *cube(other, ex, ey, apart)))

    def tell_home():
        for ex, ey in across[1:]:
            tell(at(core, *cube(core, ex, ey, 0)))

    def tell_away():
        for ex, ey in across:
            tell(at(z_lo, *cube(core, ex, ey, 0)))
            tell(at(core, *cube(core, ex, ey, 1)))

    pl.when(home)(tell_home)
    pl.when(away)(tell_away)
    early = [
        pltpu.make_async_copy(src, dst, local_sem.at[n])
        for n, (src, dst) in enumerate((
            *(
                (ref.at[1, :, columns(2 * odd + y_odd, HEAD_DIM)], raw.at[y, odd])
                for ref, raw in ((k_ref, k_raw), (v_ref, v_raw))
                for odd in range(2)
            ),
            (perm_ref, perm),
            (seg_ref, seg),
        ))
    ]
    for copy in early:
        copy.start()
    pl.semaphore_wait(barrier, 22 + 5 * apart - own_key.astype(jnp.int32))

    firsts = []

    def first(src, dst, n, device, own=False):
        copy = pltpu.make_async_remote_copy(
            src_ref=src,
            dst_ref=dst,
            send_sem=first_send.at[len(firsts)],
            recv_sem=first_recv.at[n],
            device_id=device,
            device_id_type=MESH,
        )
        firsts.append((copy, own))
        if own is False:
            copy.start()
        else:
            pl.when(jnp.logical_not(own))(copy.start)
            pl.when(own)(pltpu.make_async_copy(src, dst, first_recv.at[n]).start)

    def landed(ref, n):
        pltpu.make_async_copy(ref, ref, first_recv.at[n]).wait()

    def left(copies):
        for copy, own in copies:
            if own is False:
                copy.wait_send()
            else:
                pl.when(jnp.logical_not(own))(copy.wait_send)

    count = [0]

    def send(src, dst, device):
        n = count[0]
        count[0] += 1
        copy = pltpu.make_async_remote_copy(
            src_ref=src,
            dst_ref=dst,
            send_sem=send_sem.at[n],
            recv_sem=recv_sem.at[n],
            device_id=device,
            device_id_type=MESH,
        )
        copy.start()
        return copy

    targets = [(k, dx) for k in range(2) for dx in (1, 3, 2, 0)]
    ways = ((1, -1), (3, 1), (2, 2))
    here_x = pl.ds(2 * core, 2)

    class Spread:
        def __init__(self, ref, part, raw, everything, offset, own_sem):
            self.ref, self.part, self.raw, self.all, self.offset = ref, part, raw, everything, offset
            self.own_sem = own_sem
            self.shares = []

        def straight(self, source, dst, offset):
            before = len(firsts)
            for k, dx in targets:
                first(
                    source(((x + dx) & 1)),
                    dst,
                    self.offset + offset + z * 2 + x_odd,
                    at(half, dx, 0, apart + 2 * k),
                    own_key if k == 0 and dx == 0 else False,
                )
            return firsts[before:]

        def share(self, src, dst):
            self.shares.append(send(src, dst, at(other)))

        def start(self):
            self.out = self.straight(
                lambda odd: self.ref.at[0, :, columns(odd, 2 * HEAD_DIM)], self.part.at[z, x_odd], 0
            )
            self.along = [
                send(
                    self.ref.at[1, :, columns(2 * odd + ((y + d) & 1), HEAD_DIM)],
                    self.raw.at[y, odd],
                    at(core, 0, d),
                )
                for d, _ in ways
                for odd in range(2)
            ]

        def first_lands(self):
            for line in range(RING):
                for odd in range(2):
                    landed(self.part.at[line, odd], self.offset + line * 2 + odd)
            dst = self.all.at[0:RING, y, here_x]

            def piece(d):
                return self.part.at[:, :, :, columns(((y + d) & 1), HEAD_DIM)]

            self.far = [send(piece(d), dst, at(core, 0, d)) for d, _ in ways]
            self.share(piece(0), dst)
            self.own = pltpu.make_async_copy(piece(0), dst, self.own_sem)
            self.own.start()

        def second_lands(self):
            for copy in self.along:
                copy.wait_recv()
            self.second = self.straight(
                lambda odd: self.raw.at[:, odd], self.all.at[RING + z, :, x], 8
            )

        def take_first(self, n):
            self.far[n].wait_recv()
            ref = self.all.at[0:RING, turn(y, ways[n][1]), here_x]
            self.share(ref, ref)

        def take_second(self, dz):
            line = turn(z, dz)
            for odd in range(2):
                landed(self.all.at[RING + line, :, 2 * core + odd], self.offset + 8 + line * 2 + odd)
            ref = self.all.at[RING + line, :, here_x]
            self.share(ref, ref)

    keys = Spread(k_ref, k_part, k_raw, k_all, 0, local_sem.at[7])
    values = Spread(v_ref, v_part, v_raw, v_all, 16, local_sem.at[8])
    keys.start()
    before = len(firsts)
    for b in range(2):
        for ex, ey in reversed(across):
            n = apart * 4 + ey * 2 + ex
            first(
                q_ref.at[b, :, columns(2 * ((x + ex) & 1) + ((y + ey) & 1), WIDE)],
                q_all.at[n],
                32 + n,
                at(b, *cube(b, ex, ey, apart)),
                home & (core == b) if not (ex or ey) else False,
            )
    asked = firsts[before:]
    values.start()
    for copy in early:
        copy.wait()
    meta_vec[...] = tables(perm[...], seg[...])
    to_scalars = pltpu.make_async_copy(meta_vec, meta, local_sem.at[6])
    to_scalars.start()

    keys.second_lands()
    keys.first_lands()
    for copy in keys.far:
        copy.wait_send()
    values.first_lands()
    left(keys.second)
    values.second_lands()
    for n in range(3):
        keys.take_first(n)
    for dz in (0, 1, 3, 2):
        keys.take_second(dz)
    to_scalars.wait()
    for n in range(HELD):
        landed(q_all.at[n], 32 + n)
    keys.own.wait()
    for copy in keys.shares:
        copy.wait_recv()

    def later():
        left(keys.out + values.out + asked)
        for copy in keys.along + values.along + keys.shares:
            copy.wait_send()
        yield
        for n in range(3):
            values.take_first(n)
            yield
        for dz in (0, 1, 3, 2):
            values.take_second(dz)
            yield
        left(values.second)
        for copy in values.far + values.shares:
            copy.wait_send()
        values.own.wait()
        for copy in values.shares:
            copy.wait_recv()
        yield

    v_steps = later()
    next(v_steps)

    def slot(n):
        dx, dy, dz = cube(core, n % 2, n // 2 % 2, n // 4)
        far_z = turn(z, dz)
        return ((((far_z >> 1) * RING + turn(y, dy)) * 2 + (far_z & 1)) * RING + turn(x, dx)) * 2 + core

    def rows_of(ref, block, start, count):
        parts = []
        for u in range(count):
            there = jnp.clip(block - (REACH - 1) + start + u, 0, BLOCKS - 1)
            place = meta[2, there]
            parts.append(ref[place >> 4, (place >> 2) & 3, place & 3])
        return jnp.concatenate(parts, axis=0)

    def score(i):
        block = meta[0, slot(i)]
        row_pos = block * BLOCK + lax.broadcasted_iota(jnp.int32, (BLOCK, HEAD_DIM), 0)
        row_low = jnp.zeros((BLOCK, HEAD_DIM), jnp.int32)
        for s in range(1, SEGMENTS):
            row_low = jnp.where(meta[1, s] <= row_pos, meta[1, s], row_low)
        q = jnp.concatenate(
            [q_all[i, :, j * HEAD_DIM:(j + 1) * HEAD_DIM] for j in range(GROUP)], axis=0
        )
        pieces = []
        top = None
        for start in range(-2, REACH - 2, 4):
            begin, count = max(start, 0), 4 + min(start, 0)
            s = lax.dot_general(
                q, rows_of(k_all, block, begin, count), (((1,), (1,)), ((), ())),
                preferred_element_type=jnp.float32,
            )
            for half in range(count // 2):
                index = begin + 2 * half
                col = (block - (REACH - 1) + index) * BLOCK + lax.broadcasted_iota(
                    jnp.int32, (BLOCK, HEAD_DIM), 1
                )
                seen = col >= row_low
                if index == REACH - 2:
                    seen = seen & (col <= row_pos)
                seen = jnp.concatenate([seen] * GROUP, axis=0)
                piece = jnp.where(seen, s[:, half * HEAD_DIM:(half + 1) * HEAD_DIM], NEG)
                pieces.append(piece)
                top = piece if top is None else jnp.maximum(top, piece)
        top = jnp.max(top, axis=1, keepdims=True)
        total = None
        for n, piece in enumerate(pieces):
            weight = jnp.exp2((piece - top) * SCALE)
            total = weight if total is None else total + weight
            weights[i, :, n * HEAD_DIM:(n + 1) * HEAD_DIM] = weight.astype(jnp.bfloat16)
        total = jnp.sum(total, axis=1, keepdims=True)
        scale[i] = jnp.broadcast_to(1.0 / total, (ROWS, HEAD_DIM))

    for n in range(0, HELD, 4):
        for m in range(n, n + 4):
            score(m)
        for _ in range(4):
            next(v_steps)

    def blend(i):
        block = meta[0, slot(i)]
        mixed = jnp.dot(weights[i], rows_of(v_all, block, 0, REACH), preferred_element_type=jnp.float32)
        return (mixed * scale[i]).astype(jnp.bfloat16)

    def place(ref, mixed):
        for j in range(GROUP):
            ref[:, j * HEAD_DIM:(j + 1) * HEAD_DIM] = mixed[j * BLOCK:(j + 1) * BLOCK]

    rows = pl.ds(pl.multiple_of(core * BLOCK, BLOCK), BLOCK)
    mine = columns(2 * x_odd + y_odd, WIDE)

    def answer(n):
        return pltpu.make_async_remote_copy(
            src_ref=o_all.at[n],
            dst_ref=out_ref.at[rows, mine],
            send_sem=o_send.at[n],
            recv_sem=o_recv.at[core * 4 + n % 4],
            device_id=at(z_lo, *cube(core, n % 2, n // 2 % 2, n // 4)),
            device_id_type=MESH,
        )

    for n in (7, 3, 6, 5, 1, 2, 4, 0):
        mixed = blend(n)
        for j in range(GROUP):
            o_all[n, :, j * HEAD_DIM:(j + 1) * HEAD_DIM] = mixed[j * BLOCK:(j + 1) * BLOCK]
        if n:
            answer(n).start()
    pl.when(away)(answer(0).start)
    pl.when(home)(
        pltpu.make_async_copy(o_all.at[0], out_ref.at[rows, mine], o_recv.at[core * 4]).start
    )
    for b in range(2):
        for n, (ex, ey) in enumerate(across):
            j = 2 * ((x + ex) & 1) + ((y + ey) & 1)
            ref = out_ref.at[b * BLOCK:(b + 1) * BLOCK, columns(j, WIDE)]
            pltpu.make_async_copy(ref, ref, o_recv.at[b * 4 + n]).wait()
    for n in range(1, HELD):
        answer(n).wait_send()
    pl.when(away)(answer(0).wait_send)


COPIES = 2 * (6 + 3 + 8)
FIRSTS = 2 * (8 + 8) + 8


def shards(queries, keys, values, permutation, segment):
    hbm = pl.BlockSpec(memory_space=pltpu.HBM)
    inputs = (
        *(a.reshape(2, BLOCK, -1) for a in (queries, keys, values)),
        permutation.reshape(1, BLOCKS),
        segment.reshape(SEQ // BLOCKS, BLOCKS),
    )
    return pl.pallas_call(
        episode_kernel,
        out_shape=jax.ShapeDtypeStruct(queries.shape, jnp.bfloat16),
        in_specs=[hbm] * 5,
        out_specs=pl.BlockSpec(memory_space=pltpu.VMEM),
        scratch_shapes=[
            pltpu.VMEM((1, BLOCKS), jnp.int32),
            pltpu.VMEM((SEQ // BLOCKS, BLOCKS), jnp.int32),
            pltpu.VMEM((8, BLOCKS), jnp.int32),
            pltpu.SMEM((8, BLOCKS), jnp.int32),
            pltpu.VMEM((HELD, BLOCK, WIDE), jnp.bfloat16),
            pltpu.VMEM((2 * RING, RING, RING, BLOCK, HEAD_DIM), jnp.bfloat16),
            pltpu.VMEM((2 * RING, RING, RING, BLOCK, HEAD_DIM), jnp.bfloat16),
            pltpu.VMEM((RING, 2, BLOCK, 2 * HEAD_DIM), jnp.bfloat16),
            pltpu.VMEM((RING, 2, BLOCK, 2 * HEAD_DIM), jnp.bfloat16),
            pltpu.VMEM((RING, 2, BLOCK, HEAD_DIM), jnp.bfloat16),
            pltpu.VMEM((RING, 2, BLOCK, HEAD_DIM), jnp.bfloat16),
            pltpu.VMEM((HELD, ROWS, WIDTH), jnp.bfloat16),
            pltpu.VMEM((HELD, ROWS, HEAD_DIM), jnp.float32),
            pltpu.VMEM((HELD, BLOCK, WIDE), jnp.bfloat16),
            pltpu.SemaphoreType.DMA((COPIES,)),
            pltpu.SemaphoreType.DMA((COPIES,)),
            pltpu.SemaphoreType.DMA((FIRSTS,)),
            pltpu.SemaphoreType.DMA((FIRSTS,)),
            pltpu.SemaphoreType.DMA((HELD,)),
            pltpu.SemaphoreType.DMA((HELD,)),
            pltpu.SemaphoreType.DMA((9,)),
        ],
        compiler_params=pltpu.CompilerParams(
            collective_id=0, has_side_effects=True, vmem_limit_bytes=40 << 20
        ),
        name="episode",
    )(*(pltpu.with_memory_space_constraint(a, pltpu.HBM) for a in inputs))


def solution(mesh):
    fine = Mesh(mesh.devices.reshape(2, 2, 4, 2, 4), AXES)
    slots = AXES[1:]
    return jax.shard_map(
        shards,
        mesh=fine,
        in_specs=(P(slots, "head"), P(slots, "head"), P(slots, "head"), P(), P()),
        out_specs=P(slots, "head"),
        check_vma=False,
    )
```
